128 devices in a mesh: row: 16 (over x, y), col: 8 (over z, core).
Axes of the slice: x: 4, y: 4, z: 4, core: 2. Of those that a mesh axis runs over, the one named last changes fastest.
Arguments:
- parent_front: float32 [16384, 16384], P('row', 'col'), may hold values from -3 to 169.6, as said below
- children: float32 [20480, 10240], P('row', 'col'), may hold values from -1 to 1, as said below
- child_map: int32 [2, 80], replicated, may hold values from 0 to 127, as said below
- fill: int32 [2, 80, 80], replicated, may hold values from 0 to 1, as said below
Outputs:
- factored_front: float32 [16384, 16384], P('row', 'col')
The draws below stay inside these ranges and needn't reach their ends.
Inputs may be any that keep to these rules, and one draw needn't show every extreme that they name: `parent_front`: Symmetric. Together with the children's terms, its leading block of order 2 * 512 is positive definite. `children`: each child's block of 10240 rows is symmetric. `child_map`: each row maps the 80 blocks of one child to distinct parent blocks. Child blocks a, b with a // 10 == b // 10 share one run of 16 parent blocks (parent block // 16) at most 2 times and one run of 8 parent blocks at most 1 times; both bounds are reached in every draw. Each child maps exactly 10 blocks into each run of 16 parent blocks. `fill`: symmetric in its last two dimensions, with ones on the diagonal.
All inputs are finite; a program needn't handle non-finite values.
Results may differ from the reference program's by a relative error of at most 0.00011.
Values sent between devices are 32-bit elements; how exact they have to be, the bound alone decides.
No kernel may reach another device: no remote copies, remote signals or barrier semaphores. Data moves between devices by JAX's collectives and lax.ppermute only.
A program may use at most 192 MiB of HBM per device.

```python
import jax
import jax.numpy as jnp
from jax import lax

BLOCK = 128
PANEL = 512
PANELS = 2
NP = 16384
NC = 10240
NPB = 128
NCB = 80
GRP = 10
PRB = 8


def draw_parent_front(key, part):
    key = jax.random.fold_in(key, 31)
    entry_key, height_key = jax.random.split(key)
    entries = jax.random.uniform(entry_key, (NP, NP), jnp.float32, -1.0, 1.0)
    entries = 0.5 * (entries + entries.T)
    leading = PANELS * PANEL
    places = jnp.arange(NP)
    inside = places < leading
    across = inside[:, None] != inside[None, :]
    entries = jnp.where(across, 3.0 * entries, entries)
    heights = leading * jax.random.uniform(height_key, (NP,), jnp.float32, 0.1, 0.15) + 16.0
    on_diag = (places[:, None] == places[None, :]) & inside[:, None]
    return jnp.where(on_diag, heights[:, None], entries)


def draw_children(key, part):
    key = jax.random.fold_in(key, 41)
    entries = jax.random.uniform(key, (2, NC, NC), jnp.float32, -1.0, 1.0)
    entries = 0.5 * (entries + jnp.swapaxes(entries, 1, 2))
    return entries.reshape(2 * NC, NC)


def draw_child_map(key, part):
    key = jax.random.fold_in(key, 11)
    columns = NCB // GRP
    rowdevs = NPB // PRB
    blocks = jnp.arange(NCB, dtype=jnp.int32)
    groups = blocks // GRP
    within = blocks % GRP
    mappings = []
    for child_id in range(2):
        child_key = jax.random.fold_in(key, child_id)
        offset_key, order_key = jax.random.split(child_key)
        offset = jax.random.randint(offset_key, (), 0, columns)
        ranges = (groups + within + offset) % columns
        layers = within // columns
        target = 2 * ranges + layers % 2
        matches = target[:, None] == target[None, :]
        before = blocks[None, :] < blocks[:, None]
        ranks = jnp.sum((matches & before).astype(jnp.int32), axis=1)
        scores = jax.random.randint(order_key, (rowdevs, PRB), 0, 1 << 20) * PRB + jnp.arange(PRB, dtype=jnp.int32)[None, :]
        orders = jnp.argsort(scores, axis=1).astype(jnp.int32)
        positions = orders[target, ranks]
        mappings.append(target * PRB + positions)
    return jnp.stack(mappings).astype(jnp.int32)


def draw_fill(key, part):
    key = jax.random.fold_in(key, 23)
    coins = jax.random.randint(key, (2, NCB, NCB), 0, 8)
    present = (coins < 7).astype(jnp.int32)
    places = jnp.arange(NCB)
    upper = places[:, None] <= places[None, :]
    mirrored = jnp.where(upper[None], present, jnp.swapaxes(present, 1, 2))
    diagonal = (places[:, None] == places[None, :])[None]
    return jnp.where(diagonal, 1, mirrored).astype(jnp.int32)


def setup_inputs(seed: int = 0) -> dict:
    seeds = jax.random.split(jax.random.key(seed), 5)
    parent_front = draw_parent_front(jax.random.fold_in(seeds[4], 71), 0)
    children = draw_children(jax.random.fold_in(seeds[4], 71), 0)
    child_map = draw_child_map(jax.random.fold_in(seeds[4], 71), 0)
    fill = draw_fill(jax.random.fold_in(seeds[4], 71), 0)
    return {"parent_front": parent_front, "children": children, "child_map": child_map, "fill": fill}


def reference(parent_front, children, child_map, fill):
    assembled = parent_front
    offsets = jnp.arange(BLOCK, dtype=jnp.int32)
    for child_id in range(2):
        child_tile = children[child_id * NC:(child_id + 1) * NC].reshape(NCB, BLOCK, NCB, BLOCK)
        weights = fill[child_id].astype(jnp.float32)
        masked = (child_tile * weights[:, None, :, None]).reshape(NC, NC)
        indices = (child_map[child_id][:, None] * BLOCK + offsets[None, :]).reshape(NC).astype(jnp.int32)
        spread = jnp.zeros((NC, NP), jnp.float32).at[:, indices].add(masked)
        assembled = assembled.at[indices].add(spread)
    current = assembled
    row_ids = jnp.arange(NP)
    for panel_step in range(PANELS):
        first_col = panel_step * PANEL
        factor = jnp.linalg.cholesky(current[first_col:first_col + PANEL, first_col:first_col + PANEL])
        solved = lax.linalg.triangular_solve(factor, current[:, first_col:first_col + PANEL], left_side=False, lower=True, transpose_a=True)
        panel_vals = jnp.where((row_ids >= first_col)[:, None], solved, 0.0)
        current = current - jnp.dot(panel_vals, panel_vals.T, precision=lax.Precision.HIGHEST)
        current = current.at[:, first_col:first_col + PANEL].set(panel_vals)
    return current
```

```python
import functools

import jax
import jax.numpy as jnp
from jax import lax
from jax.experimental import pallas as pl
from jax.experimental.pallas import tpu as pltpu
from jax.sharding import PartitionSpec as P

BLOCK = 128
LEAD = 1024
NLEAD = LEAD // BLOCK
GRP = 10
ROWS = 16
COLS = 8
VMEM = 56 * 1024 * 1024
F32 = jnp.float32
BF16 = jnp.bfloat16


def params(**kw):
    return pltpu.CompilerParams(vmem_limit_bytes=VMEM, **kw)


def cost(flops, bytes_accessed):
    return pl.CostEstimate(flops=flops, bytes_accessed=bytes_accessed, transcendentals=0)


def copy_kernel(table, src, dst):
    dst[...] = src[...].reshape(dst.shape)


def pack_columns(table, children):
    rows = children.shape[0]
    return pl.pallas_call(
        copy_kernel,
        grid_spec=pltpu.PrefetchScalarGridSpec(
            num_scalar_prefetch=1,
            grid=(2 * COLS,),
            in_specs=[pl.BlockSpec((rows, BLOCK), lambda s, t: (0, t[s]))],
            out_specs=pl.BlockSpec((1, rows, BLOCK), lambda s, t: (s, 0, 0)),
        ),
        out_shape=jax.ShapeDtypeStruct((2 * COLS, rows, BLOCK), F32),
        compiler_params=params(),
        cost_estimate=cost(0, 2 * 2 * COLS * rows * BLOCK * 4),
        name="pack_columns",
    )(table, children)


def pack_early(table, children):
    return pl.pallas_call(
        copy_kernel,
        grid_spec=pltpu.PrefetchScalarGridSpec(
            num_scalar_prefetch=1,
            grid=(2 * COLS,),
            in_specs=[pl.BlockSpec((BLOCK, BLOCK), lambda s, t: (t[2 * COLS], t[s]))],
            out_specs=pl.BlockSpec((1, BLOCK, BLOCK), lambda s, t: (s, 0, 0)),
        ),
        out_shape=jax.ShapeDtypeStruct((2 * COLS, BLOCK, BLOCK), F32),
        compiler_params=params(),
        cost_estimate=cost(0, 2 * 2 * COLS * BLOCK * BLOCK * 4),
        name="pack_early",
    )(table, children)


def pick_early(table, blocks):
    return pl.pallas_call(
        copy_kernel,
        grid_spec=pltpu.PrefetchScalarGridSpec(
            num_scalar_prefetch=1,
            grid=(ROWS,),
            in_specs=[pl.BlockSpec((1, BLOCK, BLOCK), lambda s, t: (t[s], 0, 0))],
            out_specs=pl.BlockSpec((1, BLOCK, BLOCK), lambda s, t: (s, 0, 0)),
        ),
        out_shape=jax.ShapeDtypeStruct((ROWS, BLOCK, BLOCK), F32),
        compiler_params=params(),
        cost_estimate=cost(0, 2 * ROWS * BLOCK * BLOCK * 4),
        name="pick_early",
    )(table, blocks)


def pack_rows_kernel(row_table, col_table, *refs):
    dst = refs[-1]
    for k in range(GRP):
        dst[0, k] = refs[k][0, 0]


def pack_rows(row_table, col_table, arrived):
    def spec(k):
        return pl.BlockSpec((1, 1, BLOCK, BLOCK), lambda d, rt, ct: (ct[k], rt[d], 0, 0))

    return pl.pallas_call(
        pack_rows_kernel,
        grid_spec=pltpu.PrefetchScalarGridSpec(
            num_scalar_prefetch=2,
            grid=(ROWS,),
            in_specs=[spec(k) for k in range(GRP)],
            out_specs=pl.BlockSpec((1, GRP, BLOCK, BLOCK), lambda d, rt, ct: (d, 0, 0, 0)),
        ),
        out_shape=jax.ShapeDtypeStruct((ROWS, GRP, BLOCK, BLOCK), F32),
        compiler_params=params(),
        cost_estimate=cost(0, 2 * ROWS * GRP * BLOCK * BLOCK * 4),
        name="pack_rows",
    )(row_table, col_table, *([arrived] * GRP))


def strip_kernel(place, keep, parent, blocks, out):
    out[...] = parent[...]
    for s in range(ROWS):

        @pl.when(keep[s] != 0)
        def _():
            at = pl.ds(pl.multiple_of(place[s] * BLOCK, BLOCK), BLOCK)
            out[:, at] = out[:, at] + blocks[s].T


def assemble_strip(place, keep, parent, blocks):
    return pl.pallas_call(
        strip_kernel,
        in_specs=[
            pl.BlockSpec(memory_space=pltpu.SMEM),
            pl.BlockSpec(memory_space=pltpu.SMEM),
            pl.BlockSpec(memory_space=pltpu.VMEM),
            pl.BlockSpec(memory_space=pltpu.VMEM),
        ],
        out_specs=pl.BlockSpec(memory_space=pltpu.VMEM),
        out_shape=jax.ShapeDtypeStruct((BLOCK, LEAD), F32),
        compiler_params=params(),
        cost_estimate=cost(0, 2 << 20),
        name="assemble_strip",
    )(place, keep, parent, blocks)


def split(x):
    hi = x.astype(BF16)
    return hi, (x - hi.astype(F32)).astype(BF16)


def dot3(a_hi, a_lo, b_hi, b_lo):
    dims = (((1,), (1,)), ((), ()))
    total = lax.dot_general(a_hi, b_lo, dims, preferred_element_type=F32)
    total += lax.dot_general(a_lo, b_hi, dims, preferred_element_type=F32)
    return total + lax.dot_general(a_hi, b_hi, dims, preferred_element_type=F32)


def dot_full(a, b, dims):
    return lax.dot_general(
        a, b, (dims, ((), ())), precision=lax.Precision.HIGHEST, preferred_element_type=F32
    )


def invert_diagonal(work):
    lanes = lax.broadcasted_iota(jnp.int32, (BLOCK, BLOCK), 1)
    rows = lax.broadcasted_iota(jnp.int32, (BLOCK, BLOCK), 0)
    lane8 = lax.broadcasted_iota(jnp.int32, (8, BLOCK), 1)
    row8 = lax.broadcasted_iota(jnp.int32, (8, BLOCK), 0)
    done = []
    for t in range(BLOCK // 8):
        base = 8 * t
        part = work[0:8]
        cols = [jnp.broadcast_to(part[:, base + i : base + i + 1], (8, BLOCK)) for i in range(8)]
        pivots = jnp.zeros((8, BLOCK), F32)
        for i in range(8):
            pivot = jnp.broadcast_to(cols[i][i : i + 1], (8, BLOCK))
            pivots = jnp.where(row8 == i, pivot, pivots)
            factor = jnp.where(row8 > i, cols[i] / pivot, 0.0)
            for other in range(i + 1, 8):
                cols[other] = cols[other] - factor * jnp.broadcast_to(cols[other][i : i + 1], (8, BLOCK))
            row = jnp.broadcast_to(part[i : i + 1], (8, BLOCK))
            row = jnp.where(lane8 == base + i, 1.0, row)
            part = jnp.where((lane8 == base + i) & (row8 > i), 0.0, part)
            part = jnp.where((lane8 == base + i) & (row8 == i), 1.0, part)
            part = part - factor * row
        part = part * lax.rsqrt(pivots)
        done.append(part)
        if t < BLOCK // 8 - 1:
            above = (lane8 > base + row8) & (lane8 < base + 8)
            update = dot_full(part[:, base + 8 :], jnp.where(above, 0.0, part), ((0,), (0,)))
            work = work[8:]
            inside = (lanes[: work.shape[0]] >= base) & (lanes[: work.shape[0]] < base + 8)
            work = jnp.where(inside, 0.0, work) - update
    whole = jnp.concatenate(done, axis=0)
    return jnp.where(rows >= lanes, whole, 0.0)


def factor_kernel(lead, inv_hi, inv_lo, work):
    work[...] = lead[...]
    count = LEAD // BLOCK

    def step(k, carry):
        here = pl.ds(pl.multiple_of(k * BLOCK, BLOCK), BLOCK)
        inverse = invert_diagonal(work[here, here])
        work[here, :] = dot_full(inverse, work[here, :], ((1,), (0,)))
        work[here, here] = inverse

        def below(i, carry):
            there = pl.ds(pl.multiple_of(i * BLOCK, BLOCK), BLOCK)
            lower = work[here, there]
            work[there, here] = jnp.zeros((BLOCK, BLOCK), F32)
            work[there, :] = work[there, :] - dot_full(lower, work[here, :], ((0,), (0,)))
            return carry

        return lax.fori_loop(k + 1, count, below, carry)

    lax.fori_loop(0, count, step, 0)

    def finish(k, carry):
        here = pl.ds(pl.multiple_of(k * BLOCK, BLOCK), BLOCK)
        rows = lax.broadcasted_iota(jnp.int32, (BLOCK, LEAD), 0) + k * BLOCK
        lanes = lax.broadcasted_iota(jnp.int32, (BLOCK, LEAD), 1)
        hi, lo = split(jnp.where(rows >= lanes, work[here, :], 0.0))
        inv_hi[here, :] = hi
        inv_lo[here, :] = lo
        return carry

    lax.fori_loop(0, count, finish, 0)


def factor_lead(lead):
    shape = jax.ShapeDtypeStruct((LEAD, LEAD), BF16)
    return pl.pallas_call(
        factor_kernel,
        in_specs=[pl.BlockSpec(memory_space=pltpu.VMEM)],
        out_specs=[pl.BlockSpec(memory_space=pltpu.VMEM)] * 2,
        out_shape=(shape, shape),
        scratch_shapes=[pltpu.VMEM((LEAD, LEAD), F32)],
        compiler_params=params(),
        cost_estimate=cost(100 * 10**9, 8 << 20),
        name="factor_lead",
    )(lead)


TILE = 256


def update_kernel(flags, row_strip, col_strip, inv_hi, inv_lo, parent, out, panel, hi, lo):
    step = pl.program_id(0)

    @pl.when(step == 0)
    def _():
        def chunk(n, carry):
            at = pl.ds(pl.multiple_of(n * TILE, TILE), TILE)
            values = dot3(*split(row_strip[at, :]), inv_hi[...], inv_lo[...])
            panel[at, :] = values
            hi[at, :], lo[at, :] = split(values)
            return carry

        lax.fori_loop(0, LEAD // TILE, chunk, 0)

    in_panel = (flags[1] == 0) & (step < LEAD // TILE)
    top = flags[0] == 0

    @pl.when(in_panel)
    def _():
        at = pl.ds(pl.multiple_of(step * TILE, TILE), TILE)
        rows = lax.broadcasted_iota(jnp.int32, (LEAD, TILE), 0)
        lanes = lax.broadcasted_iota(jnp.int32, (LEAD, TILE), 1) + step * TILE
        out[...] = jnp.where((rows >= lanes) | jnp.logical_not(top), panel[:, at], 0.0)

    @pl.when(jnp.logical_not(in_panel) & top)
    def _():
        out[...] = jnp.zeros_like(out)

    @pl.when(jnp.logical_not(in_panel) & jnp.logical_not(top))
    def _():
        right = split(dot3(*split(col_strip[...]), inv_hi[...], inv_lo[...]))

        def chunk(n, carry):
            at = pl.ds(pl.multiple_of(n * TILE, TILE), TILE)
            out[at, :] = parent[at, :] - dot3(hi[at, :], lo[at, :], *right)
            return carry

        lax.fori_loop(0, LEAD // TILE, chunk, 0)


def update_front(flags, row_strip, col_strip, inv_hi, inv_lo, parent):
    rows, columns = parent.shape
    whole = lambda t, f: (0, 0)
    return pl.pallas_call(
        update_kernel,
        grid_spec=pltpu.PrefetchScalarGridSpec(
            num_scalar_prefetch=1,
            grid=(columns // TILE,),
            in_specs=[
                pl.BlockSpec((LEAD, LEAD), whole),
                pl.BlockSpec((TILE, LEAD), lambda t, f: (t, 0)),
                pl.BlockSpec((LEAD, LEAD), whole),
                pl.BlockSpec((LEAD, LEAD), whole),
                pl.BlockSpec((rows, TILE), lambda t, f: (0, t)),
            ],
            out_specs=pl.BlockSpec((rows, TILE), lambda t, f: (0, t)),
            scratch_shapes=[
                pltpu.VMEM((LEAD, LEAD), F32),
                pltpu.VMEM((LEAD, LEAD), BF16),
                pltpu.VMEM((LEAD, LEAD), BF16),
            ],
        ),
        out_shape=jax.ShapeDtypeStruct((rows, columns), F32),
        compiler_params=params(),
        cost_estimate=cost(40 * 10**9, 32 << 20),
        name="update_front",
    )(flags, row_strip, col_strip, inv_hi, inv_lo, parent)


def place_kernel(source, rank, keep, front, first, second, out):
    i = pl.program_id(0)
    for j in range(16):
        at = pl.ds(j * BLOCK, BLOCK)
        value = front[:, at]
        for h, blocks in ((0, first), (1, second)):
            weight = keep[h, i * 16 + j]
            value = value + jnp.where(weight != 0, blocks[0, rank[h, j]], 0.0)
        out[:, at] = value


def place_children(source, rank, keep, front, arrived):
    rows, columns = front.shape

    def spec(h):
        return pl.BlockSpec((1, GRP, BLOCK, BLOCK), lambda i, s, r, k: (s[h, i], 0, 0, 0))

    return pl.pallas_call(
        place_kernel,
        grid_spec=pltpu.PrefetchScalarGridSpec(
            num_scalar_prefetch=3,
            grid=(rows // BLOCK,),
            in_specs=[pl.BlockSpec((BLOCK, columns), lambda i, s, r, k: (i, 0)), spec(0), spec(1)],
            out_specs=pl.BlockSpec((BLOCK, columns), lambda i, s, r, k: (i, 0)),
        ),
        out_shape=jax.ShapeDtypeStruct((rows, columns), F32),
        input_output_aliases={3: 0},
        compiler_params=params(),
        cost_estimate=cost(0, 24 << 20),
        name="place_children",
    )(source, rank, keep, front, arrived, arrived)


def earlier_count(keys):
    places = jnp.arange(keys.shape[-1], dtype=jnp.int32)
    matches = keys[..., :, None] == keys[..., None, :]
    before = places[None, :] < places[:, None]
    return jnp.sum((matches & before).astype(jnp.int32), axis=-1)


def lookup(codes, values, length):
    hits = codes[..., :, None] == jnp.arange(length, dtype=jnp.int32)
    found = jnp.sum(jnp.where(hits, values[..., :, None], 0), axis=-2)
    return found, jnp.any(hits, axis=-2)


def body(parent_front, children, child_map, fill):
    row_index = lax.axis_index("row")
    col_index = lax.axis_index("col")
    child_id = row_index // COLS
    group_row = row_index % COLS
    blocks = child_map.shape[1]
    places = jnp.arange(blocks, dtype=jnp.int32)
    groups = places // GRP
    within = places % GRP
    run16 = child_map // 16
    run8 = child_map // 8
    slot = earlier_count(groups * COLS + run16)
    pick = lambda x: lax.dynamic_index_in_dim(x, child_id, 0, keepdims=False)
    own_map, own_run16, own_run8, own_slot = pick(child_map), pick(run16), pick(run8), pick(slot)

    col_codes = jnp.where(groups == col_index, own_run16 * 2 + own_slot, -1)
    send_cols, _ = lookup(col_codes, within, 2 * COLS)
    row_codes = jnp.where(groups == group_row, own_run8, -1)
    send_rows, _ = lookup(row_codes, within, ROWS)
    rank_all = earlier_count(run16)
    rank_codes = jnp.where(own_run16 == col_index, pick(rank_all), -1)
    incoming = groups * 2 + own_slot
    pick_cols, _ = lookup(rank_codes, incoming, GRP)
    own_codes = jnp.where(own_run16 == col_index, own_map % 16, -1)
    pick_owner, _ = lookup(own_codes, incoming, 16)

    tile_rows = jnp.where(run8 == row_index, child_map % 8, -1)
    row_block, row_has = lookup(tile_rows, jnp.broadcast_to(places, (2, blocks)), 8)
    tile_cols = jnp.where(run16 == col_index, child_map % 16, -1)
    col_rank, col_has = lookup(tile_cols, rank_all, 16)
    row_hit = (tile_rows[:, None, :] == jnp.arange(8, dtype=jnp.int32)[None, :, None]).astype(F32)
    col_hit = (tile_cols[:, None, :] == jnp.arange(16, dtype=jnp.int32)[None, :, None]).astype(F32)
    present = fill.astype(F32)
    keep = jnp.einsum("hia,hab->hib", row_hit, present)
    keep = jnp.einsum("hib,hjb->hij", keep, col_hit)
    panel_col = (col_index == 0) & (jnp.arange(16) < NLEAD)
    keep = jnp.where(panel_col | (row_index == 0), 0.0, keep)
    keep = (keep > 0.5).astype(jnp.int32).reshape(2, 8 * 16)
    source = jnp.arange(2, dtype=jnp.int32)[:, None] * COLS + row_block // GRP

    owned = col_index * 16 + row_index
    lead_codes = jnp.where(run8 == 0, groups, -1)
    strip_place, strip_has = lookup(lead_codes, child_map, COLS)
    lead_hit = (lead_codes[:, None, :] == jnp.arange(COLS, dtype=jnp.int32)[None, :, None]).astype(F32)
    owned_hit = (child_map == owned).astype(F32)
    strip_keep = jnp.einsum("hga,hab->hgb", lead_hit, present)
    strip_keep = jnp.sum(strip_keep * owned_hit[:, None, :], axis=-1)
    strip_keep = (strip_keep > 0.5).astype(jnp.int32).reshape(ROWS)
    strip_place = jnp.where(strip_has, strip_place, 0).reshape(ROWS)

    axes = ("row", "col")
    number = lambda r, c: r * COLS + c

    parent_strip = None
    for i in range(NLEAD):
        pairs = [(number(r, 0), number((8 * r + i) % 16, r // 2)) for r in range(ROWS)]
        part = lax.ppermute(parent_front[i * BLOCK : (i + 1) * BLOCK, :LEAD], axes, pairs)
        parent_strip = part if parent_strip is None else parent_strip + part

    early = pack_early(jnp.concatenate([send_cols, send_rows[:1]]), children)
    early = lax.all_to_all(early, "col", split_axis=0, concat_axis=0, tiled=True)
    early = pick_early(pick_owner, early)
    early = lax.all_to_all(early, "row", split_axis=0, concat_axis=0, tiled=True)
    strip = assemble_strip(strip_place, strip_keep, parent_strip, early)

    half = BLOCK // 2
    lead = None
    for part in range(2):
        pairs = [(number(j, 0), number(2 * j + part, 0)) for j in range(NLEAD)]
        piece = lax.ppermute(strip[part * half : (part + 1) * half], axes, pairs)
        lead = piece if lead is None else lead + piece
    lead = lax.all_gather(lead, "col", axis=0, tiled=False)[0]
    lead = lax.all_gather(lead, "row", axis=0, tiled=True)

    col_strip = lax.all_gather(strip, "row", axis=0, tiled=True)
    pairs = [(number(j % 16, j // 16), number(j // 8, j % 8)) for j in range(128)]
    row_strip = lax.ppermute(strip, axes, pairs)
    row_strip = lax.all_gather(row_strip, "col", axis=0, tiled=True)

    outgoing = pack_columns(send_cols, children)
    arrived = lax.all_to_all(outgoing, "col", split_axis=0, concat_axis=0, tiled=True)
    arrived = arrived.reshape(2 * COLS, GRP, BLOCK, BLOCK)
    outgoing = pack_rows(send_rows, pick_cols, arrived)
    arrived = lax.all_to_all(outgoing, "row", split_axis=0, concat_axis=0, tiled=True)

    inv_hi, inv_lo = factor_lead(lead)
    flags = jnp.stack([row_index, col_index]).astype(jnp.int32)
    front = update_front(flags, row_strip, col_strip, inv_hi, inv_lo, parent_front)
    return place_children(source, col_rank, keep, front, arrived)


def solution(mesh):
    in_specs = (P("row", "col"), P("row", "col"), P(), P())
    out_specs = P("row", "col")
    return jax.shard_map(body, mesh=mesh, in_specs=in_specs, out_specs=out_specs, check_vma=False)
```

```python
import functools

import jax
import jax.numpy as jnp
from jax import lax
from jax.experimental import pallas as pl
from jax.experimental.pallas import tpu as pltpu
from jax.sharding import PartitionSpec as P

BLOCK = 128
LEAD = 1024
NLEAD = LEAD // BLOCK
GRP = 10
ROWS = 16
COLS = 8
VMEM = 56 * 1024 * 1024
F32 = jnp.float32
BF16 = jnp.bfloat16


def params(**kw):
    return pltpu.CompilerParams(vmem_limit_bytes=VMEM, **kw)


def cost(flops, bytes_accessed):
    return pl.CostEstimate(flops=flops, bytes_accessed=bytes_accessed, transcendentals=0)


def gather_call(kernel, tables, arrays, shapes, scratch, sems, name, after=()):
    moved = sum(4 * functools.reduce(lambda x, y: x * y, shape) for shape in shapes)
    count = len(tables) + len(arrays)

    def run(*refs):
        kernel(*refs[:count], *refs[count + len(after) :])

    return pl.pallas_call(
        run,
        in_specs=[pl.BlockSpec(memory_space=pltpu.SMEM)] * len(tables)
        + [pl.BlockSpec(memory_space=pl.ANY)] * (len(arrays) + len(after)),
        out_specs=[pl.BlockSpec(memory_space=pl.ANY)] * len(shapes),
        out_shape=[jax.ShapeDtypeStruct(shape, F32) for shape in shapes],
        scratch_shapes=[pltpu.VMEM(shape, F32) for shape in scratch]
        + [pltpu.SemaphoreType.DMA(sems), pltpu.SemaphoreType.DMA(sems)],
        compiler_params=params(),
        cost_estimate=cost(0, 2 * moved),
        name=name,
    )(*tables, *arrays, *after)


def lanes_of(block):
    return pl.ds(pl.multiple_of(block * BLOCK, BLOCK), BLOCK)


def relay(moves, sem_in, sem_out):
    first = [pltpu.make_async_copy(s, v, sem_in.at[n]) for n, (s, v, t) in enumerate(moves)]
    second = [pltpu.make_async_copy(v, t, sem_out.at[n]) for n, (s, v, t) in enumerate(moves)]
    for copy in first:
        copy.start()
    for one, other in zip(first, second):
        one.wait()
        other.start()
    for copy in second:
        copy.wait()


def pack_first_kernel(table, children, *refs):
    outs, early = refs[:COLS], refs[COLS]
    wide, small, sem_in, sem_out = refs[COLS + 1 :]
    moves = []
    for s in range(2 * COLS):
        source = children.at[lanes_of(table[3 * COLS]), lanes_of(table[COLS + s])]
        moves.append((source, small.at[s], early.at[s]))
    for s in range(COLS):
        moves.append((children.at[:, lanes_of(table[s])], wide.at[s], outs[s]))
    relay(moves, sem_in, sem_out)


def pack_first(table, children):
    wide = (children.shape[0], BLOCK)
    small = (2 * COLS, BLOCK, BLOCK)
    return gather_call(
        pack_first_kernel,
        [table],
        [children],
        [wide] * COLS + [small],
        [(COLS,) + wide, small],
        (3 * COLS,),
        "pack_first",
    )


def pack_second_kernel(table, children, *refs):
    wide, sem_in, sem_out = refs[COLS:]
    moves = [
        (children.at[:, lanes_of(table[s])], wide.at[s], refs[s]) for s in range(COLS)
    ]
    relay(moves, sem_in, sem_out)


def pack_second(table, children, after):
    wide = (children.shape[0], BLOCK)
    return gather_call(
        pack_second_kernel,
        [table],
        [children],
        [wide] * COLS,
        [(COLS,) + wide],
        (COLS,),
        "pack_second",
        after,
    )


def cut_kernel(parent, *refs):
    held, sem_in, sem_out = refs[NLEAD:]
    moves = []
    for i in range(NLEAD):
        source = parent.at[pl.ds(i * BLOCK, BLOCK), pl.ds(0, LEAD)]
        moves.append((source, held.at[i], refs[i]))
    relay(moves, sem_in, sem_out)


def cut_strip(parent):
    shape = (BLOCK, LEAD)
    return gather_call(
        cut_kernel, [], [parent], [shape] * NLEAD, [(NLEAD,) + shape], (NLEAD,), "cut_strip"
    )


def pick_early_kernel(table, blocks, out, held, sem_in, sem_out):
    relay([(blocks.at[table[s]], held.at[s], out.at[s]) for s in range(ROWS)], sem_in, sem_out)


def pick_early(table, blocks, after):
    shape = (ROWS, BLOCK, BLOCK)
    return gather_call(
        pick_early_kernel, [table], [blocks], [shape], [shape], (ROWS,), "pick_early", after
    )[0]


HALF = GRP // 2


def pack_rows_kernel(row_table, row_has, origin, *refs):
    sources, (out, held, sem_in, sem_out) = refs[:-4], refs[-4:]

    def each(act):
        def one(r, carry):
            @pl.when(row_has[r] != 0)
            def _():
                act(r)

            return carry

        lax.fori_loop(0, ROWS, one, 0)

    def start(r):
        for k in range(HALF):
            for n, source in enumerate(sources):

                @pl.when(origin[k] == n)
                def _():
                    pltpu.make_async_copy(
                        source.at[row_table[r]], held.at[r, k], sem_in.at[r, k]
                    ).start()

    def leave(r):
        return pltpu.make_async_copy(held.at[r], out.at[r], sem_out.at[r, 0])

    def send(r):
        for k in range(HALF):
            pltpu.make_async_copy(sources[0].at[0], held.at[r, k], sem_in.at[r, k]).wait()
        leave(r).start()

    each(start)
    each(send)
    each(lambda r: leave(r).wait())


def pack_rows(row_table, row_has, origin, arrays, after):
    arrays = [x.reshape(GRP, BLOCK, BLOCK) for x in arrays]
    shape = (ROWS, HALF, BLOCK, BLOCK)
    return gather_call(
        pack_rows_kernel,
        [row_table, row_has, origin],
        arrays,
        [shape],
        [shape],
        (ROWS, HALF),
        "pack_rows",
        after,
    )[0]


def strip_kernel(place, keep, parent, blocks, *refs):
    out = refs[-1]
    out[...] = parent[...]
    for s in range(ROWS):

        @pl.when(keep[s] != 0)
        def _():
            at = lanes_of(place[s])
            out[:, at] = out[:, at] + blocks[s].T


def assemble_strip(place, keep, parent, blocks, after):
    vmem = pl.BlockSpec(memory_space=pltpu.VMEM)
    smem = pl.BlockSpec(memory_space=pltpu.SMEM)
    return pl.pallas_call(
        strip_kernel,
        in_specs=[smem, smem, vmem, vmem] + [pl.BlockSpec(memory_space=pl.ANY)] * len(after),
        out_specs=vmem,
        out_shape=jax.ShapeDtypeStruct((BLOCK, LEAD), F32),
        compiler_params=params(),
        cost_estimate=cost(0, 2 << 20),
        name="assemble_strip",
    )(place, keep, parent, blocks, *after)


def split(x):
    hi = x.astype(BF16)
    return hi, (x - hi.astype(F32)).astype(BF16)


def dot3(a_hi, a_lo, b_hi, b_lo):
    dims = (((1,), (1,)), ((), ()))
    total = lax.dot_general(a_hi, b_lo, dims, preferred_element_type=F32)
    total += lax.dot_general(a_lo, b_hi, dims, preferred_element_type=F32)
    return total + lax.dot_general(a_hi, b_hi, dims, preferred_element_type=F32)


def dot_full(a, b, dims):
    return lax.dot_general(
        a, b, (dims, ((), ())), precision=lax.Precision.HIGHEST, preferred_element_type=F32
    )


def invert_diagonal(work):
    lanes = lax.broadcasted_iota(jnp.int32, (BLOCK, BLOCK), 1)
    rows = lax.broadcasted_iota(jnp.int32, (BLOCK, BLOCK), 0)
    lane8 = lax.broadcasted_iota(jnp.int32, (8, BLOCK), 1)
    row8 = lax.broadcasted_iota(jnp.int32, (8, BLOCK), 0)
    done = []
    for t in range(BLOCK // 8):
        base = 8 * t
        part = work[0:8]
        cols = [jnp.broadcast_to(part[:, base + i : base + i + 1], (8, BLOCK)) for i in range(8)]
        pivots = jnp.zeros((8, BLOCK), F32)
        for i in range(8):
            pivot = jnp.broadcast_to(cols[i][i : i + 1], (8, BLOCK))
            pivots = jnp.where(row8 == i, pivot, pivots)
            factor = jnp.where(row8 > i, cols[i] / pivot, 0.0)
            for other in range(i + 1, 8):
                cols[other] = cols[other] - factor * jnp.broadcast_to(cols[other][i : i + 1], (8, BLOCK))
            row = jnp.broadcast_to(part[i : i + 1], (8, BLOCK))
            row = jnp.where(lane8 == base + i, 1.0, row)
            part = jnp.where((lane8 == base + i) & (row8 > i), 0.0, part)
            part = jnp.where((lane8 == base + i) & (row8 == i), 1.0, part)
            part = part - factor * row
        part = part * lax.rsqrt(pivots)
        done.append(part)
        if t < BLOCK // 8 - 1:
            above = (lane8 > base + row8) & (lane8 < base + 8)
            update = dot_full(part[:, base + 8 :], jnp.where(above, 0.0, part), ((0,), (0,)))
            work = work[8:]
            inside = (lanes[: work.shape[0]] >= base) & (lanes[: work.shape[0]] < base + 8)
            work = jnp.where(inside, 0.0, work) - update
    whole = jnp.concatenate(done, axis=0)
    return jnp.where(rows >= lanes, whole, 0.0)


def factor_kernel(first, count, last, given, after, *refs):
    work = refs[-1] if last else refs[0]
    work[...] = given[...]
    total = LEAD // BLOCK

    def step(k, carry):
        here = lanes_of(k)
        inverse = invert_diagonal(work[here, here])
        work[here, :] = dot_full(inverse, work[here, :], ((1,), (0,)))
        work[here, here] = inverse

        def below(i, carry):
            there = lanes_of(i)
            lower = work[here, there]
            work[there, here] = jnp.zeros((BLOCK, BLOCK), F32)
            work[there, :] = work[there, :] - dot_full(lower, work[here, :], ((0,), (0,)))
            return carry

        return lax.fori_loop(k + 1, total, below, carry)

    lax.fori_loop(first, first + count, step, 0)
    if not last:
        return
    inv_hi, inv_lo = refs[0], refs[1]

    def finish(k, carry):
        here = lanes_of(k)
        rows = lax.broadcasted_iota(jnp.int32, (BLOCK, LEAD), 0) + k * BLOCK
        lanes = lax.broadcasted_iota(jnp.int32, (BLOCK, LEAD), 1)
        hi, lo = split(jnp.where(rows >= lanes, work[here, :], 0.0))
        inv_hi[here, :] = hi
        inv_lo[here, :] = lo
        return carry

    lax.fori_loop(0, total, finish, 0)


PARTS = 4


def factor_part(part, work, after):
    count = LEAD // BLOCK // PARTS
    whole = pl.BlockSpec(memory_space=pltpu.VMEM)
    last = part == PARTS - 1
    half = jax.ShapeDtypeStruct((LEAD, LEAD), BF16)
    full = jax.ShapeDtypeStruct((LEAD, LEAD), F32)
    return pl.pallas_call(
        functools.partial(factor_kernel, part * count, count, last),
        in_specs=[whole, pl.BlockSpec(memory_space=pl.ANY)],
        out_specs=[whole] * 2 if last else whole,
        out_shape=(half, half) if last else full,
        scratch_shapes=[pltpu.VMEM((LEAD, LEAD), F32)] if last else [],
        compiler_params=params(),
        cost_estimate=cost(25 * 10**9, 8 << 20),
        name="factor_lead",
    )(work, after)


TILE = 256


def solve_rows(rows, inv_hi, inv_lo):
    hi, lo = split(rows)
    parts = []
    for n in range(LEAD // TILE):
        at, upto = pl.ds(n * TILE, TILE), (n + 1) * TILE
        parts.append(
            dot3(hi[:, :upto], lo[:, :upto], inv_hi[at, pl.ds(0, upto)], inv_lo[at, pl.ds(0, upto)])
        )
    return jnp.concatenate(parts, axis=1)


def update_kernel(flags, row_strip, col_strip, inv_hi, inv_lo, parent, out, panel, hi, lo):
    step = pl.program_id(0)

    @pl.when(step == 0)
    def _():
        def chunk(n, carry):
            at = pl.ds(pl.multiple_of(n * TILE, TILE), TILE)
            values = solve_rows(row_strip[at, :], inv_hi, inv_lo)
            panel[at, :] = values
            hi[at, :], lo[at, :] = split(values)
            return carry

        lax.fori_loop(0, LEAD // TILE, chunk, 0)

    in_panel = (flags[1] == 0) & (step < LEAD // TILE)
    top = flags[0] == 0

    @pl.when(in_panel)
    def _():
        at = pl.ds(pl.multiple_of(step * TILE, TILE), TILE)
        rows = lax.broadcasted_iota(jnp.int32, (LEAD, TILE), 0)
        lanes = lax.broadcasted_iota(jnp.int32, (LEAD, TILE), 1) + step * TILE
        out[...] = jnp.where((rows >= lanes) | jnp.logical_not(top), panel[:, at], 0.0)

    @pl.when(jnp.logical_not(in_panel) & top)
    def _():
        out[...] = jnp.zeros_like(out)

    @pl.when(jnp.logical_not(in_panel) & jnp.logical_not(top))
    def _():
        right = split(solve_rows(col_strip[...], inv_hi, inv_lo))

        def chunk(n, carry):
            at = pl.ds(pl.multiple_of(n * TILE, TILE), TILE)
            out[at, :] = parent[at, :] - dot3(hi[at, :], lo[at, :], *right)
            return carry

        lax.fori_loop(0, LEAD // TILE, chunk, 0)


def update_front(flags, row_strip, col_strip, inv_hi, inv_lo, parent):
    rows, columns = parent.shape
    whole = lambda t, f: (0, 0)
    return pl.pallas_call(
        update_kernel,
        grid_spec=pltpu.PrefetchScalarGridSpec(
            num_scalar_prefetch=1,
            grid=(columns // TILE,),
            in_specs=[
                pl.BlockSpec((LEAD, LEAD), whole),
                pl.BlockSpec((TILE, LEAD), lambda t, f: (t, 0)),
                pl.BlockSpec((LEAD, LEAD), whole),
                pl.BlockSpec((LEAD, LEAD), whole),
                pl.BlockSpec((rows, TILE), lambda t, f: (0, t)),
            ],
            out_specs=pl.BlockSpec((rows, TILE), lambda t, f: (0, t)),
            scratch_shapes=[
                pltpu.VMEM((LEAD, LEAD), F32),
                pltpu.VMEM((LEAD, LEAD), BF16),
                pltpu.VMEM((LEAD, LEAD), BF16),
            ],
        ),
        out_shape=jax.ShapeDtypeStruct((rows, columns), F32),
        compiler_params=params(),
        cost_estimate=cost(40 * 10**9, 32 << 20),
        name="update_front",
    )(flags, row_strip, col_strip, inv_hi, inv_lo, parent)


def place_kernel(source, rank, keep, front, *refs):
    out = refs[-1]
    i = pl.program_id(0)
    for j in range(16):
        at = pl.ds(j * BLOCK, BLOCK)
        value = front[:, at]
        for h in range(2):
            k = rank[h, j]
            near, far = refs[2 * h], refs[2 * h + 1]
            block = jnp.where(
                k < HALF, near[0, jnp.minimum(k, HALF - 1)], far[0, jnp.maximum(k - HALF, 0)]
            )
            value = value + jnp.where(keep[h, i * 16 + j] != 0, block, 0.0)
        out[:, at] = value


def place_children(source, rank, keep, front, near, far):
    rows, columns = front.shape

    def spec(h):
        return pl.BlockSpec((1, HALF, BLOCK, BLOCK), lambda i, s, r, k: (s[h, i], 0, 0, 0))

    return pl.pallas_call(
        place_kernel,
        grid_spec=pltpu.PrefetchScalarGridSpec(
            num_scalar_prefetch=3,
            grid=(rows // BLOCK,),
            in_specs=[pl.BlockSpec((BLOCK, columns), lambda i, s, r, k: (i, 0))]
            + [spec(0), spec(0), spec(1), spec(1)],
            out_specs=pl.BlockSpec((BLOCK, columns), lambda i, s, r, k: (i, 0)),
        ),
        out_shape=jax.ShapeDtypeStruct((rows, columns), F32),
        input_output_aliases={3: 0},
        compiler_params=params(),
        cost_estimate=cost(0, 24 << 20),
        name="place_children",
    )(source, rank, keep, front, near, far, near, far)


def earlier_count(keys):
    places = jnp.arange(keys.shape[-1], dtype=jnp.int32)
    matches = keys[..., :, None] == keys[..., None, :]
    before = places[None, :] < places[:, None]
    return jnp.sum((matches & before).astype(jnp.int32), axis=-1)


def lookup(codes, values, length):
    hits = codes[..., :, None] == jnp.arange(length, dtype=jnp.int32)
    found = jnp.sum(jnp.where(hits, values[..., :, None], 0), axis=-2)
    return found, jnp.any(hits, axis=-2)


def body(parent_front, children, child_map, fill):
    row_index = lax.axis_index("row")
    col_index = lax.axis_index("col")
    child_id = row_index // COLS
    group_row = row_index % COLS
    blocks = child_map.shape[1]
    places = jnp.arange(blocks, dtype=jnp.int32)
    groups = places // GRP
    within = places % GRP
    run16 = child_map // 16
    run8 = child_map // 8
    slot = earlier_count(groups * COLS + run16)
    pick = lambda x: lax.dynamic_index_in_dim(x, child_id, 0, keepdims=False)
    own_map, own_run16, own_run8, own_slot = pick(child_map), pick(run16), pick(run8), pick(slot)

    col_codes = jnp.where(groups == col_index, own_run16 * 2 + own_slot, -1)
    send_cols, _ = lookup(col_codes, within, 2 * COLS)
    row_codes = jnp.where(groups == group_row, own_run8, -1)
    send_rows, sends = lookup(row_codes, within, ROWS)
    ahead = slot[:, None, :] * blocks + places < (slot * blocks + places)[:, :, None]
    rank_all = jnp.sum((ahead & (run16[:, None, :] == run16[:, :, None])).astype(jnp.int32), axis=-1)
    rank_codes = jnp.where(own_run16 == col_index, pick(rank_all), -1)
    incoming = groups * 2 + own_slot
    origin = own_slot * COLS + (col_index - groups) % COLS
    pick_cols, _ = lookup(rank_codes, origin, GRP)
    own_codes = jnp.where(own_run16 == col_index, own_map % 16, -1)
    pick_owner, _ = lookup(own_codes, incoming, 16)

    tile_rows = jnp.where(run8 == row_index, child_map % 8, -1)
    row_block, row_has = lookup(tile_rows, jnp.broadcast_to(places, (2, blocks)), 8)
    tile_cols = jnp.where(run16 == col_index, child_map % 16, -1)
    col_rank, col_has = lookup(tile_cols, rank_all, 16)
    row_hit = (tile_rows[:, None, :] == jnp.arange(8, dtype=jnp.int32)[None, :, None]).astype(F32)
    col_hit = (tile_cols[:, None, :] == jnp.arange(16, dtype=jnp.int32)[None, :, None]).astype(F32)
    present = fill.astype(F32)
    keep = jnp.einsum("hia,hab->hib", row_hit, present)
    keep = jnp.einsum("hib,hjb->hij", keep, col_hit)
    panel_col = (col_index == 0) & (jnp.arange(16) < NLEAD)
    keep = jnp.where(panel_col | (row_index == 0), 0.0, keep)
    keep = (keep > 0.5).astype(jnp.int32).reshape(2, 8 * 16)
    source = jnp.arange(2, dtype=jnp.int32)[:, None] * COLS + row_block // GRP

    owned = col_index * 16 + row_index
    lead_codes = jnp.where(run8 == 0, groups, -1)
    strip_place, strip_has = lookup(lead_codes, child_map, COLS)
    lead_hit = (lead_codes[:, None, :] == jnp.arange(COLS, dtype=jnp.int32)[None, :, None]).astype(F32)
    owned_hit = (child_map == owned).astype(F32)
    strip_keep = jnp.einsum("hga,hab->hgb", lead_hit, present)
    strip_keep = jnp.sum(strip_keep * owned_hit[:, None, :], axis=-1)
    strip_keep = (strip_keep > 0.5).astype(jnp.int32).reshape(ROWS)
    strip_place = jnp.where(strip_has, strip_place, 0).reshape(ROWS)

    axes = ("row", "col")
    number = lambda r, c: r * COLS + c

    total = lambda values: functools.reduce(lambda x, y: x + y, values)

    total = lambda values: functools.reduce(lambda x, y: x + y, values)

    pieces = cut_strip(parent_front)
    own = total([jnp.where(col_index == 0, pieces[0], 0.0)] + [
        lax.ppermute(pieces[i], axes, [(number(r, 0), number(r, i)) for r in range(ROWS)])
        for i in range(1, NLEAD)
    ])
    pairs = [(number(j % 16, j // 16), number(j // 8, j % 8)) for j in range(128)]
    strip_parent = lax.ppermute(own, axes, [(b, a) for a, b in pairs])

    shifts = (col_index + jnp.arange(COLS, dtype=jnp.int32)) % COLS
    table = jnp.concatenate([jnp.take(send_cols, shifts * 2), send_cols, send_rows[:1]])
    *parts, early = pack_first(table, children)
    shift = lambda parts: [parts[0]] + [
        lax.ppermute(parts[d], "col", [(c, (c + d) % COLS) for c in range(COLS)])
        for d in range(1, COLS)
    ]
    first = shift(parts)
    early = lax.all_to_all(early, "col", split_axis=0, concat_axis=0, tiled=True)
    early = pick_early(pick_owner, early, [strip_parent])
    early = lax.all_to_all(early, "row", split_axis=0, concat_axis=0, tiled=True)
    strip = assemble_strip(strip_place, strip_keep, strip_parent, early, first[1:])

    half = BLOCK // 2
    piece = total([
        lax.ppermute(
            strip[part * half : (part + 1) * half],
            axes,
            [(number(j, 0), number(2 * j + part, 0)) for j in range(NLEAD)],
        )
        for part in range(2)
    ])
    piece = total([piece] + [
        lax.ppermute(piece, axes, [(number(r, 0), number(r, d)) for r in range(ROWS)])
        for d in range(1, COLS)
    ])
    lead = lax.all_gather(piece, "row", axis=0, tiled=True)

    row_piece = lax.ppermute(strip, axes, pairs)
    col_strip = lax.all_gather(strip, "row", axis=0, tiled=True)
    row_strip = lax.all_gather(row_piece, "col", axis=0, tiled=True)

    sends = sends.astype(jnp.int32)
    near_out = pack_rows(send_rows, sends, pick_cols[:HALF], first, [piece, row_piece])
    near = lax.all_to_all(near_out, "row", split_axis=0, concat_axis=0, tiled=True)
    parts = pack_second(jnp.take(send_cols, shifts * 2 + 1), children, [near_out])
    second = shift(parts)
    work = factor_part(0, lead, near_out)
    far_out = pack_rows(send_rows, sends, pick_cols[HALF:], first + second, [near, work])
    far = lax.all_to_all(far_out, "row", split_axis=0, concat_axis=0, tiled=True)

    work = factor_part(1, work, far_out)
    work = factor_part(2, work, far_out)
    inv_hi, inv_lo = factor_part(3, work, far_out)
    flags = jnp.stack([row_index, col_index]).astype(jnp.int32)
    front = update_front(flags, row_strip, col_strip, inv_hi, inv_lo, parent_front)
    return place_children(source, col_rank, keep, front, near, far)


def solution(mesh):
    in_specs = (P("row", "col"), P("row", "col"), P(), P())
    out_specs = P("row", "col")
    return jax.shard_map(body, mesh=mesh, in_specs=in_specs, out_specs=out_specs, check_vma=False)
```

```python
import functools

import jax
import jax.numpy as jnp
from jax import lax
from jax.experimental import pallas as pl
from jax.experimental.pallas import tpu as pltpu
from jax.sharding import PartitionSpec as P

BLOCK = 128
LEAD = 1024
NLEAD = LEAD // BLOCK
GRP = 10
ROWS = 16
COLS = 8
VMEM = 56 * 1024 * 1024
F32 = jnp.float32
BF16 = jnp.bfloat16


def params(**kw):
    return pltpu.CompilerParams(vmem_limit_bytes=VMEM, **kw)


def cost(flops, bytes_accessed):
    return pl.CostEstimate(flops=flops, bytes_accessed=bytes_accessed, transcendentals=0)


def gather_call(kernel, tables, arrays, shapes, scratch, sems, name, after=()):
    moved = sum(4 * functools.reduce(lambda x, y: x * y, shape) for shape in shapes)
    count = len(tables) + len(arrays)

    def run(*refs):
        kernel(*refs[:count], *refs[count + len(after) :])

    return pl.pallas_call(
        run,
        in_specs=[pl.BlockSpec(memory_space=pltpu.SMEM)] * len(tables)
        + [pl.BlockSpec(memory_space=pl.ANY)] * (len(arrays) + len(after)),
        out_specs=[pl.BlockSpec(memory_space=pl.ANY)] * len(shapes),
        out_shape=[jax.ShapeDtypeStruct(shape, F32) for shape in shapes],
        scratch_shapes=[pltpu.VMEM(shape, F32) for shape in scratch]
        + [pltpu.SemaphoreType.DMA(sems), pltpu.SemaphoreType.DMA(sems)],
        compiler_params=params(),
        cost_estimate=cost(0, 2 * moved),
        name=name,
    )(*tables, *arrays, *after)


def lanes_of(block):
    return pl.ds(pl.multiple_of(block * BLOCK, BLOCK), BLOCK)


def relay(moves, sem_in, sem_out):
    first = [pltpu.make_async_copy(s, v, sem_in.at[n]) for n, (s, v, t) in enumerate(moves)]
    second = [pltpu.make_async_copy(v, t, sem_out.at[n]) for n, (s, v, t) in enumerate(moves)]
    for copy in first:
        copy.start()
    for one, other in zip(first, second):
        one.wait()
        other.start()
    for copy in second:
        copy.wait()


def pack_early_kernel(table, children, out, held, sem_in, sem_out):
    moves = []
    for s in range(2 * COLS):
        source = children.at[lanes_of(table[2 * COLS]), lanes_of(table[s])]
        moves.append((source, held.at[s], out.at[s]))
    relay(moves, sem_in, sem_out)


def pack_early(table, children):
    shape = (2 * COLS, BLOCK, BLOCK)
    return gather_call(
        pack_early_kernel, [table], [children], [shape], [shape], (2 * COLS,), "pack_early"
    )[0]


def pack_first_kernel(table, children, out, held, sem_in, sem_out):
    moves = [
        (children.at[:, lanes_of(table[s])], held.at[s], out.at[s]) for s in range(COLS)
    ]
    relay(moves, sem_in, sem_out)


def pack_first(table, children, after):
    shape = (COLS, children.shape[0], BLOCK)
    return gather_call(
        pack_first_kernel, [table], [children], [shape], [shape], (COLS,), "pack_first", after
    )[0]


def pack_second_kernel(table, children, *refs):
    wide, sem_in, sem_out = refs[COLS:]
    moves = [
        (children.at[:, lanes_of(table[s])], wide.at[s], refs[s]) for s in range(COLS)
    ]
    relay(moves, sem_in, sem_out)


def pack_second(table, children, after):
    wide = (children.shape[0], BLOCK)
    return gather_call(
        pack_second_kernel,
        [table],
        [children],
        [wide] * COLS,
        [(COLS,) + wide],
        (COLS,),
        "pack_second",
        after,
    )


def cut_kernel(parent, *refs):
    held, sem_in, sem_out = refs[NLEAD:]
    moves = []
    for i in range(NLEAD):
        source = parent.at[pl.ds(i * BLOCK, BLOCK), pl.ds(0, LEAD)]
        moves.append((source, held.at[i], refs[i]))
    relay(moves, sem_in, sem_out)


def cut_strip(parent):
    shape = (BLOCK, LEAD)
    return gather_call(
        cut_kernel, [], [parent], [shape] * NLEAD, [(NLEAD,) + shape], (NLEAD,), "cut_strip"
    )


def pick_early_kernel(table, blocks, out, held, sem_in, sem_out):
    relay([(blocks.at[table[s]], held.at[s], out.at[s]) for s in range(ROWS)], sem_in, sem_out)


def pick_early(table, blocks, after):
    shape = (ROWS, BLOCK, BLOCK)
    return gather_call(
        pick_early_kernel, [table], [blocks], [shape], [shape], (ROWS,), "pick_early", after
    )[0]


HALF = GRP // 2


def pack_rows_kernel(row_table, row_has, origin, first, *refs):
    second, (out, held, sem_in, sem_out) = refs[:-4], refs[-4:]

    def each(act):
        def one(r, carry):
            @pl.when(row_has[r] != 0)
            def _():
                act(r)

            return carry

        lax.fori_loop(0, ROWS, one, 0)

    def start(r):
        for k in range(HALF):
            target = (held.at[r, k], sem_in.at[r, k])

            @pl.when(origin[k] < COLS)
            def _():
                pltpu.make_async_copy(first.at[origin[k], row_table[r]], *target).start()

            for n, source in enumerate(second):

                @pl.when(origin[k] == COLS + n)
                def _():
                    pltpu.make_async_copy(source.at[row_table[r]], *target).start()

    def leave(r):
        return pltpu.make_async_copy(held.at[r], out.at[r], sem_out.at[r, 0])

    def send(r):
        for k in range(HALF):
            pltpu.make_async_copy(first.at[0, 0], held.at[r, k], sem_in.at[r, k]).wait()
        leave(r).start()

    each(start)
    each(send)
    each(lambda r: leave(r).wait())


def pack_rows(row_table, row_has, origin, first, second, after):
    first = first.reshape(COLS, GRP, BLOCK, BLOCK)
    second = [x.reshape(GRP, BLOCK, BLOCK) for x in second]
    shape = (ROWS, HALF, BLOCK, BLOCK)
    return gather_call(
        pack_rows_kernel,
        [row_table, row_has, origin],
        [first] + second,
        [shape],
        [shape],
        (ROWS, HALF),
        "pack_rows",
        after,
    )[0]


def strip_kernel(place, keep, parent, blocks, *refs):
    out = refs[-1]
    out[...] = parent[...]
    for s in range(ROWS):

        @pl.when(keep[s] != 0)
        def _():
            at = lanes_of(place[s])
            out[:, at] = out[:, at] + blocks[s].T


def assemble_strip(place, keep, parent, blocks, after):
    vmem = pl.BlockSpec(memory_space=pltpu.VMEM)
    smem = pl.BlockSpec(memory_space=pltpu.SMEM)
    return pl.pallas_call(
        strip_kernel,
        in_specs=[smem, smem, vmem, vmem] + [pl.BlockSpec(memory_space=pl.ANY)] * len(after),
        out_specs=vmem,
        out_shape=jax.ShapeDtypeStruct((BLOCK, LEAD), F32),
        compiler_params=params(),
        cost_estimate=cost(0, 2 << 20),
        name="assemble_strip",
    )(place, keep, parent, blocks, *after)


def split(x):
    hi = x.astype(BF16)
    return hi, (x - hi.astype(F32)).astype(BF16)


def dot3(a_hi, a_lo, b_hi, b_lo):
    dims = (((1,), (1,)), ((), ()))
    total = lax.dot_general(a_hi, b_lo, dims, preferred_element_type=F32)
    total += lax.dot_general(a_lo, b_hi, dims, preferred_element_type=F32)
    return total + lax.dot_general(a_hi, b_hi, dims, preferred_element_type=F32)


def dot_full(a, b, dims):
    return lax.dot_general(
        a, b, (dims, ((), ())), precision=lax.Precision.HIGHEST, preferred_element_type=F32
    )


def invert_diagonal(work):
    lanes = lax.broadcasted_iota(jnp.int32, (BLOCK, BLOCK), 1)
    rows = lax.broadcasted_iota(jnp.int32, (BLOCK, BLOCK), 0)
    lane8 = lax.broadcasted_iota(jnp.int32, (8, BLOCK), 1)
    row8 = lax.broadcasted_iota(jnp.int32, (8, BLOCK), 0)
    done = []
    for t in range(BLOCK // 8):
        base = 8 * t
        part = work[0:8]
        cols = [jnp.broadcast_to(part[:, base + i : base + i + 1], (8, BLOCK)) for i in range(8)]
        pivots = jnp.zeros((8, BLOCK), F32)
        for i in range(8):
            pivot = jnp.broadcast_to(cols[i][i : i + 1], (8, BLOCK))
            pivots = jnp.where(row8 == i, pivot, pivots)
            factor = jnp.where(row8 > i, cols[i] / pivot, 0.0)
            for other in range(i + 1, 8):
                cols[other] = cols[other] - factor * jnp.broadcast_to(cols[other][i : i + 1], (8, BLOCK))
            row = jnp.broadcast_to(part[i : i + 1], (8, BLOCK))
            row = jnp.where(lane8 == base + i, 1.0, row)
            part = jnp.where((lane8 == base + i) & (row8 > i), 0.0, part)
            part = jnp.where((lane8 == base + i) & (row8 == i), 1.0, part)
            part = part - factor * row
        part = part * lax.rsqrt(pivots)
        done.append(part)
        if t < BLOCK // 8 - 1:
            above = (lane8 > base + row8) & (lane8 < base + 8)
            update = dot_full(part[:, base + 8 :], jnp.where(above, 0.0, part), ((0,), (0,)))
            work = work[8:]
            inside = (lanes[: work.shape[0]] >= base) & (lanes[: work.shape[0]] < base + 8)
            work = jnp.where(inside, 0.0, work) - update
    whole = jnp.concatenate(done, axis=0)
    return jnp.where(rows >= lanes, whole, 0.0)


def factor_kernel(first, count, last, *refs):
    if first == 0:
        parity, mine, other, _, work = refs
        rows = LEAD // 2 // ROWS

        def join(r, carry):
            source = pl.ds(pl.multiple_of(r * rows, rows), rows)
            low = pl.ds(pl.multiple_of(2 * r * rows, rows), rows)
            high = pl.ds(pl.multiple_of((2 * r + 1) * rows, rows), rows)
            even = parity[0] == 0
            work[low, :] = jnp.where(even, mine[source, :], other[source, :])
            work[high, :] = jnp.where(even, other[source, :], mine[source, :])
            return carry

        lax.fori_loop(0, ROWS, join, 0)
    else:
        given, _, *refs = refs
        work = refs[-1] if last else refs[0]
        work[...] = given[...]
    total = LEAD // BLOCK

    def step(k, carry):
        here = lanes_of(k)
        inverse = invert_diagonal(work[here, here])
        work[here, :] = dot_full(inverse, work[here, :], ((1,), (0,)))
        work[here, here] = inverse

        def below(i, carry):
            there = lanes_of(i)
            lower = work[here, there]
            work[there, here] = jnp.zeros((BLOCK, BLOCK), F32)
            work[there, :] = work[there, :] - dot_full(lower, work[here, :], ((0,), (0,)))
            return carry

        return lax.fori_loop(k + 1, total, below, carry)

    lax.fori_loop(first, first + count, step, 0)
    if not last:
        return
    inv_hi, inv_lo = refs[0], refs[1]

    def finish(k, carry):
        here = lanes_of(k)
        rows = lax.broadcasted_iota(jnp.int32, (BLOCK, LEAD), 0) + k * BLOCK
        lanes = lax.broadcasted_iota(jnp.int32, (BLOCK, LEAD), 1)
        hi, lo = split(jnp.where(rows >= lanes, work[here, :], 0.0))
        inv_hi[here, :] = hi
        inv_lo[here, :] = lo
        return carry

    lax.fori_loop(0, total, finish, 0)


PARTS = 4


def factor_part(part, given, after):
    count = LEAD // BLOCK // PARTS
    whole = pl.BlockSpec(memory_space=pltpu.VMEM)
    last = part == PARTS - 1
    half = jax.ShapeDtypeStruct((LEAD, LEAD), BF16)
    full = jax.ShapeDtypeStruct((LEAD, LEAD), F32)
    return pl.pallas_call(
        functools.partial(factor_kernel, part * count, count, last),
        in_specs=([pl.BlockSpec(memory_space=pltpu.SMEM), whole] if part == 0 else [])
        + [whole, pl.BlockSpec(memory_space=pl.ANY)],
        out_specs=[whole] * 2 if last else whole,
        out_shape=(half, half) if last else full,
        scratch_shapes=[pltpu.VMEM((LEAD, LEAD), F32)] if last else [],
        compiler_params=params(),
        cost_estimate=cost(25 * 10**9, 8 << 20),
        name="factor_lead",
    )(*given, after)


TILE = 256


def solve_rows(rows, inv_hi, inv_lo):
    hi, lo = split(rows)
    parts = []
    for n in range(LEAD // TILE):
        at, upto = pl.ds(n * TILE, TILE), (n + 1) * TILE
        parts.append(
            dot3(hi[:, :upto], lo[:, :upto], inv_hi[at, pl.ds(0, upto)], inv_lo[at, pl.ds(0, upto)])
        )
    return jnp.concatenate(parts, axis=1)


def update_kernel(flags, row_strip, col_strip, inv_hi, inv_lo, parent, out, panel, hi, lo):
    step = pl.program_id(0)

    @pl.when(step == 0)
    def _():
        def chunk(n, carry):
            at = pl.ds(pl.multiple_of(n * TILE, TILE), TILE)
            values = solve_rows(row_strip[at, :], inv_hi, inv_lo)
            panel[at, :] = values
            hi[at, :], lo[at, :] = split(values)
            return carry

        lax.fori_loop(0, LEAD // TILE, chunk, 0)

    in_panel = (flags[1] == 0) & (step < LEAD // TILE)
    top = flags[0] == 0

    @pl.when(in_panel)
    def _():
        at = pl.ds(pl.multiple_of(step * TILE, TILE), TILE)
        rows = lax.broadcasted_iota(jnp.int32, (LEAD, TILE), 0)
        lanes = lax.broadcasted_iota(jnp.int32, (LEAD, TILE), 1) + step * TILE
        out[...] = jnp.where((rows >= lanes) | jnp.logical_not(top), panel[:, at], 0.0)

    @pl.when(jnp.logical_not(in_panel) & top)
    def _():
        out[...] = jnp.zeros_like(out)

    @pl.when(jnp.logical_not(in_panel) & jnp.logical_not(top))
    def _():
        right = split(solve_rows(col_strip[...], inv_hi, inv_lo))

        def chunk(n, carry):
            at = pl.ds(pl.multiple_of(n * TILE, TILE), TILE)
            out[at, :] = parent[at, :] - dot3(hi[at, :], lo[at, :], *right)
            return carry

        lax.fori_loop(0, LEAD // TILE, chunk, 0)


def update_front(flags, row_strip, col_strip, inv_hi, inv_lo, parent):
    rows, columns = parent.shape
    whole = lambda t, f: (0, 0)
    return pl.pallas_call(
        update_kernel,
        grid_spec=pltpu.PrefetchScalarGridSpec(
            num_scalar_prefetch=1,
            grid=(columns // TILE,),
            in_specs=[
                pl.BlockSpec((LEAD, LEAD), whole),
                pl.BlockSpec((TILE, LEAD), lambda t, f: (t, 0)),
                pl.BlockSpec((LEAD, LEAD), whole),
                pl.BlockSpec((LEAD, LEAD), whole),
                pl.BlockSpec((rows, TILE), lambda t, f: (0, t)),
            ],
            out_specs=pl.BlockSpec((rows, TILE), lambda t, f: (0, t)),
            scratch_shapes=[
                pltpu.VMEM((LEAD, LEAD), F32),
                pltpu.VMEM((LEAD, LEAD), BF16),
                pltpu.VMEM((LEAD, LEAD), BF16),
            ],
        ),
        out_shape=jax.ShapeDtypeStruct((rows, columns), F32),
        compiler_params=params(),
        cost_estimate=cost(40 * 10**9, 32 << 20),
        name="update_front",
    )(flags, row_strip, col_strip, inv_hi, inv_lo, parent)


def place_kernel(source, rank, keep, front, *refs):
    out = refs[-1]
    i = pl.program_id(0)
    for j in range(16):
        at = pl.ds(j * BLOCK, BLOCK)
        value = front[:, at]
        for h in range(2):
            k = rank[h, j]
            near, far = refs[2 * h], refs[2 * h + 1]
            block = jnp.where(
                k < HALF, near[0, jnp.minimum(k, HALF - 1)], far[0, jnp.maximum(k - HALF, 0)]
            )
            value = value + jnp.where(keep[h, i * 16 + j] != 0, block, 0.0)
        out[:, at] = value


def place_children(source, rank, keep, front, near, far):
    rows, columns = front.shape

    def spec(h):
        return pl.BlockSpec((1, HALF, BLOCK, BLOCK), lambda i, s, r, k: (s[h, i], 0, 0, 0))

    return pl.pallas_call(
        place_kernel,
        grid_spec=pltpu.PrefetchScalarGridSpec(
            num_scalar_prefetch=3,
            grid=(rows // BLOCK,),
            in_specs=[pl.BlockSpec((BLOCK, columns), lambda i, s, r, k: (i, 0))]
            + [spec(0), spec(0), spec(1), spec(1)],
            out_specs=pl.BlockSpec((BLOCK, columns), lambda i, s, r, k: (i, 0)),
        ),
        out_shape=jax.ShapeDtypeStruct((rows, columns), F32),
        input_output_aliases={3: 0},
        compiler_params=params(),
        cost_estimate=cost(0, 24 << 20),
        name="place_children",
    )(source, rank, keep, front, near, far, near, far)


def earlier_count(keys):
    places = jnp.arange(keys.shape[-1], dtype=jnp.int32)
    matches = keys[..., :, None] == keys[..., None, :]
    before = places[None, :] < places[:, None]
    return jnp.sum((matches & before).astype(jnp.int32), axis=-1)


def lookup(codes, values, length):
    hits = codes[..., :, None] == jnp.arange(length, dtype=jnp.int32)
    found = jnp.sum(jnp.where(hits, values[..., :, None], 0), axis=-2)
    return found, jnp.any(hits, axis=-2)


def body(parent_front, children, child_map, fill):
    row_index = lax.axis_index("row")
    col_index = lax.axis_index("col")
    child_id = row_index // COLS
    group_row = row_index % COLS
    blocks = child_map.shape[1]
    places = jnp.arange(blocks, dtype=jnp.int32)
    groups = places // GRP
    within = places % GRP
    run16 = child_map // 16
    run8 = child_map // 8
    slot = earlier_count(groups * COLS + run16)
    pick = lambda x: lax.dynamic_index_in_dim(x, child_id, 0, keepdims=False)
    own_map, own_run16, own_run8, own_slot = pick(child_map), pick(run16), pick(run8), pick(slot)

    col_codes = jnp.where(groups == col_index, own_run16 * 2 + own_slot, -1)
    send_cols, _ = lookup(col_codes, within, 2 * COLS)
    row_codes = jnp.where(groups == group_row, own_run8, -1)
    send_rows, sends = lookup(row_codes, within, ROWS)
    ahead = slot[:, None, :] * blocks + places < (slot * blocks + places)[:, :, None]
    rank_all = jnp.sum((ahead & (run16[:, None, :] == run16[:, :, None])).astype(jnp.int32), axis=-1)
    rank_codes = jnp.where(own_run16 == col_index, pick(rank_all), -1)
    origin = jnp.where(own_slot == 0, groups, COLS + (col_index - groups) % COLS)
    pick_cols, _ = lookup(rank_codes, origin, GRP)
    own_codes = jnp.where(own_run16 == col_index, own_map % 16, -1)
    pick_owner, _ = lookup(own_codes, groups * 2 + own_slot, 16)

    tile_rows = jnp.where(run8 == row_index, child_map % 8, -1)
    row_block, row_has = lookup(tile_rows, jnp.broadcast_to(places, (2, blocks)), 8)
    tile_cols = jnp.where(run16 == col_index, child_map % 16, -1)
    col_rank, col_has = lookup(tile_cols, rank_all, 16)
    row_hit = (tile_rows[:, None, :] == jnp.arange(8, dtype=jnp.int32)[None, :, None]).astype(F32)
    col_hit = (tile_cols[:, None, :] == jnp.arange(16, dtype=jnp.int32)[None, :, None]).astype(F32)
    present = fill.astype(F32)
    keep = jnp.einsum("hia,hab->hib", row_hit, present)
    keep = jnp.einsum("hib,hjb->hij", keep, col_hit)
    panel_col = (col_index == 0) & (jnp.arange(16) < NLEAD)
    keep = jnp.where(panel_col | (row_index == 0), 0.0, keep)
    keep = (keep > 0.5).astype(jnp.int32).reshape(2, 8 * 16)
    source = jnp.arange(2, dtype=jnp.int32)[:, None] * COLS + row_block // GRP

    owned = col_index * 16 + row_index
    lead_codes = jnp.where(run8 == 0, groups, -1)
    strip_place, strip_has = lookup(lead_codes, child_map, COLS)
    lead_hit = (lead_codes[:, None, :] == jnp.arange(COLS, dtype=jnp.int32)[None, :, None]).astype(F32)
    owned_hit = (child_map == owned).astype(F32)
    strip_keep = jnp.einsum("hga,hab->hgb", lead_hit, present)
    strip_keep = jnp.sum(strip_keep * owned_hit[:, None, :], axis=-1)
    strip_keep = (strip_keep > 0.5).astype(jnp.int32).reshape(ROWS)
    strip_place = jnp.where(strip_has, strip_place, 0).reshape(ROWS)

    axes = ("row", "col")
    number = lambda r, c: r * COLS + c

    total = lambda values: functools.reduce(lambda x, y: x + y, values)

    total = lambda values: functools.reduce(lambda x, y: x + y, values)

    pieces = cut_strip(parent_front)
    own = total([jnp.where(col_index == 0, pieces[0], 0.0)] + [
        lax.ppermute(pieces[i], axes, [(number(r, 0), number(r, i)) for r in range(ROWS)])
        for i in range(1, NLEAD)
    ])
    pairs = [(number(j % 16, j // 16), number(j // 8, j % 8)) for j in range(128)]
    strip_parent = lax.ppermute(own, axes, [(b, a) for a, b in pairs])

    early = pack_early(jnp.concatenate([send_cols, send_rows[:1]]), children)
    early = lax.all_to_all(early, "col", split_axis=0, concat_axis=0, tiled=True)
    early = pick_early(pick_owner, early, [])
    early = lax.all_to_all(early, "row", split_axis=0, concat_axis=0, tiled=True)
    strip = assemble_strip(strip_place, strip_keep, strip_parent, early, [])

    first = pack_first(send_cols[0::2], children, [])
    first = lax.all_to_all(first, "col", split_axis=0, concat_axis=0, tiled=True)

    half = BLOCK // 2
    piece = total([
        lax.ppermute(
            strip[part * half : (part + 1) * half],
            axes,
            [(number(j, 0), number(2 * j + part, 0)) for j in range(NLEAD)],
        )
        for part in range(2)
    ])
    halves = [piece[: half // 2], piece[half // 2 :]]
    piece = total([jnp.where(col_index == 0, halves[0], 0.0)] + [
        lax.ppermute(halves[d % 2], axes, [(number(r, 0), number(r, d)) for r in range(ROWS)])
        for d in range(1, COLS)
    ])
    lead = lax.all_gather(piece, "row", axis=0, tiled=True)
    other = lax.ppermute(lead, "col", [(c, c ^ 1) for c in range(COLS)])
    parity = (col_index % 2).astype(jnp.int32).reshape(1)

    row_piece = lax.ppermute(strip, axes, pairs)
    col_strip = lax.all_gather(strip, "row", axis=0, tiled=True)
    row_strip = lax.all_gather(row_piece, "col", axis=0, tiled=True)

    sends = sends.astype(jnp.int32)
    near_out = pack_rows(send_rows, sends, pick_cols[:HALF], first, [], [])
    near = lax.all_to_all(near_out, "row", split_axis=0, concat_axis=0, tiled=True)
    shifts = (col_index + jnp.arange(COLS, dtype=jnp.int32)) % COLS
    parts = pack_second(jnp.take(send_cols, shifts * 2 + 1), children, [near_out])
    second = [parts[0]] + [
        lax.ppermute(parts[d], "col", [(c, (c + d) % COLS) for c in range(COLS)])
        for d in range(1, COLS)
    ]
    work = factor_part(0, [parity, lead, other], near_out)
    far_out = pack_rows(send_rows, sends, pick_cols[HALF:], first, second, [near, work])
    far = lax.all_to_all(far_out, "row", split_axis=0, concat_axis=0, tiled=True)
    work = factor_part(1, [work], far_out)
    work = factor_part(2, [work], far_out)
    inv_hi, inv_lo = factor_part(3, [work], far_out)
    flags = jnp.stack([row_index, col_index]).astype(jnp.int32)
    front = update_front(flags, row_strip, col_strip, inv_hi, inv_lo, parent_front)
    return place_children(source, col_rank, keep, front, near, far)


def solution(mesh):
    in_specs = (P("row", "col"), P("row", "col"), P(), P())
    out_specs = P("row", "col")
    return jax.shard_map(body, mesh=mesh, in_specs=in_specs, out_specs=out_specs, check_vma=False)
```

```python
import functools

import jax
import jax.numpy as jnp
from jax import lax
from jax.experimental import pallas as pl
from jax.experimental.pallas import tpu as pltpu
from jax.sharding import PartitionSpec as P

BLOCK = 128
LEAD = 1024
NLEAD = LEAD // BLOCK
GRP = 10
ROWS = 16
COLS = 8
VMEM = 56 * 1024 * 1024
F32 = jnp.float32
BF16 = jnp.bfloat16


def params(**kw):
    return pltpu.CompilerParams(vmem_limit_bytes=VMEM, **kw)


def cost(flops, bytes_accessed):
    return pl.CostEstimate(flops=flops, bytes_accessed=bytes_accessed, transcendentals=0)


def gather_call(kernel, tables, arrays, shapes, scratch, sems, name, after=()):
    moved = sum(4 * functools.reduce(lambda x, y: x * y, shape) for shape in shapes)
    count = len(tables) + len(arrays)

    def run(*refs):
        kernel(*refs[:count], *refs[count + len(after) :])

    return pl.pallas_call(
        run,
        in_specs=[pl.BlockSpec(memory_space=pltpu.SMEM)] * len(tables)
        + [pl.BlockSpec(memory_space=pl.ANY)] * (len(arrays) + len(after)),
        out_specs=[pl.BlockSpec(memory_space=pl.ANY)] * len(shapes),
        out_shape=[jax.ShapeDtypeStruct(shape, F32) for shape in shapes],
        scratch_shapes=[pltpu.VMEM(shape, F32) for shape in scratch]
        + [pltpu.SemaphoreType.DMA(sems), pltpu.SemaphoreType.DMA(sems)],
        compiler_params=params(),
        cost_estimate=cost(0, 2 * moved),
        name=name,
    )(*tables, *arrays, *after)


def lanes_of(block):
    return pl.ds(pl.multiple_of(block * BLOCK, BLOCK), BLOCK)


def relay(moves, sem_in, sem_out):
    first = [pltpu.make_async_copy(s, v, sem_in.at[n]) for n, (s, v, t) in enumerate(moves)]
    second = [pltpu.make_async_copy(v, t, sem_out.at[n]) for n, (s, v, t) in enumerate(moves)]
    for copy in first:
        copy.start()
    for one, other in zip(first, second):
        one.wait()
        other.start()
    for copy in second:
        copy.wait()


def pack_early_kernel(table, children, out, held, sem_in, sem_out):
    moves = []
    for s in range(2 * COLS):
        source = children.at[lanes_of(table[2 * COLS]), lanes_of(table[s])]
        moves.append((source, held.at[s], out.at[s]))
    relay(moves, sem_in, sem_out)


def pack_early(table, children):
    shape = (2 * COLS, BLOCK, BLOCK)
    return gather_call(
        pack_early_kernel, [table], [children], [shape], [shape], (2 * COLS,), "pack_early"
    )[0]


def pack_first_kernel(table, children, out, held, sem_in, sem_out):
    moves = [
        (children.at[:, lanes_of(table[s])], held.at[s], out.at[s]) for s in range(COLS)
    ]
    relay(moves, sem_in, sem_out)


def pack_first(table, children, after):
    shape = (COLS, children.shape[0], BLOCK)
    return gather_call(
        pack_first_kernel, [table], [children], [shape], [shape], (COLS,), "pack_first", after
    )[0]


def pack_second_kernel(table, children, *refs):
    wide, sem_in, sem_out = refs[COLS:]
    moves = [
        (children.at[:, lanes_of(table[s])], wide.at[s], refs[s]) for s in range(COLS)
    ]
    relay(moves, sem_in, sem_out)


def pack_second(table, children, after):
    wide = (children.shape[0], BLOCK)
    return gather_call(
        pack_second_kernel,
        [table],
        [children],
        [wide] * COLS,
        [(COLS,) + wide],
        (COLS,),
        "pack_second",
        after,
    )


def cut_kernel(parent, *refs):
    held, sem_in, sem_out = refs[NLEAD:]
    moves = []
    for i in range(NLEAD):
        source = parent.at[pl.ds(i * BLOCK, BLOCK), pl.ds(0, LEAD)]
        moves.append((source, held.at[i], refs[i]))
    relay(moves, sem_in, sem_out)


def cut_strip(parent):
    shape = (BLOCK, LEAD)
    return gather_call(
        cut_kernel, [], [parent], [shape] * NLEAD, [(NLEAD,) + shape], (NLEAD,), "cut_strip"
    )


def pick_early_kernel(table, blocks, out, held, sem_in, sem_out):
    relay([(blocks.at[table[s]], held.at[s], out.at[s]) for s in range(ROWS)], sem_in, sem_out)


def pick_early(table, blocks, after):
    shape = (ROWS, BLOCK, BLOCK)
    return gather_call(
        pick_early_kernel, [table], [blocks], [shape], [shape], (ROWS,), "pick_early", after
    )[0]


HALF = GRP // 2


def pack_rows_kernel(row_table, row_has, origin, first, *refs):
    second, (out, held, sem_in, sem_out) = refs[:-4], refs[-4:]

    def each(act):
        def one(r, carry):
            @pl.when(row_has[r] != 0)
            def _():
                act(r)

            return carry

        lax.fori_loop(0, ROWS, one, 0)

    def start(r):
        for k in range(HALF):
            target = (held.at[r, k], sem_in.at[r, k])

            @pl.when(origin[k] < COLS)
            def _():
                pltpu.make_async_copy(first.at[origin[k], row_table[r]], *target).start()

            for n, source in enumerate(second):

                @pl.when(origin[k] == COLS + n)
                def _():
                    pltpu.make_async_copy(source.at[row_table[r]], *target).start()

    def leave(r):
        return pltpu.make_async_copy(held.at[r], out.at[r], sem_out.at[r, 0])

    def send(r):
        for k in range(HALF):
            pltpu.make_async_copy(first.at[0, 0], held.at[r, k], sem_in.at[r, k]).wait()
        leave(r).start()

    each(start)
    each(send)
    each(lambda r: leave(r).wait())


def pack_rows(row_table, row_has, origin, first, second, after):
    first = first.reshape(COLS, GRP, BLOCK, BLOCK)
    second = [x.reshape(GRP, BLOCK, BLOCK) for x in second]
    shape = (ROWS, HALF, BLOCK, BLOCK)
    return gather_call(
        pack_rows_kernel,
        [row_table, row_has, origin],
        [first] + second,
        [shape],
        [shape],
        (ROWS, HALF),
        "pack_rows",
        after,
    )[0]


def strip_kernel(place, keep, parent, blocks, *refs):
    out = refs[-1]
    out[...] = parent[...]
    for s in range(ROWS):

        @pl.when(keep[s] != 0)
        def _():
            at = lanes_of(place[s])
            out[:, at] = out[:, at] + blocks[s].T


def assemble_strip(place, keep, parent, blocks, after):
    vmem = pl.BlockSpec(memory_space=pltpu.VMEM)
    smem = pl.BlockSpec(memory_space=pltpu.SMEM)
    return pl.pallas_call(
        strip_kernel,
        in_specs=[smem, smem, vmem, vmem] + [pl.BlockSpec(memory_space=pl.ANY)] * len(after),
        out_specs=vmem,
        out_shape=jax.ShapeDtypeStruct((BLOCK, LEAD), F32),
        compiler_params=params(),
        cost_estimate=cost(0, 2 << 20),
        name="assemble_strip",
    )(place, keep, parent, blocks, *after)


def hand_on_kernel(given, *refs):
    refs[-1][...] = given[...]


def hand_on(given, after):
    vmem = pl.BlockSpec(memory_space=pltpu.VMEM)
    return pl.pallas_call(
        hand_on_kernel,
        in_specs=[vmem] + [pl.BlockSpec(memory_space=pl.ANY)] * len(after),
        out_specs=vmem,
        out_shape=jax.ShapeDtypeStruct(given.shape, F32),
        compiler_params=params(),
        cost_estimate=cost(0, 1 << 20),
        name="hand_on",
    )(given, *after)


def split(x):
    hi = x.astype(BF16)
    return hi, (x - hi.astype(F32)).astype(BF16)


def dot3(a_hi, a_lo, b_hi, b_lo):
    dims = (((1,), (1,)), ((), ()))
    total = lax.dot_general(a_hi, b_lo, dims, preferred_element_type=F32)
    total += lax.dot_general(a_lo, b_hi, dims, preferred_element_type=F32)
    return total + lax.dot_general(a_hi, b_hi, dims, preferred_element_type=F32)


def dot_full(a, b, dims):
    return lax.dot_general(
        a, b, (dims, ((), ())), precision=lax.Precision.HIGHEST, preferred_element_type=F32
    )


def invert_diagonal(work):
    lanes = lax.broadcasted_iota(jnp.int32, (BLOCK, BLOCK), 1)
    rows = lax.broadcasted_iota(jnp.int32, (BLOCK, BLOCK), 0)
    lane8 = lax.broadcasted_iota(jnp.int32, (8, BLOCK), 1)
    row8 = lax.broadcasted_iota(jnp.int32, (8, BLOCK), 0)
    done = []
    for t in range(BLOCK // 8):
        base = 8 * t
        part = work[0:8]
        cols = [jnp.broadcast_to(part[:, base + i : base + i + 1], (8, BLOCK)) for i in range(8)]
        pivots = jnp.zeros((8, BLOCK), F32)
        for i in range(8):
            pivot = jnp.broadcast_to(cols[i][i : i + 1], (8, BLOCK))
            pivots = jnp.where(row8 == i, pivot, pivots)
            factor = jnp.where(row8 > i, cols[i] / pivot, 0.0)
            for other in range(i + 1, 8):
                cols[other] = cols[other] - factor * jnp.broadcast_to(cols[other][i : i + 1], (8, BLOCK))
            row = jnp.broadcast_to(part[i : i + 1], (8, BLOCK))
            row = jnp.where(lane8 == base + i, 1.0, row)
            part = jnp.where((lane8 == base + i) & (row8 > i), 0.0, part)
            part = jnp.where((lane8 == base + i) & (row8 == i), 1.0, part)
            part = part - factor * row
        part = part * lax.rsqrt(pivots)
        done.append(part)
        if t < BLOCK // 8 - 1:
            above = (lane8 > base + row8) & (lane8 < base + 8)
            update = dot_full(part[:, base + 8 :], jnp.where(above, 0.0, part), ((0,), (0,)))
            work = work[8:]
            inside = (lanes[: work.shape[0]] >= base) & (lanes[: work.shape[0]] < base + 8)
            work = jnp.where(inside, 0.0, work) - update
    whole = jnp.concatenate(done, axis=0)
    return jnp.where(rows >= lanes, whole, 0.0)


def factor_kernel(first, count, last, *refs):
    if first == 0:
        parity, mine, other, _, work = refs
        rows = LEAD // 2 // ROWS

        def join(r, carry):
            source = pl.ds(pl.multiple_of(r * rows, rows), rows)
            low = pl.ds(pl.multiple_of(2 * r * rows, rows), rows)
            high = pl.ds(pl.multiple_of((2 * r + 1) * rows, rows), rows)
            even = parity[0] == 0
            work[low, :] = jnp.where(even, mine[source, :], other[source, :])
            work[high, :] = jnp.where(even, other[source, :], mine[source, :])
            return carry

        lax.fori_loop(0, ROWS, join, 0)
    else:
        given, _, *refs = refs
        work = refs[-1] if last else refs[0]
        work[...] = given[...]
    total = LEAD // BLOCK

    def step(k, carry):
        here = lanes_of(k)
        inverse = invert_diagonal(work[here, here])
        work[here, :] = dot_full(inverse, work[here, :], ((1,), (0,)))
        work[here, here] = inverse

        def below(i, carry):
            there = lanes_of(i)
            lower = work[here, there]
            work[there, here] = jnp.zeros((BLOCK, BLOCK), F32)
            work[there, :] = work[there, :] - dot_full(lower, work[here, :], ((0,), (0,)))
            return carry

        return lax.fori_loop(k + 1, total, below, carry)

    lax.fori_loop(first, first + count, step, 0)
    if not last:
        return
    inv_hi, inv_lo = refs[0], refs[1]

    def finish(k, carry):
        here = lanes_of(k)
        rows = lax.broadcasted_iota(jnp.int32, (BLOCK, LEAD), 0) + k * BLOCK
        lanes = lax.broadcasted_iota(jnp.int32, (BLOCK, LEAD), 1)
        hi, lo = split(jnp.where(rows >= lanes, work[here, :], 0.0))
        inv_hi[here, :] = hi
        inv_lo[here, :] = lo
        return carry

    lax.fori_loop(0, total, finish, 0)


PARTS = 4


def factor_part(part, given, after):
    count = LEAD // BLOCK // PARTS
    whole = pl.BlockSpec(memory_space=pltpu.VMEM)
    last = part == PARTS - 1
    half = jax.ShapeDtypeStruct((LEAD, LEAD), BF16)
    full = jax.ShapeDtypeStruct((LEAD, LEAD), F32)
    return pl.pallas_call(
        functools.partial(factor_kernel, part * count, count, last),
        in_specs=([pl.BlockSpec(memory_space=pltpu.SMEM), whole] if part == 0 else [])
        + [whole, pl.BlockSpec(memory_space=pl.ANY)],
        out_specs=[whole] * 2 if last else whole,
        out_shape=(half, half) if last else full,
        scratch_shapes=[pltpu.VMEM((LEAD, LEAD), F32)] if last else [],
        compiler_params=params(),
        cost_estimate=cost(25 * 10**9, 8 << 20),
        name="factor_lead",
    )(*given, after)


TILE = 256


def solve_rows(rows, inv_hi, inv_lo):
    hi, lo = split(rows)
    parts = []
    for n in range(LEAD // TILE):
        at, upto = pl.ds(n * TILE, TILE), (n + 1) * TILE
        parts.append(
            dot3(hi[:, :upto], lo[:, :upto], inv_hi[at, pl.ds(0, upto)], inv_lo[at, pl.ds(0, upto)])
        )
    return jnp.concatenate(parts, axis=1)


def update_kernel(flags, row_strip, col_strip, inv_hi, inv_lo, parent, out, panel, hi, lo):
    step = pl.program_id(0)

    @pl.when(step == 0)
    def _():
        def chunk(n, carry):
            at = pl.ds(pl.multiple_of(n * TILE, TILE), TILE)
            values = solve_rows(row_strip[at, :], inv_hi, inv_lo)
            panel[at, :] = values
            hi[at, :], lo[at, :] = split(values)
            return carry

        lax.fori_loop(0, LEAD // TILE, chunk, 0)

    in_panel = (flags[1] == 0) & (step < LEAD // TILE)
    top = flags[0] == 0

    @pl.when(in_panel)
    def _():
        at = pl.ds(pl.multiple_of(step * TILE, TILE), TILE)
        rows = lax.broadcasted_iota(jnp.int32, (LEAD, TILE), 0)
        lanes = lax.broadcasted_iota(jnp.int32, (LEAD, TILE), 1) + step * TILE
        out[...] = jnp.where((rows >= lanes) | jnp.logical_not(top), panel[:, at], 0.0)

    @pl.when(jnp.logical_not(in_panel) & top)
    def _():
        out[...] = jnp.zeros_like(out)

    @pl.when(jnp.logical_not(in_panel) & jnp.logical_not(top))
    def _():
        right = split(solve_rows(col_strip[...], inv_hi, inv_lo))

        def chunk(n, carry):
            at = pl.ds(pl.multiple_of(n * TILE, TILE), TILE)
            out[at, :] = parent[at, :] - dot3(hi[at, :], lo[at, :], *right)
            return carry

        lax.fori_loop(0, LEAD // TILE, chunk, 0)


def update_front(flags, row_strip, col_strip, inv_hi, inv_lo, parent):
    rows, columns = parent.shape
    whole = lambda t, f: (0, 0)
    return pl.pallas_call(
        update_kernel,
        grid_spec=pltpu.PrefetchScalarGridSpec(
            num_scalar_prefetch=1,
            grid=(columns // TILE,),
            in_specs=[
                pl.BlockSpec((LEAD, LEAD), whole),
                pl.BlockSpec((TILE, LEAD), lambda t, f: (t, 0)),
                pl.BlockSpec((LEAD, LEAD), whole),
                pl.BlockSpec((LEAD, LEAD), whole),
                pl.BlockSpec((rows, TILE), lambda t, f: (0, t)),
            ],
            out_specs=pl.BlockSpec((rows, TILE), lambda t, f: (0, t)),
            scratch_shapes=[
                pltpu.VMEM((LEAD, LEAD), F32),
                pltpu.VMEM((LEAD, LEAD), BF16),
                pltpu.VMEM((LEAD, LEAD), BF16),
            ],
        ),
        out_shape=jax.ShapeDtypeStruct((rows, columns), F32),
        compiler_params=params(),
        cost_estimate=cost(40 * 10**9, 32 << 20),
        name="update_front",
    )(flags, row_strip, col_strip, inv_hi, inv_lo, parent)


def place_kernel(source, rank, keep, front, *refs):
    out = refs[-1]
    i = pl.program_id(0)
    for j in range(16):
        at = pl.ds(j * BLOCK, BLOCK)
        value = front[:, at]
        for h in range(2):
            k = rank[h, j]
            near, far = refs[2 * h], refs[2 * h + 1]
            block = jnp.where(
                k < HALF, near[0, jnp.minimum(k, HALF - 1)], far[0, jnp.maximum(k - HALF, 0)]
            )
            value = value + jnp.where(keep[h, i * 16 + j] != 0, block, 0.0)
        out[:, at] = value


def place_children(source, rank, keep, front, near, far):
    rows, columns = front.shape

    def spec(h):
        return pl.BlockSpec((1, HALF, BLOCK, BLOCK), lambda i, s, r, k: (s[h, i], 0, 0, 0))

    return pl.pallas_call(
        place_kernel,
        grid_spec=pltpu.PrefetchScalarGridSpec(
            num_scalar_prefetch=3,
            grid=(rows // BLOCK,),
            in_specs=[pl.BlockSpec((BLOCK, columns), lambda i, s, r, k: (i, 0))]
            + [spec(0), spec(0), spec(1), spec(1)],
            out_specs=pl.BlockSpec((BLOCK, columns), lambda i, s, r, k: (i, 0)),
        ),
        out_shape=jax.ShapeDtypeStruct((rows, columns), F32),
        input_output_aliases={3: 0},
        compiler_params=params(),
        cost_estimate=cost(0, 24 << 20),
        name="place_children",
    )(source, rank, keep, front, near, far, near, far)


def earlier_count(keys):
    places = jnp.arange(keys.shape[-1], dtype=jnp.int32)
    matches = keys[..., :, None] == keys[..., None, :]
    before = places[None, :] < places[:, None]
    return jnp.sum((matches & before).astype(jnp.int32), axis=-1)


def lookup(codes, values, length):
    hits = codes[..., :, None] == jnp.arange(length, dtype=jnp.int32)
    found = jnp.sum(jnp.where(hits, values[..., :, None], 0), axis=-2)
    return found, jnp.any(hits, axis=-2)


def body(parent_front, children, child_map, fill):
    row_index = lax.axis_index("row")
    col_index = lax.axis_index("col")
    child_id = row_index // COLS
    group_row = row_index % COLS
    blocks = child_map.shape[1]
    places = jnp.arange(blocks, dtype=jnp.int32)
    groups = places // GRP
    within = places % GRP
    run16 = child_map // 16
    run8 = child_map // 8
    slot = earlier_count(groups * COLS + run16)
    pick = lambda x: lax.dynamic_index_in_dim(x, child_id, 0, keepdims=False)
    own_map, own_run16, own_run8, own_slot = pick(child_map), pick(run16), pick(run8), pick(slot)

    col_codes = jnp.where(groups == col_index, own_run16 * 2 + own_slot, -1)
    send_cols, _ = lookup(col_codes, within, 2 * COLS)
    row_codes = jnp.where(groups == group_row, own_run8, -1)
    send_rows, sends = lookup(row_codes, within, ROWS)
    ahead = slot[:, None, :] * blocks + places < (slot * blocks + places)[:, :, None]
    rank_all = jnp.sum((ahead & (run16[:, None, :] == run16[:, :, None])).astype(jnp.int32), axis=-1)
    rank_codes = jnp.where(own_run16 == col_index, pick(rank_all), -1)
    origin = jnp.where(own_slot == 0, groups, COLS + (col_index - groups) % COLS)
    pick_cols, _ = lookup(rank_codes, origin, GRP)
    own_codes = jnp.where(own_run16 == col_index, own_map % 16, -1)
    pick_owner, _ = lookup(own_codes, groups * 2 + own_slot, 16)

    tile_rows = jnp.where(run8 == row_index, child_map % 8, -1)
    row_block, row_has = lookup(tile_rows, jnp.broadcast_to(places, (2, blocks)), 8)
    tile_cols = jnp.where(run16 == col_index, child_map % 16, -1)
    col_rank, col_has = lookup(tile_cols, rank_all, 16)
    row_hit = (tile_rows[:, None, :] == jnp.arange(8, dtype=jnp.int32)[None, :, None]).astype(F32)
    col_hit = (tile_cols[:, None, :] == jnp.arange(16, dtype=jnp.int32)[None, :, None]).astype(F32)
    present = fill.astype(F32)
    keep = jnp.einsum("hia,hab->hib", row_hit, present)
    keep = jnp.einsum("hib,hjb->hij", keep, col_hit)
    panel_col = (col_index == 0) & (jnp.arange(16) < NLEAD)
    keep = jnp.where(panel_col | (row_index == 0), 0.0, keep)
    keep = (keep > 0.5).astype(jnp.int32).reshape(2, 8 * 16)
    source = jnp.arange(2, dtype=jnp.int32)[:, None] * COLS + row_block // GRP

    owned = col_index * 16 + row_index
    lead_codes = jnp.where(run8 == 0, groups, -1)
    strip_place, strip_has = lookup(lead_codes, child_map, COLS)
    lead_hit = (lead_codes[:, None, :] == jnp.arange(COLS, dtype=jnp.int32)[None, :, None]).astype(F32)
    owned_hit = (child_map == owned).astype(F32)
    strip_keep = jnp.einsum("hga,hab->hgb", lead_hit, present)
    strip_keep = jnp.sum(strip_keep * owned_hit[:, None, :], axis=-1)
    strip_keep = (strip_keep > 0.5).astype(jnp.int32).reshape(ROWS)
    strip_place = jnp.where(strip_has, strip_place, 0).reshape(ROWS)

    axes = ("row", "col")
    number = lambda r, c: r * COLS + c

    total = lambda values: functools.reduce(lambda x, y: x + y, values)

    total = lambda values: functools.reduce(lambda x, y: x + y, values)

    pieces = cut_strip(parent_front)
    own = total([jnp.where(col_index == 0, pieces[0], 0.0)] + [
        lax.ppermute(pieces[i], axes, [(number(r, 0), number(r, i)) for r in range(ROWS)])
        for i in range(1, NLEAD)
    ])
    pairs = [(number(j % 16, j // 16), number(j // 8, j % 8)) for j in range(128)]
    strip_parent = lax.ppermute(own, axes, [(b, a) for a, b in pairs])

    early = pack_early(jnp.concatenate([send_cols, send_rows[:1]]), children)
    early = lax.all_to_all(early, "col", split_axis=0, concat_axis=0, tiled=True)
    early = pick_early(pick_owner, early, [])
    early = lax.all_to_all(early, "row", split_axis=0, concat_axis=0, tiled=True)
    strip = assemble_strip(strip_place, strip_keep, strip_parent, early, [])

    first = pack_first(send_cols[0::2], children, [])
    first = lax.all_to_all(first, "col", split_axis=0, concat_axis=0, tiled=True)

    half = BLOCK // 2
    piece = total([
        lax.ppermute(
            strip[part * half : (part + 1) * half],
            axes,
            [(number(j, 0), number(2 * j + part, 0)) for j in range(NLEAD)],
        )
        for part in range(2)
    ])
    halves = [piece[: half // 2], piece[half // 2 :]]
    piece = total([jnp.where(col_index == 0, halves[0], 0.0)] + [
        lax.ppermute(halves[d % 2], axes, [(number(r, 0), number(r, d)) for r in range(ROWS)])
        for d in range(1, COLS)
    ])
    lead = lax.all_gather(piece, "row", axis=0, tiled=True)
    other = lax.ppermute(lead, "col", [(c, c ^ 1) for c in range(COLS)])
    parity = (col_index % 2).astype(jnp.int32).reshape(1)

    col_strip = lax.all_gather(strip, "row", axis=0, tiled=True)

    sends = sends.astype(jnp.int32)
    work = factor_part(0, [parity, lead, other], strip)
    near_out = pack_rows(send_rows, sends, pick_cols[:HALF], first, [], [])
    near = lax.all_to_all(near_out, "row", split_axis=0, concat_axis=0, tiled=True)
    shifts = (col_index + jnp.arange(COLS, dtype=jnp.int32)) % COLS
    parts = pack_second(jnp.take(send_cols, shifts * 2 + 1), children, [near_out])
    second = [parts[0]] + [
        lax.ppermute(parts[d], "col", [(c, (c + d) % COLS) for c in range(COLS)])
        for d in range(1, COLS)
    ]
    work = factor_part(1, [work], near_out)
    far_out = pack_rows(send_rows, sends, pick_cols[HALF:], first, second, [near, work])
    far = lax.all_to_all(far_out, "row", split_axis=0, concat_axis=0, tiled=True)
    work = factor_part(2, [work], far_out)
    inv_hi, inv_lo = factor_part(3, [work], far_out)
    row_piece = hand_on(lax.ppermute(strip, axes, pairs), [near_out])
    row_strip = lax.all_gather(row_piece, "col", axis=0, tiled=True)
    flags = jnp.stack([row_index, col_index]).astype(jnp.int32)
    front = update_front(flags, row_strip, col_strip, inv_hi, inv_lo, parent_front)
    return place_children(source, col_rank, keep, front, near, far)


def solution(mesh):
    in_specs = (P("row", "col"), P("row", "col"), P(), P())
    out_specs = P("row", "col")
    return jax.shard_map(body, mesh=mesh, in_specs=in_specs, out_specs=out_specs, check_vma=False)
```

```python
import functools

import jax
import jax.numpy as jnp
from jax import lax
from jax.experimental import pallas as pl
from jax.experimental.pallas import tpu as pltpu
from jax.sharding import PartitionSpec as P

BLOCK = 128
LEAD = 1024
NLEAD = LEAD // BLOCK
GRP = 10
ROWS = 16
COLS = 8
VMEM = 56 * 1024 * 1024
F32 = jnp.float32
BF16 = jnp.bfloat16


def params(**kw):
    return pltpu.CompilerParams(vmem_limit_bytes=VMEM, **kw)


def cost(flops, bytes_accessed):
    return pl.CostEstimate(flops=flops, bytes_accessed=bytes_accessed, transcendentals=0)


def gather_call(kernel, tables, arrays, shapes, scratch, sems, name, after=()):
    moved = sum(4 * functools.reduce(lambda x, y: x * y, shape) for shape in shapes)
    count = len(tables) + len(arrays)

    def run(*refs):
        kernel(*refs[:count], *refs[count + len(after) :])

    return pl.pallas_call(
        run,
        in_specs=[pl.BlockSpec(memory_space=pltpu.SMEM)] * len(tables)
        + [pl.BlockSpec(memory_space=pl.ANY)] * (len(arrays) + len(after)),
        out_specs=[pl.BlockSpec(memory_space=pl.ANY)] * len(shapes),
        out_shape=[jax.ShapeDtypeStruct(shape, F32) for shape in shapes],
        scratch_shapes=[pltpu.VMEM(shape, F32) for shape in scratch]
        + [pltpu.SemaphoreType.DMA(sems), pltpu.SemaphoreType.DMA(sems)],
        compiler_params=params(),
        cost_estimate=cost(0, 2 * moved),
        name=name,
    )(*tables, *arrays, *after)


def lanes_of(block):
    return pl.ds(pl.multiple_of(block * BLOCK, BLOCK), BLOCK)


def relay(moves, sem_in, sem_out):
    first = [pltpu.make_async_copy(s, v, sem_in.at[n]) for n, (s, v, t) in enumerate(moves)]
    second = [pltpu.make_async_copy(v, t, sem_out.at[n]) for n, (s, v, t) in enumerate(moves)]
    for copy in first:
        copy.start()
    for one, other in zip(first, second):
        one.wait()
        other.start()
    for copy in second:
        copy.wait()


def pack_early_kernel(table, children, out, held, sem_in, sem_out):
    moves = []
    for s in range(2 * COLS):
        source = children.at[lanes_of(table[2 * COLS]), lanes_of(table[s])]
        moves.append((source, held.at[s], out.at[s]))
    relay(moves, sem_in, sem_out)


def pack_early(table, children):
    shape = (2 * COLS, BLOCK, BLOCK)
    return gather_call(
        pack_early_kernel, [table], [children], [shape], [shape], (2 * COLS,), "pack_early"
    )[0]


def pack_first_kernel(table, children, out, held, sem_in, sem_out):
    moves = [
        (children.at[:, lanes_of(table[s])], held.at[s], out.at[s]) for s in range(COLS)
    ]
    relay(moves, sem_in, sem_out)


def pack_first(table, children, after):
    shape = (COLS, children.shape[0], BLOCK)
    return gather_call(
        pack_first_kernel, [table], [children], [shape], [shape], (COLS,), "pack_first", after
    )[0]


def pack_second_kernel(table, children, *refs):
    wide, sem_in, sem_out = refs[COLS:]
    moves = [
        (children.at[:, lanes_of(table[s])], wide.at[s], refs[s]) for s in range(COLS)
    ]
    relay(moves, sem_in, sem_out)


def pack_second(table, children, after):
    wide = (children.shape[0], BLOCK)
    return gather_call(
        pack_second_kernel,
        [table],
        [children],
        [wide] * COLS,
        [(COLS,) + wide],
        (COLS,),
        "pack_second",
        after,
    )


def cut_kernel(parent, *refs):
    held, sem_in, sem_out = refs[NLEAD:]
    moves = []
    for i in range(NLEAD):
        source = parent.at[pl.ds(i * BLOCK, BLOCK), pl.ds(0, LEAD)]
        moves.append((source, held.at[i], refs[i]))
    relay(moves, sem_in, sem_out)


def cut_strip(parent):
    shape = (BLOCK, LEAD)
    return gather_call(
        cut_kernel, [], [parent], [shape] * NLEAD, [(NLEAD,) + shape], (NLEAD,), "cut_strip"
    )


def pick_early_kernel(table, blocks, out, held, sem_in, sem_out):
    relay([(blocks.at[table[s]], held.at[s], out.at[s]) for s in range(ROWS)], sem_in, sem_out)


def pick_early(table, blocks, after):
    shape = (ROWS, BLOCK, BLOCK)
    return gather_call(
        pick_early_kernel, [table], [blocks], [shape], [shape], (ROWS,), "pick_early", after
    )[0]


HALF = GRP // 2


def pack_rows_kernel(row_table, row_has, origin, first, *refs):
    second, (out, held, sem_in, sem_out) = refs[:-4], refs[-4:]

    def each(act):
        def one(r, carry):
            @pl.when(row_has[r] != 0)
            def _():
                act(r)

            return carry

        lax.fori_loop(0, ROWS, one, 0)

    def start(r):
        for k in range(HALF):
            target = (held.at[r, k], sem_in.at[r, k])

            @pl.when(origin[k] < COLS)
            def _():
                pltpu.make_async_copy(first.at[origin[k], row_table[r]], *target).start()

            for n, source in enumerate(second):

                @pl.when(origin[k] == COLS + n)
                def _():
                    pltpu.make_async_copy(source.at[row_table[r]], *target).start()

    def leave(r):
        return pltpu.make_async_copy(held.at[r], out.at[r], sem_out.at[r, 0])

    def send(r):
        for k in range(HALF):
            pltpu.make_async_copy(first.at[0, 0], held.at[r, k], sem_in.at[r, k]).wait()
        leave(r).start()

    each(start)
    each(send)
    each(lambda r: leave(r).wait())


def pack_rows(row_table, row_has, origin, first, second, after):
    first = first.reshape(COLS, GRP, BLOCK, BLOCK)
    second = [x.reshape(GRP, BLOCK, BLOCK) for x in second]
    shape = (ROWS, HALF, BLOCK, BLOCK)
    return gather_call(
        pack_rows_kernel,
        [row_table, row_has, origin],
        [first] + second,
        [shape],
        [shape],
        (ROWS, HALF),
        "pack_rows",
        after,
    )[0]


def strip_kernel(place, keep, parent, blocks, *refs):
    out = refs[-1]
    out[...] = parent[...]
    for s in range(ROWS):

        @pl.when(keep[s] != 0)
        def _():
            at = lanes_of(place[s])
            out[:, at] = out[:, at] + blocks[s].T


def assemble_strip(place, keep, parent, blocks, after):
    vmem = pl.BlockSpec(memory_space=pltpu.VMEM)
    smem = pl.BlockSpec(memory_space=pltpu.SMEM)
    return pl.pallas_call(
        strip_kernel,
        in_specs=[smem, smem, vmem, vmem] + [pl.BlockSpec(memory_space=pl.ANY)] * len(after),
        out_specs=vmem,
        out_shape=jax.ShapeDtypeStruct((BLOCK, LEAD), F32),
        compiler_params=params(),
        cost_estimate=cost(0, 2 << 20),
        name="assemble_strip",
    )(place, keep, parent, blocks, *after)


def hand_on_kernel(given, *refs):
    refs[-1][...] = given[...]


def hand_on(given, after):
    vmem = pl.BlockSpec(memory_space=pltpu.VMEM)
    return pl.pallas_call(
        hand_on_kernel,
        in_specs=[vmem] + [pl.BlockSpec(memory_space=pl.ANY)] * len(after),
        out_specs=vmem,
        out_shape=jax.ShapeDtypeStruct(given.shape, F32),
        compiler_params=params(),
        cost_estimate=cost(0, 1 << 20),
        name="hand_on",
    )(given, *after)


def split(x):
    hi = x.astype(BF16)
    return hi, (x - hi.astype(F32)).astype(BF16)


def dot3(a_hi, a_lo, b_hi, b_lo):
    dims = (((1,), (1,)), ((), ()))
    total = lax.dot_general(a_hi, b_lo, dims, preferred_element_type=F32)
    total += lax.dot_general(a_lo, b_hi, dims, preferred_element_type=F32)
    return total + lax.dot_general(a_hi, b_hi, dims, preferred_element_type=F32)


def dot_full(a, b, dims):
    return lax.dot_general(
        a, b, (dims, ((), ())), precision=lax.Precision.HIGHEST, preferred_element_type=F32
    )


def invert_diagonal(work):
    lanes = lax.broadcasted_iota(jnp.int32, (BLOCK, BLOCK), 1)
    rows = lax.broadcasted_iota(jnp.int32, (BLOCK, BLOCK), 0)
    here, below, rest = work[0:8], work[8:16], work[16:]
    done = []
    for t in range(BLOCK // 8):
        base = 8 * t
        last = t == BLOCK // 8 - 1
        part = here if last else jnp.concatenate([here, below], axis=0)
        shape = part.shape
        lane = lanes[: shape[0]]
        row_id = rows[: shape[0]]
        cols = [jnp.broadcast_to(part[:, base + i : base + i + 1], shape) for i in range(8)]
        scale = jnp.zeros((8, BLOCK), F32)
        for i in range(8):
            root = lax.rsqrt(cols[i][i : i + 1])
            scale = jnp.where(row_id[:8] == i, root, scale)
            factor = jnp.where(row_id > i, cols[i] * (root * root), 0.0)
            for other in range(i + 1, 8):
                cols[other] = cols[other] - factor * cols[other][i : i + 1]
            row = jnp.where(lane[:1] == base + i, 1.0, part[i : i + 1])
            part = jnp.where(lane == base + i, jnp.where(row_id == i, 1.0, jnp.where(row_id > i, 0.0, part)), part)
            part = part - factor * row
        here = part[:8] * scale
        done.append(here)
        if t < BLOCK // 8 - 2:
            above = (lane[:8] > base + row_id[:8]) & (lane[:8] < base + 8)
            update = dot_full(here[:, base + 16 :], jnp.where(above, 0.0, here), ((0,), (0,)))
            inside = (lanes[: rest.shape[0]] >= base) & (lanes[: rest.shape[0]] < base + 8)
            rest = jnp.where(inside, 0.0, rest) - update
        if not last:
            here = part[8:]
            below, rest = rest[:8], rest[8:]
    whole = jnp.concatenate(done, axis=0)
    return jnp.where(rows >= lanes, whole, 0.0)


def factor_kernel(first, count, last, *refs):
    given, _, *refs = refs
    work = refs[-1] if last else refs[0]
    work[...] = given[...]
    total = LEAD // BLOCK

    def step(k, carry):
        here = lanes_of(k)
        inverse = invert_diagonal(work[here, here])
        work[here, :] = dot_full(inverse, work[here, :], ((1,), (0,)))
        work[here, here] = inverse

        def below(i, carry):
            there = lanes_of(i)
            lower = work[here, there]
            work[there, here] = jnp.zeros((BLOCK, BLOCK), F32)
            work[there, :] = work[there, :] - dot_full(lower, work[here, :], ((0,), (0,)))
            return carry

        return lax.fori_loop(k + 1, total, below, carry)

    lax.fori_loop(first, first + count, step, 0)
    if not last:
        return
    inv_hi, inv_lo = refs[0], refs[1]

    def finish(k, carry):
        here = lanes_of(k)
        rows = lax.broadcasted_iota(jnp.int32, (BLOCK, LEAD), 0) + k * BLOCK
        lanes = lax.broadcasted_iota(jnp.int32, (BLOCK, LEAD), 1)
        hi, lo = split(jnp.where(rows >= lanes, work[here, :], 0.0))
        inv_hi[here, :] = hi
        inv_lo[here, :] = lo
        return carry

    lax.fori_loop(0, total, finish, 0)


PARTS = 4


def factor_part(part, given, after):
    count = LEAD // BLOCK // PARTS
    whole = pl.BlockSpec(memory_space=pltpu.VMEM)
    last = part == PARTS - 1
    half = jax.ShapeDtypeStruct((LEAD, LEAD), BF16)
    full = jax.ShapeDtypeStruct((LEAD, LEAD), F32)
    return pl.pallas_call(
        functools.partial(factor_kernel, part * count, count, last),
        in_specs=[whole, pl.BlockSpec(memory_space=pl.ANY)],
        out_specs=[whole] * 2 if last else whole,
        out_shape=(half, half) if last else full,
        scratch_shapes=[pltpu.VMEM((LEAD, LEAD), F32)] if last else [],
        compiler_params=params(),
        cost_estimate=cost(25 * 10**9, 8 << 20),
        name="factor_lead",
    )(given, after)


TILE = 512
CHUNK = 1024


def solve_rows(rows, inv_hi, inv_lo):
    hi, lo = split(rows)
    parts = []
    for n in range(LEAD // 256):
        at, upto = pl.ds(n * 256, 256), (n + 1) * 256
        parts.append(
            dot3(hi[:, :upto], lo[:, :upto], inv_hi[at, pl.ds(0, upto)], inv_lo[at, pl.ds(0, upto)])
        )
    return jnp.concatenate(parts, axis=1)


def update_kernel(flags, row_strip, col_strip, inv_hi, inv_lo, parent, out, panel, hi, lo):
    step = pl.program_id(0)

    @pl.when(step == 0)
    def _():
        def chunk(n, carry):
            at = pl.ds(pl.multiple_of(n * CHUNK, CHUNK), CHUNK)
            values = solve_rows(row_strip[at, :], inv_hi, inv_lo)
            panel[at, :] = values
            hi[at, :], lo[at, :] = split(values)
            return carry

        lax.fori_loop(0, LEAD // CHUNK, chunk, 0)

    in_panel = (flags[1] == 0) & (step < LEAD // TILE)
    top = flags[0] == 0

    @pl.when(in_panel)
    def _():
        at = pl.ds(pl.multiple_of(step * TILE, TILE), TILE)
        rows = lax.broadcasted_iota(jnp.int32, (LEAD, TILE), 0)
        lanes = lax.broadcasted_iota(jnp.int32, (LEAD, TILE), 1) + step * TILE
        out[...] = jnp.where((rows >= lanes) | jnp.logical_not(top), panel[:, at], 0.0)

    @pl.when(jnp.logical_not(in_panel) & top)
    def _():
        out[...] = jnp.zeros_like(out)

    @pl.when(jnp.logical_not(in_panel) & jnp.logical_not(top))
    def _():
        right = split(solve_rows(col_strip[...], inv_hi, inv_lo))

        def chunk(n, carry):
            at = pl.ds(pl.multiple_of(n * CHUNK, CHUNK), CHUNK)
            out[at, :] = parent[at, :] - dot3(hi[at, :], lo[at, :], *right)
            return carry

        lax.fori_loop(0, LEAD // CHUNK, chunk, 0)


def update_front(flags, row_strip, col_strip, inv_hi, inv_lo, parent):
    rows, columns = parent.shape
    whole = lambda t, f: (0, 0)
    return pl.pallas_call(
        update_kernel,
        grid_spec=pltpu.PrefetchScalarGridSpec(
            num_scalar_prefetch=1,
            grid=(columns // TILE,),
            in_specs=[
                pl.BlockSpec((LEAD, LEAD), whole),
                pl.BlockSpec((TILE, LEAD), lambda t, f: (t, 0)),
                pl.BlockSpec((LEAD, LEAD), whole),
                pl.BlockSpec((LEAD, LEAD), whole),
                pl.BlockSpec((rows, TILE), lambda t, f: (0, t)),
            ],
            out_specs=pl.BlockSpec((rows, TILE), lambda t, f: (0, t)),
            scratch_shapes=[
                pltpu.VMEM((LEAD, LEAD), F32),
                pltpu.VMEM((LEAD, LEAD), BF16),
                pltpu.VMEM((LEAD, LEAD), BF16),
            ],
        ),
        out_shape=jax.ShapeDtypeStruct((rows, columns), F32),
        compiler_params=params(),
        cost_estimate=cost(40 * 10**9, 32 << 20),
        name="update_front",
    )(flags, row_strip, col_strip, inv_hi, inv_lo, parent)


def place_kernel(source, rank, keep, front, *refs):
    out = refs[-1]
    i = pl.program_id(0)
    for j in range(16):
        at = pl.ds(j * BLOCK, BLOCK)
        value = front[:, at]
        for h in range(2):
            k = rank[h, j]
            near, far = refs[2 * h], refs[2 * h + 1]
            block = jnp.where(
                k < HALF, near[0, jnp.minimum(k, HALF - 1)], far[0, jnp.maximum(k - HALF, 0)]
            )
            value = value + jnp.where(keep[h, i * 16 + j] != 0, block, 0.0)
        out[:, at] = value


def place_children(source, rank, keep, front, near, far):
    rows, columns = front.shape

    def spec(h):
        return pl.BlockSpec((1, HALF, BLOCK, BLOCK), lambda i, s, r, k: (s[h, i], 0, 0, 0))

    return pl.pallas_call(
        place_kernel,
        grid_spec=pltpu.PrefetchScalarGridSpec(
            num_scalar_prefetch=3,
            grid=(rows // BLOCK,),
            in_specs=[pl.BlockSpec((BLOCK, columns), lambda i, s, r, k: (i, 0))]
            + [spec(0), spec(0), spec(1), spec(1)],
            out_specs=pl.BlockSpec((BLOCK, columns), lambda i, s, r, k: (i, 0)),
        ),
        out_shape=jax.ShapeDtypeStruct((rows, columns), F32),
        input_output_aliases={3: 0},
        compiler_params=params(),
        cost_estimate=cost(0, 24 << 20),
        name="place_children",
    )(source, rank, keep, front, near, far, near, far)


def earlier_count(keys):
    places = jnp.arange(keys.shape[-1], dtype=jnp.int32)
    matches = keys[..., :, None] == keys[..., None, :]
    before = places[None, :] < places[:, None]
    return jnp.sum((matches & before).astype(jnp.int32), axis=-1)


def lookup(codes, values, length):
    hits = codes[..., :, None] == jnp.arange(length, dtype=jnp.int32)
    found = jnp.sum(jnp.where(hits, values[..., :, None], 0), axis=-2)
    return found, jnp.any(hits, axis=-2)


def body(parent_front, children, child_map, fill):
    row_index = lax.axis_index("row")
    col_index = lax.axis_index("col")
    child_id = row_index // COLS
    group_row = row_index % COLS
    blocks = child_map.shape[1]
    places = jnp.arange(blocks, dtype=jnp.int32)
    groups = places // GRP
    within = places % GRP
    run16 = child_map // 16
    run8 = child_map // 8
    slot = earlier_count(groups * COLS + run16)
    pick = lambda x: lax.dynamic_index_in_dim(x, child_id, 0, keepdims=False)
    own_map, own_run16, own_run8, own_slot = pick(child_map), pick(run16), pick(run8), pick(slot)

    col_codes = jnp.where(groups == col_index, own_run16 * 2 + own_slot, -1)
    send_cols, _ = lookup(col_codes, within, 2 * COLS)
    row_codes = jnp.where(groups == group_row, own_run8, -1)
    send_rows, sends = lookup(row_codes, within, ROWS)
    ahead = slot[:, None, :] * blocks + places < (slot * blocks + places)[:, :, None]
    rank_all = jnp.sum((ahead & (run16[:, None, :] == run16[:, :, None])).astype(jnp.int32), axis=-1)
    rank_codes = jnp.where(own_run16 == col_index, pick(rank_all), -1)
    origin = jnp.where(own_slot == 0, groups, COLS + (col_index - groups) % COLS)
    pick_cols, _ = lookup(rank_codes, origin, GRP)
    own_codes = jnp.where(own_run16 == col_index, own_map % 16, -1)
    pick_owner, _ = lookup(own_codes, groups * 2 + own_slot, 16)

    tile_rows = jnp.where(run8 == row_index, child_map % 8, -1)
    row_block, row_has = lookup(tile_rows, jnp.broadcast_to(places, (2, blocks)), 8)
    tile_cols = jnp.where(run16 == col_index, child_map % 16, -1)
    col_rank, col_has = lookup(tile_cols, rank_all, 16)
    row_hit = (tile_rows[:, None, :] == jnp.arange(8, dtype=jnp.int32)[None, :, None]).astype(F32)
    col_hit = (tile_cols[:, None, :] == jnp.arange(16, dtype=jnp.int32)[None, :, None]).astype(F32)
    present = fill.astype(F32)
    keep = jnp.einsum("hia,hab->hib", row_hit, present)
    keep = jnp.einsum("hib,hjb->hij", keep, col_hit)
    panel_col = (col_index == 0) & (jnp.arange(16) < NLEAD)
    keep = jnp.where(panel_col | (row_index == 0), 0.0, keep)
    keep = (keep > 0.5).astype(jnp.int32).reshape(2, 8 * 16)
    source = jnp.arange(2, dtype=jnp.int32)[:, None] * COLS + row_block // GRP

    owned = col_index * 16 + row_index
    lead_codes = jnp.where(run8 == 0, groups, -1)
    strip_place, strip_has = lookup(lead_codes, child_map, COLS)
    lead_hit = (lead_codes[:, None, :] == jnp.arange(COLS, dtype=jnp.int32)[None, :, None]).astype(F32)
    owned_hit = (child_map == owned).astype(F32)
    strip_keep = jnp.einsum("hga,hab->hgb", lead_hit, present)
    strip_keep = jnp.sum(strip_keep * owned_hit[:, None, :], axis=-1)
    strip_keep = (strip_keep > 0.5).astype(jnp.int32).reshape(ROWS)
    strip_place = jnp.where(strip_has, strip_place, 0).reshape(ROWS)

    axes = ("row", "col")
    number = lambda r, c: r * COLS + c

    total = lambda values: functools.reduce(lambda x, y: x + y, values)

    total = lambda values: functools.reduce(lambda x, y: x + y, values)

    pieces = cut_strip(parent_front)
    own = total([jnp.where(col_index == 0, pieces[0], 0.0)] + [
        lax.ppermute(pieces[i], axes, [(number(r, 0), number(r, i)) for r in range(ROWS)])
        for i in range(1, NLEAD)
    ])
    pairs = [(number(j % 16, j // 16), number(j // 8, j % 8)) for j in range(128)]
    strip_parent = lax.ppermute(own, axes, [(b, a) for a, b in pairs])

    early = pack_early(jnp.concatenate([send_cols, send_rows[:1]]), children)
    early = lax.all_to_all(early, "col", split_axis=0, concat_axis=0, tiled=True)
    early = pick_early(pick_owner, early, [])
    early = lax.all_to_all(early, "row", split_axis=0, concat_axis=0, tiled=True)
    strip = assemble_strip(strip_place, strip_keep, strip_parent, early, [])

    first = pack_first(send_cols[0::2], children, [])
    first = lax.all_to_all(first, "col", split_axis=0, concat_axis=0, tiled=True)

    col_strip = lax.all_gather(strip, "row", axis=0, tiled=True)

    half = BLOCK // 2
    piece = total([
        lax.ppermute(
            strip[part * half : (part + 1) * half],
            axes,
            [(number(j, 0), number(2 * j + part, 0)) for j in range(NLEAD)],
        )
        for part in range(2)
    ])
    piece = total([piece] + [
        lax.ppermute(piece, axes, [(number(r, 0), number(r, d)) for r in range(ROWS)])
        for d in range(1, COLS)
    ])
    lead = lax.all_gather(hand_on(piece, [first]), "row", axis=0, tiled=True)


    sends = sends.astype(jnp.int32)
    work = factor_part(0, lead, strip)
    near_out = pack_rows(send_rows, sends, pick_cols[:HALF], first, [], [col_strip])
    near = lax.all_to_all(near_out, "row", split_axis=0, concat_axis=0, tiled=True)
    shifts = (col_index + jnp.arange(COLS, dtype=jnp.int32)) % COLS
    parts = pack_second(jnp.take(send_cols, shifts * 2 + 1), children, [near_out])
    second = [parts[0]] + [
        lax.ppermute(parts[d], "col", [(c, (c + d) % COLS) for c in range(COLS)])
        for d in range(1, COLS)
    ]
    far_out = pack_rows(send_rows, sends, pick_cols[HALF:], first, second, [near, work])
    far = lax.all_to_all(far_out, "row", split_axis=0, concat_axis=0, tiled=True)
    work = factor_part(1, work, far_out)
    work = factor_part(2, work, far_out)
    inv_hi, inv_lo = factor_part(3, work, far_out)
    row_piece = hand_on(lax.ppermute(strip, axes, pairs), [near_out])
    row_strip = lax.all_gather(row_piece, "col", axis=0, tiled=True)
    flags = jnp.stack([row_index, col_index]).astype(jnp.int32)
    front = update_front(flags, row_strip, col_strip, inv_hi, inv_lo, parent_front)
    return place_children(source, col_rank, keep, front, near, far)


def solution(mesh):
    in_specs = (P("row", "col"), P("row", "col"), P(), P())
    out_specs = P("row", "col")
    return jax.shard_map(body, mesh=mesh, in_specs=in_specs, out_specs=out_specs, check_vma=False)
```

```python
import functools

import jax
import jax.numpy as jnp
from jax import lax
from jax.experimental import pallas as pl
from jax.experimental.pallas import tpu as pltpu
from jax.sharding import PartitionSpec as P

BLOCK = 128
LEAD = 1024
NLEAD = LEAD // BLOCK
GRP = 10
ROWS = 16
COLS = 8
VMEM = 56 * 1024 * 1024
F32 = jnp.float32
BF16 = jnp.bfloat16


def params(**kw):
    return pltpu.CompilerParams(vmem_limit_bytes=VMEM, **kw)


def cost(flops, bytes_accessed):
    return pl.CostEstimate(flops=flops, bytes_accessed=bytes_accessed, transcendentals=0)


def gather_call(kernel, tables, arrays, shapes, scratch, sems, name, after=()):
    moved = sum(4 * functools.reduce(lambda x, y: x * y, shape) for shape in shapes)
    count = len(tables) + len(arrays)

    def run(*refs):
        kernel(*refs[:count], *refs[count + len(after) :])

    return pl.pallas_call(
        run,
        in_specs=[pl.BlockSpec(memory_space=pltpu.SMEM)] * len(tables)
        + [pl.BlockSpec(memory_space=pl.ANY)] * (len(arrays) + len(after)),
        out_specs=[pl.BlockSpec(memory_space=pl.ANY)] * len(shapes),
        out_shape=[jax.ShapeDtypeStruct(shape, F32) for shape in shapes],
        scratch_shapes=[pltpu.VMEM(shape, F32) for shape in scratch]
        + [pltpu.SemaphoreType.DMA(sems), pltpu.SemaphoreType.DMA(sems)],
        compiler_params=params(),
        cost_estimate=cost(0, 2 * moved),
        name=name,
    )(*tables, *arrays, *after)


def lanes_of(block):
    return pl.ds(pl.multiple_of(block * BLOCK, BLOCK), BLOCK)


def relay(moves, sem_in, sem_out):
    first = [pltpu.make_async_copy(s, v, sem_in.at[n]) for n, (s, v, t) in enumerate(moves)]
    second = [pltpu.make_async_copy(v, t, sem_out.at[n]) for n, (s, v, t) in enumerate(moves)]
    for copy in first:
        copy.start()
    for one, other in zip(first, second):
        one.wait()
        other.start()
    for copy in second:
        copy.wait()


def pack_early_kernel(table, children, out, held, sem_in, sem_out):
    moves = []
    for s in range(2 * COLS):
        source = children.at[lanes_of(table[2 * COLS]), lanes_of(table[s])]
        moves.append((source, held.at[s], out.at[s]))
    relay(moves, sem_in, sem_out)


def pack_early(table, children):
    shape = (2 * COLS, BLOCK, BLOCK)
    return gather_call(
        pack_early_kernel, [table], [children], [shape], [shape], (2 * COLS,), "pack_early"
    )[0]


def pack_first_kernel(table, children, out, held, sem_in, sem_out):
    moves = [
        (children.at[:, lanes_of(table[s])], held.at[s], out.at[s]) for s in range(COLS)
    ]
    relay(moves, sem_in, sem_out)


def pack_first(table, children, after):
    shape = (COLS, children.shape[0], BLOCK)
    return gather_call(
        pack_first_kernel, [table], [children], [shape], [shape], (COLS,), "pack_first", after
    )[0]


def pack_second_kernel(table, children, *refs):
    wide, sem_in, sem_out = refs[COLS:]
    moves = [
        (children.at[:, lanes_of(table[s])], wide.at[s], refs[s]) for s in range(COLS)
    ]
    relay(moves, sem_in, sem_out)


def pack_second(table, children, after):
    wide = (children.shape[0], BLOCK)
    return gather_call(
        pack_second_kernel,
        [table],
        [children],
        [wide] * COLS,
        [(COLS,) + wide],
        (COLS,),
        "pack_second",
        after,
    )


def cut_kernel(parent, *refs):
    held, sem_in, sem_out = refs[NLEAD:]
    moves = []
    for i in range(NLEAD):
        source = parent.at[pl.ds(i * BLOCK, BLOCK), pl.ds(0, LEAD)]
        moves.append((source, held.at[i], refs[i]))
    relay(moves, sem_in, sem_out)


def cut_strip(parent):
    shape = (BLOCK, LEAD)
    return gather_call(
        cut_kernel, [], [parent], [shape] * NLEAD, [(NLEAD,) + shape], (NLEAD,), "cut_strip"
    )


def pick_early_kernel(table, blocks, out, held, sem_in, sem_out):
    relay([(blocks.at[table[s]], held.at[s], out.at[s]) for s in range(ROWS)], sem_in, sem_out)


def pick_early(table, blocks, after):
    shape = (ROWS, BLOCK, BLOCK)
    return gather_call(
        pick_early_kernel, [table], [blocks], [shape], [shape], (ROWS,), "pick_early", after
    )[0]


HALF = GRP // 2


def pack_rows_kernel(row_table, row_has, origin, first, *refs):
    second, (out, held, sem_in, sem_out) = refs[:-4], refs[-4:]

    def each(act):
        def one(r, carry):
            @pl.when(row_has[r] != 0)
            def _():
                act(r)

            return carry

        lax.fori_loop(0, ROWS, one, 0)

    def start(r):
        for k in range(HALF):
            target = (held.at[r, k], sem_in.at[r, k])

            @pl.when(origin[k] < COLS)
            def _():
                pltpu.make_async_copy(first.at[origin[k], row_table[r]], *target).start()

            for n, source in enumerate(second):

                @pl.when(origin[k] == COLS + n)
                def _():
                    pltpu.make_async_copy(source.at[row_table[r]], *target).start()

    def leave(r):
        return pltpu.make_async_copy(held.at[r], out.at[r], sem_out.at[r, 0])

    def send(r):
        for k in range(HALF):
            pltpu.make_async_copy(first.at[0, 0], held.at[r, k], sem_in.at[r, k]).wait()
        leave(r).start()

    each(start)
    each(send)
    each(lambda r: leave(r).wait())


def pack_rows(row_table, row_has, origin, first, second, after):
    first = first.reshape(COLS, GRP, BLOCK, BLOCK)
    second = [x.reshape(GRP, BLOCK, BLOCK) for x in second]
    shape = (ROWS, HALF, BLOCK, BLOCK)
    return gather_call(
        pack_rows_kernel,
        [row_table, row_has, origin],
        [first] + second,
        [shape],
        [shape],
        (ROWS, HALF),
        "pack_rows",
        after,
    )[0]


def strip_kernel(place, keep, parent, blocks, *refs):
    out = refs[-1]
    out[...] = parent[...]
    for s in range(ROWS):

        @pl.when(keep[s] != 0)
        def _():
            at = lanes_of(place[s])
            out[:, at] = out[:, at] + blocks[s].T


def assemble_strip(place, keep, parent, blocks, after):
    vmem = pl.BlockSpec(memory_space=pltpu.VMEM)
    smem = pl.BlockSpec(memory_space=pltpu.SMEM)
    return pl.pallas_call(
        strip_kernel,
        in_specs=[smem, smem, vmem, vmem] + [pl.BlockSpec(memory_space=pl.ANY)] * len(after),
        out_specs=vmem,
        out_shape=jax.ShapeDtypeStruct((BLOCK, LEAD), F32),
        compiler_params=params(),
        cost_estimate=cost(0, 2 << 20),
        name="assemble_strip",
    )(place, keep, parent, blocks, *after)


def hand_on_kernel(given, *refs):
    refs[-1][...] = given[...]


def hand_on(given, after):
    vmem = pl.BlockSpec(memory_space=pltpu.VMEM)
    return pl.pallas_call(
        hand_on_kernel,
        in_specs=[vmem] + [pl.BlockSpec(memory_space=pl.ANY)] * len(after),
        out_specs=vmem,
        out_shape=jax.ShapeDtypeStruct(given.shape, F32),
        compiler_params=params(),
        cost_estimate=cost(0, 1 << 20),
        name="hand_on",
    )(given, *after)


def split(x):
    hi = x.astype(BF16)
    return hi, (x - hi.astype(F32)).astype(BF16)


def dot3(a_hi, a_lo, b_hi, b_lo):
    dims = (((1,), (1,)), ((), ()))
    total = lax.dot_general(a_hi, b_lo, dims, preferred_element_type=F32)
    total += lax.dot_general(a_lo, b_hi, dims, preferred_element_type=F32)
    return total + lax.dot_general(a_hi, b_hi, dims, preferred_element_type=F32)


def dot_full(a, b, dims):
    return lax.dot_general(
        a, b, (dims, ((), ())), precision=lax.Precision.HIGHEST, preferred_element_type=F32
    )


def invert_diagonal(work):
    lanes = lax.broadcasted_iota(jnp.int32, (BLOCK, BLOCK), 1)
    rows = lax.broadcasted_iota(jnp.int32, (BLOCK, BLOCK), 0)
    here, below, rest = work[0:8], work[8:16], work[16:]
    done = []
    for t in range(BLOCK // 8):
        base = 8 * t
        last = t == BLOCK // 8 - 1
        part = here if last else jnp.concatenate([here, below], axis=0)
        shape = part.shape
        lane = lanes[: shape[0]]
        row_id = rows[: shape[0]]
        cols = [jnp.broadcast_to(part[:, base + i : base + i + 1], shape) for i in range(8)]
        scale = jnp.zeros((8, BLOCK), F32)
        for i in range(8):
            root = lax.rsqrt(cols[i][i : i + 1])
            scale = jnp.where(row_id[:8] == i, root, scale)
            factor = jnp.where(row_id > i, cols[i] * (root * root), 0.0)
            for other in range(i + 1, 8):
                cols[other] = cols[other] - factor * cols[other][i : i + 1]
            row = jnp.where(lane[:1] == base + i, 1.0, part[i : i + 1])
            part = jnp.where(lane == base + i, jnp.where(row_id == i, 1.0, jnp.where(row_id > i, 0.0, part)), part)
            part = part - factor * row
        here = part[:8] * scale
        done.append(here)
        if t < BLOCK // 8 - 2:
            above = (lane[:8] > base + row_id[:8]) & (lane[:8] < base + 8)
            update = dot_full(here[:, base + 16 :], jnp.where(above, 0.0, here), ((0,), (0,)))
            inside = (lanes[: rest.shape[0]] >= base) & (lanes[: rest.shape[0]] < base + 8)
            rest = jnp.where(inside, 0.0, rest) - update
        if not last:
            here = part[8:]
            below, rest = rest[:8], rest[8:]
    whole = jnp.concatenate(done, axis=0)
    return jnp.where(rows >= lanes, whole, 0.0)


def factor_kernel(first, count, last, *refs):
    given, _, *refs = refs
    work = refs[-1] if last else refs[0]
    work[...] = given[...]
    total = LEAD // BLOCK

    def step(k, carry):
        here = lanes_of(k)
        inverse = invert_diagonal(work[here, here])
        work[here, :] = dot_full(inverse, work[here, :], ((1,), (0,)))
        work[here, here] = inverse

        def below(i, carry):
            there = lanes_of(i)
            lower = work[here, there]
            work[there, here] = jnp.zeros((BLOCK, BLOCK), F32)
            work[there, :] = work[there, :] - dot_full(lower, work[here, :], ((0,), (0,)))
            return carry

        return lax.fori_loop(k + 1, total, below, carry)

    lax.fori_loop(first, first + count, step, 0)
    if not last:
        return
    inv_hi, inv_lo = refs[0], refs[1]

    def finish(k, carry):
        here = lanes_of(k)
        rows = lax.broadcasted_iota(jnp.int32, (BLOCK, LEAD), 0) + k * BLOCK
        lanes = lax.broadcasted_iota(jnp.int32, (BLOCK, LEAD), 1)
        hi, lo = split(jnp.where(rows >= lanes, work[here, :], 0.0))
        inv_hi[here, :] = hi
        inv_lo[here, :] = lo
        return carry

    lax.fori_loop(0, total, finish, 0)


PARTS = 4


def factor_part(part, given, after):
    count = LEAD // BLOCK // PARTS
    whole = pl.BlockSpec(memory_space=pltpu.VMEM)
    last = part == PARTS - 1
    half = jax.ShapeDtypeStruct((LEAD, LEAD), BF16)
    full = jax.ShapeDtypeStruct((LEAD, LEAD), F32)
    return pl.pallas_call(
        functools.partial(factor_kernel, part * count, count, last),
        in_specs=[whole, pl.BlockSpec(memory_space=pl.ANY)],
        out_specs=[whole] * 2 if last else whole,
        out_shape=(half, half) if last else full,
        scratch_shapes=[pltpu.VMEM((LEAD, LEAD), F32)] if last else [],
        compiler_params=params(),
        cost_estimate=cost(25 * 10**9, 8 << 20),
        name="factor_lead",
    )(given, after)


TILE = 512
CHUNK = 1024


def solve_rows(rows, inv_hi, inv_lo):
    hi, lo = split(rows)
    parts = []
    for n in range(LEAD // 256):
        at, upto = pl.ds(n * 256, 256), (n + 1) * 256
        parts.append(
            dot3(hi[:, :upto], lo[:, :upto], inv_hi[at, pl.ds(0, upto)], inv_lo[at, pl.ds(0, upto)])
        )
    return jnp.concatenate(parts, axis=1)


def update_kernel(flags, row_strip, col_strip, inv_hi, inv_lo, parent, out, panel, hi, lo):
    step = pl.program_id(0)

    @pl.when(step == 0)
    def _():
        def chunk(n, carry):
            at = pl.ds(pl.multiple_of(n * CHUNK, CHUNK), CHUNK)
            values = solve_rows(row_strip[at, :], inv_hi, inv_lo)
            panel[at, :] = values
            hi[at, :], lo[at, :] = split(values)
            return carry

        lax.fori_loop(0, LEAD // CHUNK, chunk, 0)

    in_panel = (flags[1] == 0) & (step < LEAD // TILE)
    top = flags[0] == 0

    @pl.when(in_panel)
    def _():
        at = pl.ds(pl.multiple_of(step * TILE, TILE), TILE)
        rows = lax.broadcasted_iota(jnp.int32, (LEAD, TILE), 0)
        lanes = lax.broadcasted_iota(jnp.int32, (LEAD, TILE), 1) + step * TILE
        out[...] = jnp.where((rows >= lanes) | jnp.logical_not(top), panel[:, at], 0.0)

    @pl.when(jnp.logical_not(in_panel) & top)
    def _():
        out[...] = jnp.zeros_like(out)

    @pl.when(jnp.logical_not(in_panel) & jnp.logical_not(top))
    def _():
        right = split(solve_rows(col_strip[...], inv_hi, inv_lo))

        def chunk(n, carry):
            at = pl.ds(pl.multiple_of(n * CHUNK, CHUNK), CHUNK)
            out[at, :] = parent[at, :] - dot3(hi[at, :], lo[at, :], *right)
            return carry

        lax.fori_loop(0, LEAD // CHUNK, chunk, 0)


def update_front(flags, row_strip, col_strip, inv_hi, inv_lo, parent):
    rows, columns = parent.shape
    whole = lambda t, f: (0, 0)
    return pl.pallas_call(
        update_kernel,
        grid_spec=pltpu.PrefetchScalarGridSpec(
            num_scalar_prefetch=1,
            grid=(columns // TILE,),
            in_specs=[
                pl.BlockSpec((LEAD, LEAD), whole),
                pl.BlockSpec((TILE, LEAD), lambda t, f: (t, 0)),
                pl.BlockSpec((LEAD, LEAD), whole),
                pl.BlockSpec((LEAD, LEAD), whole),
                pl.BlockSpec((rows, TILE), lambda t, f: (0, t)),
            ],
            out_specs=pl.BlockSpec((rows, TILE), lambda t, f: (0, t)),
            scratch_shapes=[
                pltpu.VMEM((LEAD, LEAD), F32),
                pltpu.VMEM((LEAD, LEAD), BF16),
                pltpu.VMEM((LEAD, LEAD), BF16),
            ],
        ),
        out_shape=jax.ShapeDtypeStruct((rows, columns), F32),
        compiler_params=params(),
        cost_estimate=cost(40 * 10**9, 32 << 20),
        name="update_front",
    )(flags, row_strip, col_strip, inv_hi, inv_lo, parent)


def place_kernel(source, rank, keep, front, *refs):
    out = refs[-1]
    i = pl.program_id(0)
    for j in range(16):
        at = pl.ds(j * BLOCK, BLOCK)
        value = front[:, at]
        for h in range(2):
            k = rank[h, j]
            near, far = refs[2 * h], refs[2 * h + 1]
            block = jnp.where(
                k < HALF, near[0, jnp.minimum(k, HALF - 1)], far[0, jnp.maximum(k - HALF, 0)]
            )
            value = value + jnp.where(keep[h, i * 16 + j] != 0, block, 0.0)
        out[:, at] = value


def place_children(source, rank, keep, front, near, far):
    rows, columns = front.shape

    def spec(h):
        return pl.BlockSpec((1, HALF, BLOCK, BLOCK), lambda i, s, r, k: (s[h, i], 0, 0, 0))

    return pl.pallas_call(
        place_kernel,
        grid_spec=pltpu.PrefetchScalarGridSpec(
            num_scalar_prefetch=3,
            grid=(rows // BLOCK,),
            in_specs=[pl.BlockSpec((BLOCK, columns), lambda i, s, r, k: (i, 0))]
            + [spec(0), spec(0), spec(1), spec(1)],
            out_specs=pl.BlockSpec((BLOCK, columns), lambda i, s, r, k: (i, 0)),
        ),
        out_shape=jax.ShapeDtypeStruct((rows, columns), F32),
        input_output_aliases={3: 0},
        compiler_params=params(),
        cost_estimate=cost(0, 24 << 20),
        name="place_children",
    )(source, rank, keep, front, near, far, near, far)


def earlier_count(keys):
    places = jnp.arange(keys.shape[-1], dtype=jnp.int32)
    matches = keys[..., :, None] == keys[..., None, :]
    before = places[None, :] < places[:, None]
    return jnp.sum((matches & before).astype(jnp.int32), axis=-1)


def lookup(codes, values, length):
    hits = codes[..., :, None] == jnp.arange(length, dtype=jnp.int32)
    found = jnp.sum(jnp.where(hits, values[..., :, None], 0), axis=-2)
    return found, jnp.any(hits, axis=-2)


def body(parent_front, children, child_map, fill):
    row_index = lax.axis_index("row")
    col_index = lax.axis_index("col")
    child_id = row_index // COLS
    group_row = row_index % COLS
    blocks = child_map.shape[1]
    places = jnp.arange(blocks, dtype=jnp.int32)
    groups = places // GRP
    within = places % GRP
    run16 = child_map // 16
    run8 = child_map // 8
    slot = earlier_count(groups * COLS + run16)
    pick = lambda x: lax.dynamic_index_in_dim(x, child_id, 0, keepdims=False)
    own_map, own_run16, own_run8, own_slot = pick(child_map), pick(run16), pick(run8), pick(slot)

    col_codes = jnp.where(groups == col_index, own_run16 * 2 + own_slot, -1)
    send_cols, _ = lookup(col_codes, within, 2 * COLS)
    row_codes = jnp.where(groups == group_row, own_run8, -1)
    send_rows, sends = lookup(row_codes, within, ROWS)
    ahead = slot[:, None, :] * blocks + places < (slot * blocks + places)[:, :, None]
    rank_all = jnp.sum((ahead & (run16[:, None, :] == run16[:, :, None])).astype(jnp.int32), axis=-1)
    rank_codes = jnp.where(own_run16 == col_index, pick(rank_all), -1)
    origin = jnp.where(own_slot == 0, groups, COLS + (col_index - groups) % COLS)
    pick_cols, _ = lookup(rank_codes, origin, GRP)
    own_codes = jnp.where(own_run16 == col_index, own_map % 16, -1)
    pick_owner, _ = lookup(own_codes, groups * 2 + own_slot, 16)

    tile_rows = jnp.where(run8 == row_index, child_map % 8, -1)
    row_block, row_has = lookup(tile_rows, jnp.broadcast_to(places, (2, blocks)), 8)
    tile_cols = jnp.where(run16 == col_index, child_map % 16, -1)
    col_rank, col_has = lookup(tile_cols, rank_all, 16)
    row_hit = (tile_rows[:, None, :] == jnp.arange(8, dtype=jnp.int32)[None, :, None]).astype(F32)
    col_hit = (tile_cols[:, None, :] == jnp.arange(16, dtype=jnp.int32)[None, :, None]).astype(F32)
    present = fill.astype(F32)
    keep = jnp.einsum("hia,hab->hib", row_hit, present)
    keep = jnp.einsum("hib,hjb->hij", keep, col_hit)
    panel_col = (col_index == 0) & (jnp.arange(16) < NLEAD)
    keep = jnp.where(panel_col | (row_index == 0), 0.0, keep)
    keep = (keep > 0.5).astype(jnp.int32).reshape(2, 8 * 16)
    source = jnp.arange(2, dtype=jnp.int32)[:, None] * COLS + row_block // GRP

    owned = col_index * 16 + row_index
    lead_codes = jnp.where(run8 == 0, groups, -1)
    strip_place, strip_has = lookup(lead_codes, child_map, COLS)
    lead_hit = (lead_codes[:, None, :] == jnp.arange(COLS, dtype=jnp.int32)[None, :, None]).astype(F32)
    owned_hit = (child_map == owned).astype(F32)
    strip_keep = jnp.einsum("hga,hab->hgb", lead_hit, present)
    strip_keep = jnp.sum(strip_keep * owned_hit[:, None, :], axis=-1)
    strip_keep = (strip_keep > 0.5).astype(jnp.int32).reshape(ROWS)
    strip_place = jnp.where(strip_has, strip_place, 0).reshape(ROWS)

    axes = ("row", "col")
    number = lambda r, c: r * COLS + c

    total = lambda values: functools.reduce(lambda x, y: x + y, values)

    total = lambda values: functools.reduce(lambda x, y: x + y, values)

    pieces = cut_strip(parent_front)
    own = total([jnp.where(col_index == 0, pieces[0], 0.0)] + [
        lax.ppermute(pieces[i], axes, [(number(r, 0), number(r, i)) for r in range(ROWS)])
        for i in range(1, NLEAD)
    ])
    pairs = [(number(j % 16, j // 16), number(j // 8, j % 8)) for j in range(128)]
    strip_parent = lax.ppermute(own, axes, [(b, a) for a, b in pairs])

    early = pack_early(jnp.concatenate([send_cols, send_rows[:1]]), children)
    early = lax.all_to_all(early, "col", split_axis=0, concat_axis=0, tiled=True)
    early = pick_early(pick_owner, early, [])
    early = lax.all_to_all(early, "row", split_axis=0, concat_axis=0, tiled=True)
    strip = assemble_strip(strip_place, strip_keep, strip_parent, early, [])

    first = pack_first(send_cols[0::2], children, [])
    first = lax.all_to_all(first, "col", split_axis=0, concat_axis=0, tiled=True)

    half = BLOCK // 2
    piece = total([
        lax.ppermute(
            strip[part * half : (part + 1) * half],
            axes,
            [(number(j, 0), number(2 * j + part, 0)) for j in range(NLEAD)],
        )
        for part in range(2)
    ])
    piece = total([piece] + [
        lax.ppermute(piece, axes, [(number(r, 0), number(r, d)) for r in range(ROWS)])
        for d in range(1, COLS)
    ])
    lead = lax.all_gather(piece, "row", axis=0, tiled=True)

    col_strip = lax.all_gather(strip, "row", axis=0, tiled=True)

    row_raw = lax.ppermute(strip, axes, pairs)

    sends = sends.astype(jnp.int32)
    work = factor_part(0, lead, strip)
    near_out = pack_rows(send_rows, sends, pick_cols[:HALF], first, [], [row_raw])
    near = lax.all_to_all(near_out, "row", split_axis=0, concat_axis=0, tiled=True)
    shifts = (col_index + jnp.arange(COLS, dtype=jnp.int32)) % COLS
    parts = pack_second(jnp.take(send_cols, shifts * 2 + 1), children, [near_out])
    second = [parts[0]] + [
        lax.ppermute(parts[d], "col", [(c, (c + d) % COLS) for c in range(COLS)])
        for d in range(1, COLS)
    ]
    far_out = pack_rows(send_rows, sends, pick_cols[HALF:], first, second, [near, work])
    far = lax.all_to_all(far_out, "row", split_axis=0, concat_axis=0, tiled=True)
    work = factor_part(1, work, far_out)
    work = factor_part(2, work, far_out)
    inv_hi, inv_lo = factor_part(3, work, col_strip)
    row_piece = hand_on(row_raw, [near_out])
    row_strip = lax.all_gather(row_piece, "col", axis=0, tiled=True)
    flags = jnp.stack([row_index, col_index]).astype(jnp.int32)
    front = update_front(flags, row_strip, col_strip, inv_hi, inv_lo, parent_front)
    return place_children(source, col_rank, keep, front, near, far)


def solution(mesh):
    in_specs = (P("row", "col"), P("row", "col"), P(), P())
    out_specs = P("row", "col")
    return jax.shard_map(body, mesh=mesh, in_specs=in_specs, out_specs=out_specs, check_vma=False)
```

```python
import functools

import jax
import jax.numpy as jnp
from jax import lax
from jax.experimental import pallas as pl
from jax.experimental.pallas import tpu as pltpu
from jax.sharding import PartitionSpec as P

BLOCK = 128
LEAD = 1024
NLEAD = LEAD // BLOCK
GRP = 10
ROWS = 16
COLS = 8
VMEM = 56 * 1024 * 1024
F32 = jnp.float32
BF16 = jnp.bfloat16


def params(**kw):
    return pltpu.CompilerParams(vmem_limit_bytes=VMEM, **kw)


def cost(flops, bytes_accessed):
    return pl.CostEstimate(flops=flops, bytes_accessed=bytes_accessed, transcendentals=0)


def gather_call(kernel, tables, arrays, shapes, scratch, sems, name, after=()):
    moved = sum(4 * functools.reduce(lambda x, y: x * y, shape) for shape in shapes)
    count = len(tables) + len(arrays)

    def run(*refs):
        kernel(*refs[:count], *refs[count + len(after) :])

    return pl.pallas_call(
        run,
        in_specs=[pl.BlockSpec(memory_space=pltpu.SMEM)] * len(tables)
        + [pl.BlockSpec(memory_space=pl.ANY)] * (len(arrays) + len(after)),
        out_specs=[pl.BlockSpec(memory_space=pl.ANY)] * len(shapes),
        out_shape=[jax.ShapeDtypeStruct(shape, F32) for shape in shapes],
        scratch_shapes=[pltpu.VMEM(shape, F32) for shape in scratch]
        + [pltpu.SemaphoreType.DMA(sems), pltpu.SemaphoreType.DMA(sems)],
        compiler_params=params(),
        cost_estimate=cost(0, 2 * moved),
        name=name,
    )(*tables, *arrays, *after)


def lanes_of(block):
    return pl.ds(pl.multiple_of(block * BLOCK, BLOCK), BLOCK)


def relay(moves, sem_in, sem_out):
    first = [pltpu.make_async_copy(s, v, sem_in.at[n]) for n, (s, v, t) in enumerate(moves)]
    second = [pltpu.make_async_copy(v, t, sem_out.at[n]) for n, (s, v, t) in enumerate(moves)]
    for copy in first:
        copy.start()
    for one, other in zip(first, second):
        one.wait()
        other.start()
    for copy in second:
        copy.wait()


def pack_early_kernel(table, children, out, held, sem_in, sem_out):
    moves = []
    for s in range(2 * COLS):
        source = children.at[lanes_of(table[2 * COLS]), lanes_of(table[s])]
        moves.append((source, held.at[s], out.at[s]))
    relay(moves, sem_in, sem_out)


def pack_early(table, children):
    shape = (2 * COLS, BLOCK, BLOCK)
    return gather_call(
        pack_early_kernel, [table], [children], [shape], [shape], (2 * COLS,), "pack_early"
    )[0]


def pack_first_kernel(table, children, out, held, sem_in, sem_out):
    moves = [
        (children.at[:, lanes_of(table[s])], held.at[s], out.at[s]) for s in range(COLS)
    ]
    relay(moves, sem_in, sem_out)


def pack_first(table, children, after):
    shape = (COLS, children.shape[0], BLOCK)
    return gather_call(
        pack_first_kernel, [table], [children], [shape], [shape], (COLS,), "pack_first", after
    )[0]


def pack_second_kernel(table, children, *refs):
    wide, sem_in, sem_out = refs[COLS:]
    moves = [
        (children.at[:, lanes_of(table[s])], wide.at[s], refs[s]) for s in range(COLS)
    ]
    relay(moves, sem_in, sem_out)


def pack_second(table, children, after):
    wide = (children.shape[0], BLOCK)
    return gather_call(
        pack_second_kernel,
        [table],
        [children],
        [wide] * COLS,
        [(COLS,) + wide],
        (COLS,),
        "pack_second",
        after,
    )


def cut_kernel(parent, *refs):
    held, sem_in, sem_out = refs[NLEAD:]
    moves = []
    for i in range(NLEAD):
        source = parent.at[pl.ds(i * BLOCK, BLOCK), pl.ds(0, LEAD)]
        moves.append((source, held.at[i], refs[i]))
    relay(moves, sem_in, sem_out)


def cut_strip(parent):
    shape = (BLOCK, LEAD)
    return gather_call(
        cut_kernel, [], [parent], [shape] * NLEAD, [(NLEAD,) + shape], (NLEAD,), "cut_strip"
    )


def pick_early_kernel(table, blocks, out, held, sem_in, sem_out):
    relay([(blocks.at[table[s]], held.at[s], out.at[s]) for s in range(ROWS)], sem_in, sem_out)


def pick_early(table, blocks, after):
    shape = (ROWS, BLOCK, BLOCK)
    return gather_call(
        pick_early_kernel, [table], [blocks], [shape], [shape], (ROWS,), "pick_early", after
    )[0]


HALF = GRP // 2


def pack_rows_kernel(row_table, row_has, origin, first, *refs):
    second, (out, held, sem_in, sem_out) = refs[:-4], refs[-4:]

    def each(act):
        def one(r, carry):
            @pl.when(row_has[r] != 0)
            def _():
                act(r)

            return carry

        lax.fori_loop(0, ROWS, one, 0)

    def start(r):
        for k in range(HALF):
            target = (held.at[r, k], sem_in.at[r, k])

            @pl.when(origin[k] < COLS)
            def _():
                pltpu.make_async_copy(first.at[origin[k], row_table[r]], *target).start()

            for n, source in enumerate(second):

                @pl.when(origin[k] == COLS + n)
                def _():
                    pltpu.make_async_copy(source.at[row_table[r]], *target).start()

    def leave(r):
        return pltpu.make_async_copy(held.at[r], out.at[r], sem_out.at[r, 0])

    def send(r):
        for k in range(HALF):
            pltpu.make_async_copy(first.at[0, 0], held.at[r, k], sem_in.at[r, k]).wait()
        leave(r).start()

    each(start)
    each(send)
    each(lambda r: leave(r).wait())


def pack_rows(row_table, row_has, origin, first, second, after):
    first = first.reshape(COLS, GRP, BLOCK, BLOCK)
    second = [x.reshape(GRP, BLOCK, BLOCK) for x in second]
    shape = (ROWS, HALF, BLOCK, BLOCK)
    return gather_call(
        pack_rows_kernel,
        [row_table, row_has, origin],
        [first] + second,
        [shape],
        [shape],
        (ROWS, HALF),
        "pack_rows",
        after,
    )[0]


def strip_kernel(place, keep, parent, blocks, *refs):
    out = refs[-1]
    out[...] = parent[...]
    for s in range(ROWS):

        @pl.when(keep[s] != 0)
        def _():
            at = lanes_of(place[s])
            out[:, at] = out[:, at] + blocks[s].T


def assemble_strip(place, keep, parent, blocks, after):
    vmem = pl.BlockSpec(memory_space=pltpu.VMEM)
    smem = pl.BlockSpec(memory_space=pltpu.SMEM)
    return pl.pallas_call(
        strip_kernel,
        in_specs=[smem, smem, vmem, vmem] + [pl.BlockSpec(memory_space=pl.ANY)] * len(after),
        out_specs=vmem,
        out_shape=jax.ShapeDtypeStruct((BLOCK, LEAD), F32),
        compiler_params=params(),
        cost_estimate=cost(0, 2 << 20),
        name="assemble_strip",
    )(place, keep, parent, blocks, *after)


def hand_on_kernel(given, *refs):
    refs[-1][...] = given[...]


def hand_on(given, after):
    vmem = pl.BlockSpec(memory_space=pltpu.VMEM)
    return pl.pallas_call(
        hand_on_kernel,
        in_specs=[vmem] + [pl.BlockSpec(memory_space=pl.ANY)] * len(after),
        out_specs=vmem,
        out_shape=jax.ShapeDtypeStruct(given.shape, F32),
        compiler_params=params(),
        cost_estimate=cost(0, 1 << 20),
        name="hand_on",
    )(given, *after)


def split(x):
    hi = x.astype(BF16)
    return hi, (x - hi.astype(F32)).astype(BF16)


def dot3(a_hi, a_lo, b_hi, b_lo):
    dims = (((1,), (1,)), ((), ()))
    total = lax.dot_general(a_hi, b_lo, dims, preferred_element_type=F32)
    total += lax.dot_general(a_lo, b_hi, dims, preferred_element_type=F32)
    return total + lax.dot_general(a_hi, b_hi, dims, preferred_element_type=F32)


def dot_full(a, b, dims):
    return lax.dot_general(
        a, b, (dims, ((), ())), precision=lax.Precision.HIGHEST, preferred_element_type=F32
    )


def invert_diagonal(work):
    lanes = lax.broadcasted_iota(jnp.int32, (BLOCK, BLOCK), 1)
    rows = lax.broadcasted_iota(jnp.int32, (BLOCK, BLOCK), 0)
    here, below, rest = work[0:8], work[8:16], work[16:]
    done = []
    for t in range(BLOCK // 8):
        base = 8 * t
        last = t == BLOCK // 8 - 1
        part = here if last else jnp.concatenate([here, below], axis=0)
        shape = part.shape
        lane = lanes[: shape[0]]
        row_id = rows[: shape[0]]
        cols = [jnp.broadcast_to(part[:, base + i : base + i + 1], shape) for i in range(8)]
        scale = jnp.zeros((8, BLOCK), F32)
        for i in range(8):
            root = lax.rsqrt(cols[i][i : i + 1])
            scale = jnp.where(row_id[:8] == i, root, scale)
            factor = jnp.where(row_id > i, cols[i] * (root * root), 0.0)
            for other in range(i + 1, 8):
                cols[other] = cols[other] - factor * cols[other][i : i + 1]
            row = jnp.where(lane[:1] == base + i, 1.0, part[i : i + 1])
            part = jnp.where(lane == base + i, jnp.where(row_id == i, 1.0, jnp.where(row_id > i, 0.0, part)), part)
            part = part - factor * row
        here = part[:8] * scale
        done.append(here)
        if t < BLOCK // 8 - 2:
            above = (lane[:8] > base + row_id[:8]) & (lane[:8] < base + 8)
            update = dot_full(here[:, base + 16 :], jnp.where(above, 0.0, here), ((0,), (0,)))
            inside = (lanes[: rest.shape[0]] >= base) & (lanes[: rest.shape[0]] < base + 8)
            rest = jnp.where(inside, 0.0, rest) - update
        if not last:
            here = part[8:]
            below, rest = rest[:8], rest[8:]
    whole = jnp.concatenate(done, axis=0)
    return jnp.where(rows >= lanes, whole, 0.0)


def factor_kernel(first, count, last, *refs):
    given, _, *refs = refs
    work = refs[-1] if last else refs[0]
    work[...] = given[...]
    total = LEAD // BLOCK

    def step(k, carry):
        here = lanes_of(k)
        inverse = invert_diagonal(work[here, here])
        work[here, :] = dot_full(inverse, work[here, :], ((1,), (0,)))
        work[here, here] = inverse

        def below(i, carry):
            there = lanes_of(i)
            lower = work[here, there]
            work[there, here] = jnp.zeros((BLOCK, BLOCK), F32)
            work[there, :] = work[there, :] - dot_full(lower, work[here, :], ((0,), (0,)))
            return carry

        return lax.fori_loop(k + 1, total, below, carry)

    lax.fori_loop(first, first + count, step, 0)
    if not last:
        return
    inv_hi, inv_lo = refs[0], refs[1]

    def finish(k, carry):
        here = lanes_of(k)
        rows = lax.broadcasted_iota(jnp.int32, (BLOCK, LEAD), 0) + k * BLOCK
        lanes = lax.broadcasted_iota(jnp.int32, (BLOCK, LEAD), 1)
        hi, lo = split(jnp.where(rows >= lanes, work[here, :], 0.0))
        inv_hi[here, :] = hi
        inv_lo[here, :] = lo
        return carry

    lax.fori_loop(0, total, finish, 0)


PARTS = 4


def factor_part(part, given, after):
    count = LEAD // BLOCK // PARTS
    whole = pl.BlockSpec(memory_space=pltpu.VMEM)
    last = part == PARTS - 1
    half = jax.ShapeDtypeStruct((LEAD, LEAD), BF16)
    full = jax.ShapeDtypeStruct((LEAD, LEAD), F32)
    return pl.pallas_call(
        functools.partial(factor_kernel, part * count, count, last),
        in_specs=[whole, pl.BlockSpec(memory_space=pl.ANY)],
        out_specs=[whole] * 2 if last else whole,
        out_shape=(half, half) if last else full,
        scratch_shapes=[pltpu.VMEM((LEAD, LEAD), F32)] if last else [],
        compiler_params=params(),
        cost_estimate=cost(25 * 10**9, 8 << 20),
        name="factor_lead",
    )(given, after)


TILE = 512
CHUNK = 1024


def solve_rows(rows, inv_hi, inv_lo):
    hi, lo = split(rows)
    parts = []
    for n in range(LEAD // 256):
        at, upto = pl.ds(n * 256, 256), (n + 1) * 256
        parts.append(
            dot3(hi[:, :upto], lo[:, :upto], inv_hi[at, pl.ds(0, upto)], inv_lo[at, pl.ds(0, upto)])
        )
    return jnp.concatenate(parts, axis=1)


def update_kernel(flags, row_strip, col_strip, inv_hi, inv_lo, parent, out, panel, hi, lo):
    step = pl.program_id(0)

    @pl.when(step == 0)
    def _():
        def chunk(n, carry):
            at = pl.ds(pl.multiple_of(n * CHUNK, CHUNK), CHUNK)
            values = solve_rows(row_strip[at, :], inv_hi, inv_lo)
            panel[at, :] = values
            hi[at, :], lo[at, :] = split(values)
            return carry

        lax.fori_loop(0, LEAD // CHUNK, chunk, 0)

    in_panel = (flags[1] == 0) & (step < LEAD // TILE)
    top = flags[0] == 0

    @pl.when(in_panel)
    def _():
        at = pl.ds(pl.multiple_of(step * TILE, TILE), TILE)
        rows = lax.broadcasted_iota(jnp.int32, (LEAD, TILE), 0)
        lanes = lax.broadcasted_iota(jnp.int32, (LEAD, TILE), 1) + step * TILE
        out[...] = jnp.where((rows >= lanes) | jnp.logical_not(top), panel[:, at], 0.0)

    @pl.when(jnp.logical_not(in_panel) & top)
    def _():
        out[...] = jnp.zeros_like(out)

    @pl.when(jnp.logical_not(in_panel) & jnp.logical_not(top))
    def _():
        right = split(solve_rows(col_strip[...], inv_hi, inv_lo))

        def chunk(n, carry):
            at = pl.ds(pl.multiple_of(n * CHUNK, CHUNK), CHUNK)
            out[at, :] = parent[at, :] - dot3(hi[at, :], lo[at, :], *right)
            return carry

        lax.fori_loop(0, LEAD // CHUNK, chunk, 0)


def update_front(flags, row_strip, col_strip, inv_hi, inv_lo, parent):
    rows, columns = parent.shape
    whole = lambda t, f: (0, 0)
    return pl.pallas_call(
        update_kernel,
        grid_spec=pltpu.PrefetchScalarGridSpec(
            num_scalar_prefetch=1,
            grid=(columns // TILE,),
            in_specs=[
                pl.BlockSpec((LEAD, LEAD), whole),
                pl.BlockSpec((TILE, LEAD), lambda t, f: (t, 0)),
                pl.BlockSpec((LEAD, LEAD), whole),
                pl.BlockSpec((LEAD, LEAD), whole),
                pl.BlockSpec((rows, TILE), lambda t, f: (0, t)),
            ],
            out_specs=pl.BlockSpec((rows, TILE), lambda t, f: (0, t)),
            scratch_shapes=[
                pltpu.VMEM((LEAD, LEAD), F32),
                pltpu.VMEM((LEAD, LEAD), BF16),
                pltpu.VMEM((LEAD, LEAD), BF16),
            ],
        ),
        out_shape=jax.ShapeDtypeStruct((rows, columns), F32),
        compiler_params=params(),
        cost_estimate=cost(40 * 10**9, 32 << 20),
        name="update_front",
    )(flags, row_strip, col_strip, inv_hi, inv_lo, parent)


def place_kernel(source, rank, keep, front, *refs):
    out = refs[-1]
    i = pl.program_id(0)
    for j in range(16):
        at = pl.ds(j * BLOCK, BLOCK)
        value = front[:, at]
        for h in range(2):
            k = rank[h, j]
            near, far = refs[2 * h], refs[2 * h + 1]
            block = jnp.where(
                k < HALF, near[0, jnp.minimum(k, HALF - 1)], far[0, jnp.maximum(k - HALF, 0)]
            )
            value = value + jnp.where(keep[h, i * 16 + j] != 0, block, 0.0)
        out[:, at] = value


def place_children(source, rank, keep, front, near, far):
    rows, columns = front.shape

    def spec(h):
        return pl.BlockSpec((1, HALF, BLOCK, BLOCK), lambda i, s, r, k: (s[h, i], 0, 0, 0))

    return pl.pallas_call(
        place_kernel,
        grid_spec=pltpu.PrefetchScalarGridSpec(
            num_scalar_prefetch=3,
            grid=(rows // BLOCK,),
            in_specs=[pl.BlockSpec((BLOCK, columns), lambda i, s, r, k: (i, 0))]
            + [spec(0), spec(0), spec(1), spec(1)],
            out_specs=pl.BlockSpec((BLOCK, columns), lambda i, s, r, k: (i, 0)),
        ),
        out_shape=jax.ShapeDtypeStruct((rows, columns), F32),
        input_output_aliases={3: 0},
        compiler_params=params(),
        cost_estimate=cost(0, 24 << 20),
        name="place_children",
    )(source, rank, keep, front, near, far, near, far)


def earlier_count(keys):
    places = jnp.arange(keys.shape[-1], dtype=jnp.int32)
    matches = keys[..., :, None] == keys[..., None, :]
    before = places[None, :] < places[:, None]
    return jnp.sum((matches & before).astype(jnp.int32), axis=-1)


def lookup(codes, values, length):
    hits = codes[..., :, None] == jnp.arange(length, dtype=jnp.int32)
    found = jnp.sum(jnp.where(hits, values[..., :, None], 0), axis=-2)
    return found, jnp.any(hits, axis=-2)


def body(parent_front, children, child_map, fill):
    row_index = lax.axis_index("row")
    col_index = lax.axis_index("col")
    child_id = row_index // COLS
    group_row = row_index % COLS
    blocks = child_map.shape[1]
    places = jnp.arange(blocks, dtype=jnp.int32)
    groups = places // GRP
    within = places % GRP
    run16 = child_map // 16
    run8 = child_map // 8
    slot = earlier_count(groups * COLS + run16)
    pick = lambda x: lax.dynamic_index_in_dim(x, child_id, 0, keepdims=False)
    own_map, own_run16, own_run8, own_slot = pick(child_map), pick(run16), pick(run8), pick(slot)

    col_codes = jnp.where(groups == col_index, own_run16 * 2 + own_slot, -1)
    send_cols, _ = lookup(col_codes, within, 2 * COLS)
    row_codes = jnp.where(groups == group_row, own_run8, -1)
    send_rows, sends = lookup(row_codes, within, ROWS)
    ahead = slot[:, None, :] * blocks + places < (slot * blocks + places)[:, :, None]
    rank_all = jnp.sum((ahead & (run16[:, None, :] == run16[:, :, None])).astype(jnp.int32), axis=-1)
    rank_codes = jnp.where(own_run16 == col_index, pick(rank_all), -1)
    origin = jnp.where(own_slot == 0, groups, COLS + (col_index - groups) % COLS)
    pick_cols, _ = lookup(rank_codes, origin, GRP)
    own_codes = jnp.where(own_run16 == col_index, own_map % 16, -1)
    pick_owner, _ = lookup(own_codes, groups * 2 + own_slot, 16)

    tile_rows = jnp.where(run8 == row_index, child_map % 8, -1)
    row_block, row_has = lookup(tile_rows, jnp.broadcast_to(places, (2, blocks)), 8)
    tile_cols = jnp.where(run16 == col_index, child_map % 16, -1)
    col_rank, col_has = lookup(tile_cols, rank_all, 16)
    row_hit = (tile_rows[:, None, :] == jnp.arange(8, dtype=jnp.int32)[None, :, None]).astype(F32)
    col_hit = (tile_cols[:, None, :] == jnp.arange(16, dtype=jnp.int32)[None, :, None]).astype(F32)
    present = fill.astype(F32)
    keep = jnp.einsum("hia,hab->hib", row_hit, present)
    keep = jnp.einsum("hib,hjb->hij", keep, col_hit)
    panel_col = (col_index == 0) & (jnp.arange(16) < NLEAD)
    keep = jnp.where(panel_col | (row_index == 0), 0.0, keep)
    keep = (keep > 0.5).astype(jnp.int32).reshape(2, 8 * 16)
    source = jnp.arange(2, dtype=jnp.int32)[:, None] * COLS + row_block // GRP

    owned = col_index * 16 + row_index
    lead_codes = jnp.where(run8 == 0, groups, -1)
    strip_place, strip_has = lookup(lead_codes, child_map, COLS)
    lead_hit = (lead_codes[:, None, :] == jnp.arange(COLS, dtype=jnp.int32)[None, :, None]).astype(F32)
    owned_hit = (child_map == owned).astype(F32)
    strip_keep = jnp.einsum("hga,hab->hgb", lead_hit, present)
    strip_keep = jnp.sum(strip_keep * owned_hit[:, None, :], axis=-1)
    strip_keep = (strip_keep > 0.5).astype(jnp.int32).reshape(ROWS)
    strip_place = jnp.where(strip_has, strip_place, 0).reshape(ROWS)

    axes = ("row", "col")
    number = lambda r, c: r * COLS + c

    total = lambda values: functools.reduce(lambda x, y: x + y, values)

    total = lambda values: functools.reduce(lambda x, y: x + y, values)

    pieces = cut_strip(parent_front)
    own = total([jnp.where(col_index == 0, pieces[0], 0.0)] + [
        lax.ppermute(pieces[i], axes, [(number(r, 0), number(r, i)) for r in range(ROWS)])
        for i in range(1, NLEAD)
    ])
    pairs = [(number(j % 16, j // 16), number(j // 8, j % 8)) for j in range(128)]
    strip_parent = lax.ppermute(own, axes, [(b, a) for a, b in pairs])

    early = pack_early(jnp.concatenate([send_cols, send_rows[:1]]), children)
    early = lax.all_to_all(early, "col", split_axis=0, concat_axis=0, tiled=True)
    early = pick_early(pick_owner, early, [])
    early = lax.all_to_all(early, "row", split_axis=0, concat_axis=0, tiled=True)
    strip = assemble_strip(strip_place, strip_keep, strip_parent, early, [])

    first = pack_first(send_cols[0::2], children, [strip])
    first = lax.all_to_all(first, "col", split_axis=0, concat_axis=0, tiled=True)

    col_strip = lax.all_gather(strip, "row", axis=0, tiled=True)

    row_raw = lax.ppermute(strip, axes, pairs)

    half = BLOCK // 2
    piece = total([
        lax.ppermute(
            strip[part * half : (part + 1) * half],
            axes,
            [(number(j, 0), number(2 * j + part, 0)) for j in range(NLEAD)],
        )
        for part in range(2)
    ])
    piece = total([piece] + [
        lax.ppermute(piece, axes, [(number(r, 0), number(r, d)) for r in range(ROWS)])
        for d in range(1, COLS)
    ])
    lead = lax.all_gather(hand_on(piece, [first, row_raw, col_strip]), "row", axis=0, tiled=True)


    sends = sends.astype(jnp.int32)
    work = factor_part(0, lead, strip)
    near_out = pack_rows(send_rows, sends, pick_cols[:HALF], first, [], [lead])
    near = lax.all_to_all(near_out, "row", split_axis=0, concat_axis=0, tiled=True)
    shifts = (col_index + jnp.arange(COLS, dtype=jnp.int32)) % COLS
    parts = pack_second(jnp.take(send_cols, shifts * 2 + 1), children, [near_out])
    second = [parts[0]] + [
        lax.ppermute(parts[d], "col", [(c, (c + d) % COLS) for c in range(COLS)])
        for d in range(1, COLS)
    ]
    work = factor_part(1, work, near_out)
    far_out = pack_rows(send_rows, sends, pick_cols[HALF:], first, second, [near, work])
    far = lax.all_to_all(far_out, "row", split_axis=0, concat_axis=0, tiled=True)
    work = factor_part(2, work, far_out)
    inv_hi, inv_lo = factor_part(3, work, far_out)
    row_piece = hand_on(row_raw, [near_out])
    row_strip = lax.all_gather(row_piece, "col", axis=0, tiled=True)
    flags = jnp.stack([row_index, col_index]).astype(jnp.int32)
    front = update_front(flags, row_strip, col_strip, inv_hi, inv_lo, parent_front)
    return place_children(source, col_rank, keep, front, near, far)


def solution(mesh):
    in_specs = (P("row", "col"), P("row", "col"), P(), P())
    out_specs = P("row", "col")
    return jax.shard_map(body, mesh=mesh, in_specs=in_specs, out_specs=out_specs, check_vma=False)
```

```python
import functools

import jax
import jax.numpy as jnp
from jax import lax
from jax.experimental import pallas as pl
from jax.experimental.pallas import tpu as pltpu
from jax.sharding import PartitionSpec as P

BLOCK = 128
LEAD = 1024
NLEAD = LEAD // BLOCK
GRP = 10
ROWS = 16
COLS = 8
VMEM = 56 * 1024 * 1024
F32 = jnp.float32
BF16 = jnp.bfloat16


def params(**kw):
    return pltpu.CompilerParams(vmem_limit_bytes=VMEM, **kw)


def cost(flops, bytes_accessed):
    return pl.CostEstimate(flops=flops, bytes_accessed=bytes_accessed, transcendentals=0)


def gather_call(kernel, tables, arrays, shapes, scratch, sems, name, after=()):
    moved = sum(4 * functools.reduce(lambda x, y: x * y, shape) for shape in shapes)
    count = len(tables) + len(arrays)

    def run(*refs):
        kernel(*refs[:count], *refs[count + len(after) :])

    return pl.pallas_call(
        run,
        in_specs=[pl.BlockSpec(memory_space=pltpu.SMEM)] * len(tables)
        + [pl.BlockSpec(memory_space=pl.ANY)] * (len(arrays) + len(after)),
        out_specs=[pl.BlockSpec(memory_space=pl.ANY)] * len(shapes),
        out_shape=[jax.ShapeDtypeStruct(shape, F32) for shape in shapes],
        scratch_shapes=[pltpu.VMEM(shape, F32) for shape in scratch]
        + [pltpu.SemaphoreType.DMA(sems), pltpu.SemaphoreType.DMA(sems)],
        compiler_params=params(),
        cost_estimate=cost(0, 2 * moved),
        name=name,
    )(*tables, *arrays, *after)


def lanes_of(block):
    return pl.ds(pl.multiple_of(block * BLOCK, BLOCK), BLOCK)


def relay(moves, sem_in, sem_out):
    first = [pltpu.make_async_copy(s, v, sem_in.at[n]) for n, (s, v, t) in enumerate(moves)]
    second = [pltpu.make_async_copy(v, t, sem_out.at[n]) for n, (s, v, t) in enumerate(moves)]
    for copy in first:
        copy.start()
    for one, other in zip(first, second):
        one.wait()
        other.start()
    for copy in second:
        copy.wait()


def pack_early_kernel(table, children, out, held, sem_in, sem_out):
    moves = []
    for s in range(2 * COLS):
        source = children.at[lanes_of(table[2 * COLS]), lanes_of(table[s])]
        moves.append((source, held.at[s], out.at[s]))
    relay(moves, sem_in, sem_out)


def pack_early(table, children):
    shape = (2 * COLS, BLOCK, BLOCK)
    return gather_call(
        pack_early_kernel, [table], [children], [shape], [shape], (2 * COLS,), "pack_early"
    )[0]


def pack_first_kernel(table, children, out, held, sem_in, sem_out):
    moves = [
        (children.at[:, lanes_of(table[s])], held.at[s], out.at[s]) for s in range(COLS)
    ]
    relay(moves, sem_in, sem_out)


def pack_first(table, children, after):
    shape = (COLS, children.shape[0], BLOCK)
    return gather_call(
        pack_first_kernel, [table], [children], [shape], [shape], (COLS,), "pack_first", after
    )[0]


def pack_second_kernel(table, children, *refs):
    wide, sem_in, sem_out = refs[COLS:]
    moves = [
        (children.at[:, lanes_of(table[s])], wide.at[s], refs[s]) for s in range(COLS)
    ]
    relay(moves, sem_in, sem_out)


def pack_second(table, children, after):
    wide = (children.shape[0], BLOCK)
    return gather_call(
        pack_second_kernel,
        [table],
        [children],
        [wide] * COLS,
        [(COLS,) + wide],
        (COLS,),
        "pack_second",
        after,
    )


def cut_kernel(parent, *refs):
    held, sem_in, sem_out = refs[NLEAD:]
    moves = []
    for i in range(NLEAD):
        source = parent.at[pl.ds(i * BLOCK, BLOCK), pl.ds(0, LEAD)]
        moves.append((source, held.at[i], refs[i]))
    relay(moves, sem_in, sem_out)


def cut_strip(parent):
    shape = (BLOCK, LEAD)
    return gather_call(
        cut_kernel, [], [parent], [shape] * NLEAD, [(NLEAD,) + shape], (NLEAD,), "cut_strip"
    )


def pick_early_kernel(table, blocks, out, held, sem_in, sem_out):
    relay([(blocks.at[table[s]], held.at[s], out.at[s]) for s in range(ROWS)], sem_in, sem_out)


def pick_early(table, blocks, after):
    shape = (ROWS, BLOCK, BLOCK)
    return gather_call(
        pick_early_kernel, [table], [blocks], [shape], [shape], (ROWS,), "pick_early", after
    )[0]


HALF = GRP // 2


def pack_rows_kernel(row_table, row_has, origin, first, *refs):
    second, (out, held, sem_in, sem_out) = refs[:-4], refs[-4:]

    def each(act):
        def one(r, carry):
            @pl.when(row_has[r] != 0)
            def _():
                act(r)

            return carry

        lax.fori_loop(0, ROWS, one, 0)

    def start(r):
        for k in range(HALF):
            target = (held.at[r, k], sem_in.at[r, k])

            @pl.when(origin[k] < COLS)
            def _():
                pltpu.make_async_copy(first.at[origin[k], row_table[r]], *target).start()

            for n, source in enumerate(second):

                @pl.when(origin[k] == COLS + n)
                def _():
                    pltpu.make_async_copy(source.at[row_table[r]], *target).start()

    def leave(r):
        return pltpu.make_async_copy(held.at[r], out.at[r], sem_out.at[r, 0])

    def send(r):
        for k in range(HALF):
            pltpu.make_async_copy(first.at[0, 0], held.at[r, k], sem_in.at[r, k]).wait()
        leave(r).start()

    each(start)
    each(send)
    each(lambda r: leave(r).wait())


def pack_rows(row_table, row_has, origin, first, second, after):
    first = first.reshape(COLS, GRP, BLOCK, BLOCK)
    second = [x.reshape(GRP, BLOCK, BLOCK) for x in second]
    shape = (ROWS, HALF, BLOCK, BLOCK)
    return gather_call(
        pack_rows_kernel,
        [row_table, row_has, origin],
        [first] + second,
        [shape],
        [shape],
        (ROWS, HALF),
        "pack_rows",
        after,
    )[0]


def strip_kernel(place, keep, parent, blocks, *refs):
    out = refs[-1]
    out[...] = parent[...]
    for s in range(ROWS):

        @pl.when(keep[s] != 0)
        def _():
            at = lanes_of(place[s])
            out[:, at] = out[:, at] + blocks[s].T


def assemble_strip(place, keep, parent, blocks, after):
    vmem = pl.BlockSpec(memory_space=pltpu.VMEM)
    smem = pl.BlockSpec(memory_space=pltpu.SMEM)
    return pl.pallas_call(
        strip_kernel,
        in_specs=[smem, smem, vmem, vmem] + [pl.BlockSpec(memory_space=pl.ANY)] * len(after),
        out_specs=vmem,
        out_shape=jax.ShapeDtypeStruct((BLOCK, LEAD), F32),
        compiler_params=params(),
        cost_estimate=cost(0, 2 << 20),
        name="assemble_strip",
    )(place, keep, parent, blocks, *after)


def hand_on_kernel(given, *refs):
    refs[-1][...] = given[...]


def hand_on(given, after):
    vmem = pl.BlockSpec(memory_space=pltpu.VMEM)
    return pl.pallas_call(
        hand_on_kernel,
        in_specs=[vmem] + [pl.BlockSpec(memory_space=pl.ANY)] * len(after),
        out_specs=vmem,
        out_shape=jax.ShapeDtypeStruct(given.shape, F32),
        compiler_params=params(),
        cost_estimate=cost(0, 1 << 20),
        name="hand_on",
    )(given, *after)


def split(x):
    hi = x.astype(BF16)
    return hi, (x - hi.astype(F32)).astype(BF16)


def dot3(a_hi, a_lo, b_hi, b_lo):
    dims = (((1,), (1,)), ((), ()))
    total = lax.dot_general(a_hi, b_lo, dims, preferred_element_type=F32)
    total += lax.dot_general(a_lo, b_hi, dims, preferred_element_type=F32)
    return total + lax.dot_general(a_hi, b_hi, dims, preferred_element_type=F32)


def dot_full(a, b, dims):
    return lax.dot_general(
        a, b, (dims, ((), ())), precision=lax.Precision.HIGHEST, preferred_element_type=F32
    )


def invert_diagonal(work):
    lanes = lax.broadcasted_iota(jnp.int32, (BLOCK, BLOCK), 1)
    rows = lax.broadcasted_iota(jnp.int32, (BLOCK, BLOCK), 0)
    here, below, rest = work[0:8], work[8:16], work[16:]
    done = []
    for t in range(BLOCK // 8):
        base = 8 * t
        last = t == BLOCK // 8 - 1
        part = here if last else jnp.concatenate([here, below], axis=0)
        shape = part.shape
        lane = lanes[: shape[0]]
        row_id = rows[: shape[0]]
        cols = [jnp.broadcast_to(part[:, base + i : base + i + 1], shape) for i in range(8)]
        scale = jnp.zeros((8, BLOCK), F32)
        for i in range(8):
            root = lax.rsqrt(cols[i][i : i + 1])
            scale = jnp.where(row_id[:8] == i, root, scale)
            factor = jnp.where(row_id > i, cols[i] * (root * root), 0.0)
            for other in range(i + 1, 8):
                cols[other] = cols[other] - factor * cols[other][i : i + 1]
            row = jnp.where(lane[:1] == base + i, 1.0, part[i : i + 1])
            part = jnp.where(lane == base + i, jnp.where(row_id == i, 1.0, jnp.where(row_id > i, 0.0, part)), part)
            part = part - factor * row
        here = part[:8] * scale
        done.append(here)
        if t < BLOCK // 8 - 2:
            above = (lane[:8] > base + row_id[:8]) & (lane[:8] < base + 8)
            update = dot_full(here[:, base + 16 :], jnp.where(above, 0.0, here), ((0,), (0,)))
            inside = (lanes[: rest.shape[0]] >= base) & (lanes[: rest.shape[0]] < base + 8)
            rest = jnp.where(inside, 0.0, rest) - update
        if not last:
            here = part[8:]
            below, rest = rest[:8], rest[8:]
    whole = jnp.concatenate(done, axis=0)
    return jnp.where(rows >= lanes, whole, 0.0)


def factor_kernel(first, count, last, *refs):
    given, _, *refs = refs
    work = refs[-1] if last else refs[0]
    work[...] = given[...]
    total = LEAD // BLOCK

    def step(k, carry):
        here = lanes_of(k)
        inverse = invert_diagonal(work[here, here])
        work[here, :] = dot_full(inverse, work[here, :], ((1,), (0,)))
        work[here, here] = inverse

        def below(i, carry):
            there = lanes_of(i)
            lower = work[here, there]
            work[there, here] = jnp.zeros((BLOCK, BLOCK), F32)
            work[there, :] = work[there, :] - dot_full(lower, work[here, :], ((0,), (0,)))
            return carry

        return lax.fori_loop(k + 1, total, below, carry)

    lax.fori_loop(first, first + count, step, 0)
    if not last:
        return
    inv_hi, inv_lo = refs[0], refs[1]

    def finish(k, carry):
        here = lanes_of(k)
        rows = lax.broadcasted_iota(jnp.int32, (BLOCK, LEAD), 0) + k * BLOCK
        lanes = lax.broadcasted_iota(jnp.int32, (BLOCK, LEAD), 1)
        hi, lo = split(jnp.where(rows >= lanes, work[here, :], 0.0))
        inv_hi[here, :] = hi
        inv_lo[here, :] = lo
        return carry

    lax.fori_loop(0, total, finish, 0)


PARTS = 4


def factor_part(part, given, after):
    count = LEAD // BLOCK // PARTS
    whole = pl.BlockSpec(memory_space=pltpu.VMEM)
    last = part == PARTS - 1
    half = jax.ShapeDtypeStruct((LEAD, LEAD), BF16)
    full = jax.ShapeDtypeStruct((LEAD, LEAD), F32)
    return pl.pallas_call(
        functools.partial(factor_kernel, part * count, count, last),
        in_specs=[whole, pl.BlockSpec(memory_space=pl.ANY)],
        out_specs=[whole] * 2 if last else whole,
        out_shape=(half, half) if last else full,
        scratch_shapes=[pltpu.VMEM((LEAD, LEAD), F32)] if last else [],
        compiler_params=params(),
        cost_estimate=cost(25 * 10**9, 8 << 20),
        name="factor_lead",
    )(given, after)


TILE = 512
CHUNK = 1024


def solve_rows(rows, inv_hi, inv_lo):
    hi, lo = split(rows)
    parts = []
    for n in range(LEAD // 256):
        at, upto = pl.ds(n * 256, 256), (n + 1) * 256
        parts.append(
            dot3(hi[:, :upto], lo[:, :upto], inv_hi[at, pl.ds(0, upto)], inv_lo[at, pl.ds(0, upto)])
        )
    return jnp.concatenate(parts, axis=1)


def update_kernel(flags, row_strip, col_strip, inv_hi, inv_lo, parent, out, panel, hi, lo):
    step = pl.program_id(0)

    @pl.when(step == 0)
    def _():
        def chunk(n, carry):
            at = pl.ds(pl.multiple_of(n * CHUNK, CHUNK), CHUNK)
            values = solve_rows(row_strip[at, :], inv_hi, inv_lo)
            panel[at, :] = values
            hi[at, :], lo[at, :] = split(values)
            return carry

        lax.fori_loop(0, LEAD // CHUNK, chunk, 0)

    in_panel = (flags[1] == 0) & (step < LEAD // TILE)
    top = flags[0] == 0

    @pl.when(in_panel)
    def _():
        at = pl.ds(pl.multiple_of(step * TILE, TILE), TILE)
        rows = lax.broadcasted_iota(jnp.int32, (LEAD, TILE), 0)
        lanes = lax.broadcasted_iota(jnp.int32, (LEAD, TILE), 1) + step * TILE
        out[...] = jnp.where((rows >= lanes) | jnp.logical_not(top), panel[:, at], 0.0)

    @pl.when(jnp.logical_not(in_panel) & top)
    def _():
        out[...] = jnp.zeros_like(out)

    @pl.when(jnp.logical_not(in_panel) & jnp.logical_not(top))
    def _():
        right = split(solve_rows(col_strip[...], inv_hi, inv_lo))

        def chunk(n, carry):
            at = pl.ds(pl.multiple_of(n * CHUNK, CHUNK), CHUNK)
            out[at, :] = parent[at, :] - dot3(hi[at, :], lo[at, :], *right)
            return carry

        lax.fori_loop(0, LEAD // CHUNK, chunk, 0)


def update_front(flags, row_strip, col_strip, inv_hi, inv_lo, parent):
    rows, columns = parent.shape
    whole = lambda t, f: (0, 0)
    return pl.pallas_call(
        update_kernel,
        grid_spec=pltpu.PrefetchScalarGridSpec(
            num_scalar_prefetch=1,
            grid=(columns // TILE,),
            in_specs=[
                pl.BlockSpec((LEAD, LEAD), whole),
                pl.BlockSpec((TILE, LEAD), lambda t, f: (t, 0)),
                pl.BlockSpec((LEAD, LEAD), whole),
                pl.BlockSpec((LEAD, LEAD), whole),
                pl.BlockSpec((rows, TILE), lambda t, f: (0, t)),
            ],
            out_specs=pl.BlockSpec((rows, TILE), lambda t, f: (0, t)),
            scratch_shapes=[
                pltpu.VMEM((LEAD, LEAD), F32),
                pltpu.VMEM((LEAD, LEAD), BF16),
                pltpu.VMEM((LEAD, LEAD), BF16),
            ],
        ),
        out_shape=jax.ShapeDtypeStruct((rows, columns), F32),
        compiler_params=params(),
        cost_estimate=cost(40 * 10**9, 32 << 20),
        name="update_front",
    )(flags, row_strip, col_strip, inv_hi, inv_lo, parent)


def place_kernel(source, rank, keep, front, *refs):
    out = refs[-1]
    i = pl.program_id(0)
    for j in range(16):
        at = pl.ds(j * BLOCK, BLOCK)
        value = front[:, at]
        for h in range(2):
            k = rank[h, j]
            near, far = refs[2 * h], refs[2 * h + 1]
            block = jnp.where(
                k < HALF, near[0, jnp.minimum(k, HALF - 1)], far[0, jnp.maximum(k - HALF, 0)]
            )
            value = value + jnp.where(keep[h, i * 16 + j] != 0, block, 0.0)
        out[:, at] = value


def place_children(source, rank, keep, front, near, far):
    rows, columns = front.shape

    def spec(h):
        return pl.BlockSpec((1, HALF, BLOCK, BLOCK), lambda i, s, r, k: (s[h, i], 0, 0, 0))

    return pl.pallas_call(
        place_kernel,
        grid_spec=pltpu.PrefetchScalarGridSpec(
            num_scalar_prefetch=3,
            grid=(rows // BLOCK,),
            in_specs=[pl.BlockSpec((BLOCK, columns), lambda i, s, r, k: (i, 0))]
            + [spec(0), spec(0), spec(1), spec(1)],
            out_specs=pl.BlockSpec((BLOCK, columns), lambda i, s, r, k: (i, 0)),
        ),
        out_shape=jax.ShapeDtypeStruct((rows, columns), F32),
        input_output_aliases={3: 0},
        compiler_params=params(),
        cost_estimate=cost(0, 24 << 20),
        name="place_children",
    )(source, rank, keep, front, near, far, near, far)


def earlier_count(keys):
    places = jnp.arange(keys.shape[-1], dtype=jnp.int32)
    matches = keys[..., :, None] == keys[..., None, :]
    before = places[None, :] < places[:, None]
    return jnp.sum((matches & before).astype(jnp.int32), axis=-1)


def lookup(codes, values, length):
    hits = codes[..., :, None] == jnp.arange(length, dtype=jnp.int32)
    found = jnp.sum(jnp.where(hits, values[..., :, None], 0), axis=-2)
    return found, jnp.any(hits, axis=-2)


def body(parent_front, children, child_map, fill):
    row_index = lax.axis_index("row")
    col_index = lax.axis_index("col")
    child_id = row_index // COLS
    group_row = row_index % COLS
    blocks = child_map.shape[1]
    places = jnp.arange(blocks, dtype=jnp.int32)
    groups = places // GRP
    within = places % GRP
    run16 = child_map // 16
    run8 = child_map // 8
    slot = earlier_count(groups * COLS + run16)
    pick = lambda x: lax.dynamic_index_in_dim(x, child_id, 0, keepdims=False)
    own_map, own_run16, own_run8, own_slot = pick(child_map), pick(run16), pick(run8), pick(slot)

    col_codes = jnp.where(groups == col_index, own_run16 * 2 + own_slot, -1)
    send_cols, _ = lookup(col_codes, within, 2 * COLS)
    row_codes = jnp.where(groups == group_row, own_run8, -1)
    send_rows, sends = lookup(row_codes, within, ROWS)
    ahead = slot[:, None, :] * blocks + places < (slot * blocks + places)[:, :, None]
    rank_all = jnp.sum((ahead & (run16[:, None, :] == run16[:, :, None])).astype(jnp.int32), axis=-1)
    rank_codes = jnp.where(own_run16 == col_index, pick(rank_all), -1)
    origin = jnp.where(own_slot == 0, groups, COLS + (col_index - groups) % COLS)
    pick_cols, _ = lookup(rank_codes, origin, GRP)
    own_codes = jnp.where(own_run16 == col_index, own_map % 16, -1)
    pick_owner, _ = lookup(own_codes, groups * 2 + own_slot, 16)

    tile_rows = jnp.where(run8 == row_index, child_map % 8, -1)
    row_block, row_has = lookup(tile_rows, jnp.broadcast_to(places, (2, blocks)), 8)
    tile_cols = jnp.where(run16 == col_index, child_map % 16, -1)
    col_rank, col_has = lookup(tile_cols, rank_all, 16)
    row_hit = (tile_rows[:, None, :] == jnp.arange(8, dtype=jnp.int32)[None, :, None]).astype(F32)
    col_hit = (tile_cols[:, None, :] == jnp.arange(16, dtype=jnp.int32)[None, :, None]).astype(F32)
    present = fill.astype(F32)
    keep = jnp.einsum("hia,hab->hib", row_hit, present)
    keep = jnp.einsum("hib,hjb->hij", keep, col_hit)
    panel_col = (col_index == 0) & (jnp.arange(16) < NLEAD)
    keep = jnp.where(panel_col | (row_index == 0), 0.0, keep)
    keep = (keep > 0.5).astype(jnp.int32).reshape(2, 8 * 16)
    source = jnp.arange(2, dtype=jnp.int32)[:, None] * COLS + row_block // GRP

    owned = col_index * 16 + row_index
    lead_codes = jnp.where(run8 == 0, groups, -1)
    strip_place, strip_has = lookup(lead_codes, child_map, COLS)
    lead_hit = (lead_codes[:, None, :] == jnp.arange(COLS, dtype=jnp.int32)[None, :, None]).astype(F32)
    owned_hit = (child_map == owned).astype(F32)
    strip_keep = jnp.einsum("hga,hab->hgb", lead_hit, present)
    strip_keep = jnp.sum(strip_keep * owned_hit[:, None, :], axis=-1)
    strip_keep = (strip_keep > 0.5).astype(jnp.int32).reshape(ROWS)
    strip_place = jnp.where(strip_has, strip_place, 0).reshape(ROWS)

    axes = ("row", "col")
    number = lambda r, c: r * COLS + c

    total = lambda values: functools.reduce(lambda x, y: x + y, values)

    total = lambda values: functools.reduce(lambda x, y: x + y, values)

    pieces = cut_strip(parent_front)
    own = total([jnp.where(col_index == 0, pieces[0], 0.0)] + [
        lax.ppermute(pieces[i], axes, [(number(r, 0), number(r, i)) for r in range(ROWS)])
        for i in range(1, NLEAD)
    ])
    pairs = [(number(j % 16, j // 16), number(j // 8, j % 8)) for j in range(128)]
    strip_parent = lax.ppermute(own, axes, [(b, a) for a, b in pairs])

    early = pack_early(jnp.concatenate([send_cols, send_rows[:1]]), children)
    early = lax.all_to_all(early, "col", split_axis=0, concat_axis=0, tiled=True)
    early = pick_early(pick_owner, early, [])
    early = lax.all_to_all(early, "row", split_axis=0, concat_axis=0, tiled=True)
    strip = assemble_strip(strip_place, strip_keep, strip_parent, early, [])

    first = pack_first(send_cols[0::2], children, [])
    first = lax.all_to_all(first, "col", split_axis=0, concat_axis=0, tiled=True)

    row_raw = lax.ppermute(strip, axes, pairs)

    half = BLOCK // 2
    piece = total([
        lax.ppermute(
            strip[part * half : (part + 1) * half],
            axes,
            [(number(j, 0), number(2 * j + part, 0)) for j in range(NLEAD)],
        )
        for part in range(2)
    ])
    piece = hand_on(piece, [row_raw])
    piece = total([piece] + [
        lax.ppermute(piece, axes, [(number(r, 0), number(r, d)) for r in range(ROWS)])
        for d in range(1, COLS)
    ])
    lead = lax.all_gather(piece, "row", axis=0, tiled=True)

    col_strip = lax.all_gather(strip, "row", axis=0, tiled=True)

    sends = sends.astype(jnp.int32)
    work = factor_part(0, lead, strip)
    near_out = pack_rows(send_rows, sends, pick_cols[:HALF], first, [], [])
    near = lax.all_to_all(near_out, "row", split_axis=0, concat_axis=0, tiled=True)
    shifts = (col_index + jnp.arange(COLS, dtype=jnp.int32)) % COLS
    parts = pack_second(jnp.take(send_cols, shifts * 2 + 1), children, [near_out])
    second = [parts[0]] + [
        lax.ppermute(parts[d], "col", [(c, (c + d) % COLS) for c in range(COLS)])
        for d in range(1, COLS)
    ]
    work = factor_part(1, work, near_out)
    far_out = pack_rows(send_rows, sends, pick_cols[HALF:], first, second, [near, work])
    far = lax.all_to_all(far_out, "row", split_axis=0, concat_axis=0, tiled=True)
    work = factor_part(2, work, far_out)
    inv_hi, inv_lo = factor_part(3, work, col_strip)
    row_piece = hand_on(row_raw, [near_out])
    row_strip = lax.all_gather(row_piece, "col", axis=0, tiled=True)
    flags = jnp.stack([row_index, col_index]).astype(jnp.int32)
    front = update_front(flags, row_strip, col_strip, inv_hi, inv_lo, parent_front)
    return place_children(source, col_rank, keep, front, near, far)


def solution(mesh):
    in_specs = (P("row", "col"), P("row", "col"), P(), P())
    out_specs = P("row", "col")
    return jax.shard_map(body, mesh=mesh, in_specs=in_specs, out_specs=out_specs, check_vma=False)
```

```python
import functools

import jax
import jax.numpy as jnp
from jax import lax
from jax.experimental import pallas as pl
from jax.experimental.pallas import tpu as pltpu
from jax.sharding import PartitionSpec as P

BLOCK = 128
LEAD = 1024
NLEAD = LEAD // BLOCK
GRP = 10
ROWS = 16
COLS = 8
VMEM = 56 * 1024 * 1024
F32 = jnp.float32
BF16 = jnp.bfloat16


def params(**kw):
    return pltpu.CompilerParams(vmem_limit_bytes=VMEM, **kw)


def cost(flops, bytes_accessed):
    return pl.CostEstimate(flops=flops, bytes_accessed=bytes_accessed, transcendentals=0)


def gather_call(kernel, tables, arrays, shapes, scratch, sems, name, after=()):
    moved = sum(4 * functools.reduce(lambda x, y: x * y, shape) for shape in shapes)
    count = len(tables) + len(arrays)

    def run(*refs):
        kernel(*refs[:count], *refs[count + len(after) :])

    return pl.pallas_call(
        run,
        in_specs=[pl.BlockSpec(memory_space=pltpu.SMEM)] * len(tables)
        + [pl.BlockSpec(memory_space=pl.ANY)] * (len(arrays) + len(after)),
        out_specs=[pl.BlockSpec(memory_space=pl.ANY)] * len(shapes),
        out_shape=[jax.ShapeDtypeStruct(shape, F32) for shape in shapes],
        scratch_shapes=[pltpu.VMEM(shape, F32) for shape in scratch]
        + [pltpu.SemaphoreType.DMA(sems), pltpu.SemaphoreType.DMA(sems)],
        compiler_params=params(),
        cost_estimate=cost(0, 2 * moved),
        name=name,
    )(*tables, *arrays, *after)


def lanes_of(block):
    return pl.ds(pl.multiple_of(block * BLOCK, BLOCK), BLOCK)


def relay(moves, sem_in, sem_out):
    first = [pltpu.make_async_copy(s, v, sem_in.at[n]) for n, (s, v, t) in enumerate(moves)]
    second = [pltpu.make_async_copy(v, t, sem_out.at[n]) for n, (s, v, t) in enumerate(moves)]
    for copy in first:
        copy.start()
    for one, other in zip(first, second):
        one.wait()
        other.start()
    for copy in second:
        copy.wait()


def pack_early_kernel(table, children, out, held, sem_in, sem_out):
    moves = []
    for s in range(2 * COLS):
        source = children.at[lanes_of(table[2 * COLS]), lanes_of(table[s])]
        moves.append((source, held.at[s], out.at[s]))
    relay(moves, sem_in, sem_out)


def pack_early(table, children):
    shape = (2 * COLS, BLOCK, BLOCK)
    return gather_call(
        pack_early_kernel, [table], [children], [shape], [shape], (2 * COLS,), "pack_early"
    )[0]


def pack_first_kernel(table, children, out, held, sem_in, sem_out):
    moves = [
        (children.at[:, lanes_of(table[s])], held.at[s], out.at[s]) for s in range(COLS)
    ]
    relay(moves, sem_in, sem_out)


def pack_first(table, children, after):
    shape = (COLS, children.shape[0], BLOCK)
    return gather_call(
        pack_first_kernel, [table], [children], [shape], [shape], (COLS,), "pack_first", after
    )[0]


def pack_second_kernel(table, children, *refs):
    wide, sem_in, sem_out = refs[COLS:]
    moves = [
        (children.at[:, lanes_of(table[s])], wide.at[s], refs[s]) for s in range(COLS)
    ]
    relay(moves, sem_in, sem_out)


def pack_second(table, children, after):
    wide = (children.shape[0], BLOCK)
    return gather_call(
        pack_second_kernel,
        [table],
        [children],
        [wide] * COLS,
        [(COLS,) + wide],
        (COLS,),
        "pack_second",
        after,
    )


def cut_kernel(parent, *refs):
    held, sem_in, sem_out = refs[NLEAD:]
    moves = []
    for i in range(NLEAD):
        source = parent.at[pl.ds(i * BLOCK, BLOCK), pl.ds(0, LEAD)]
        moves.append((source, held.at[i], refs[i]))
    relay(moves, sem_in, sem_out)


def cut_strip(parent):
    shape = (BLOCK, LEAD)
    return gather_call(
        cut_kernel, [], [parent], [shape] * NLEAD, [(NLEAD,) + shape], (NLEAD,), "cut_strip"
    )


def pick_early_kernel(table, blocks, out, held, sem_in, sem_out):
    relay([(blocks.at[table[s]], held.at[s], out.at[s]) for s in range(ROWS)], sem_in, sem_out)


def pick_early(table, blocks, after):
    shape = (ROWS, BLOCK, BLOCK)
    return gather_call(
        pick_early_kernel, [table], [blocks], [shape], [shape], (ROWS,), "pick_early", after
    )[0]


HALF = GRP // 2


def pack_rows_kernel(row_table, row_has, origin, first, *refs):
    second, (out, held, sem_in, sem_out) = refs[:-4], refs[-4:]

    def each(act):
        def one(r, carry):
            @pl.when(row_has[r] != 0)
            def _():
                act(r)

            return carry

        lax.fori_loop(0, ROWS, one, 0)

    def start(r):
        for k in range(HALF):
            target = (held.at[r, k], sem_in.at[r, k])

            @pl.when(origin[k] < COLS)
            def _():
                pltpu.make_async_copy(first.at[origin[k], row_table[r]], *target).start()

            for n, source in enumerate(second):

                @pl.when(origin[k] == COLS + n)
                def _():
                    pltpu.make_async_copy(source.at[row_table[r]], *target).start()

    def leave(r):
        return pltpu.make_async_copy(held.at[r], out.at[r], sem_out.at[r, 0])

    def send(r):
        for k in range(HALF):
            pltpu.make_async_copy(first.at[0, 0], held.at[r, k], sem_in.at[r, k]).wait()
        leave(r).start()

    each(start)
    each(send)
    each(lambda r: leave(r).wait())


def pack_rows(row_table, row_has, origin, first, second, after):
    first = first.reshape(COLS, GRP, BLOCK, BLOCK)
    second = [x.reshape(GRP, BLOCK, BLOCK) for x in second]
    shape = (ROWS, HALF, BLOCK, BLOCK)
    return gather_call(
        pack_rows_kernel,
        [row_table, row_has, origin],
        [first] + second,
        [shape],
        [shape],
        (ROWS, HALF),
        "pack_rows",
        after,
    )[0]


def strip_kernel(place, keep, parent, blocks, *refs):
    out = refs[-1]
    out[...] = parent[...]
    for s in range(ROWS):

        @pl.when(keep[s] != 0)
        def _():
            at = lanes_of(place[s])
            out[:, at] = out[:, at] + blocks[s].T


def assemble_strip(place, keep, parent, blocks, after):
    vmem = pl.BlockSpec(memory_space=pltpu.VMEM)
    smem = pl.BlockSpec(memory_space=pltpu.SMEM)
    return pl.pallas_call(
        strip_kernel,
        in_specs=[smem, smem, vmem, vmem] + [pl.BlockSpec(memory_space=pl.ANY)] * len(after),
        out_specs=vmem,
        out_shape=jax.ShapeDtypeStruct((BLOCK, LEAD), F32),
        compiler_params=params(),
        cost_estimate=cost(0, 2 << 20),
        name="assemble_strip",
    )(place, keep, parent, blocks, *after)


def hand_on_kernel(given, *refs):
    refs[-1][...] = given[...]


def hand_on(given, after):
    vmem = pl.BlockSpec(memory_space=pltpu.VMEM)
    return pl.pallas_call(
        hand_on_kernel,
        in_specs=[vmem] + [pl.BlockSpec(memory_space=pl.ANY)] * len(after),
        out_specs=vmem,
        out_shape=jax.ShapeDtypeStruct(given.shape, F32),
        compiler_params=params(),
        cost_estimate=cost(0, 1 << 20),
        name="hand_on",
    )(given, *after)


def split(x):
    hi = x.astype(BF16)
    return hi, (x - hi.astype(F32)).astype(BF16)


def dot3(a_hi, a_lo, b_hi, b_lo):
    dims = (((1,), (1,)), ((), ()))
    total = lax.dot_general(a_hi, b_lo, dims, preferred_element_type=F32)
    total += lax.dot_general(a_lo, b_hi, dims, preferred_element_type=F32)
    return total + lax.dot_general(a_hi, b_hi, dims, preferred_element_type=F32)


def dot_full(a, b, dims):
    return lax.dot_general(
        a, b, (dims, ((), ())), precision=lax.Precision.HIGHEST, preferred_element_type=F32
    )


def invert_diagonal(work):
    lanes = lax.broadcasted_iota(jnp.int32, (BLOCK, BLOCK), 1)
    rows = lax.broadcasted_iota(jnp.int32, (BLOCK, BLOCK), 0)
    here, below, rest = work[0:8], work[8:16], work[16:]
    done = []
    for t in range(BLOCK // 8):
        base = 8 * t
        last = t == BLOCK // 8 - 1
        part = here if last else jnp.concatenate([here, below], axis=0)
        shape = part.shape
        lane = lanes[: shape[0]]
        row_id = rows[: shape[0]]
        cols = [jnp.broadcast_to(part[:, base + i : base + i + 1], shape) for i in range(8)]
        scale = jnp.zeros((8, BLOCK), F32)
        for i in range(8):
            root = lax.rsqrt(cols[i][i : i + 1])
            scale = jnp.where(row_id[:8] == i, root, scale)
            factor = jnp.where(row_id > i, cols[i] * (root * root), 0.0)
            for other in range(i + 1, 8):
                cols[other] = cols[other] - factor * cols[other][i : i + 1]
            row = jnp.where(lane[:1] == base + i, 1.0, part[i : i + 1])
            part = jnp.where(lane == base + i, jnp.where(row_id == i, 1.0, jnp.where(row_id > i, 0.0, part)), part)
            part = part - factor * row
        here = part[:8] * scale
        done.append(here)
        if t < BLOCK // 8 - 2:
            above = (lane[:8] > base + row_id[:8]) & (lane[:8] < base + 8)
            update = dot_full(here[:, base + 16 :], jnp.where(above, 0.0, here), ((0,), (0,)))
            inside = (lanes[: rest.shape[0]] >= base) & (lanes[: rest.shape[0]] < base + 8)
            rest = jnp.where(inside, 0.0, rest) - update
        if not last:
            here = part[8:]
            below, rest = rest[:8], rest[8:]
    whole = jnp.concatenate(done, axis=0)
    return jnp.where(rows >= lanes, whole, 0.0)


def factor_kernel(first, count, last, *refs):
    given, _, *refs = refs
    work = refs[-1] if last else refs[0]
    work[...] = given[...]
    total = LEAD // BLOCK

    def step(k, carry):
        here = lanes_of(k)
        inverse = invert_diagonal(work[here, here])
        work[here, :] = dot_full(inverse, work[here, :], ((1,), (0,)))
        work[here, here] = inverse

        def below(i, carry):
            there = lanes_of(i)
            lower = work[here, there]
            work[there, here] = jnp.zeros((BLOCK, BLOCK), F32)
            work[there, :] = work[there, :] - dot_full(lower, work[here, :], ((0,), (0,)))
            return carry

        return lax.fori_loop(k + 1, total, below, carry)

    lax.fori_loop(first, first + count, step, 0)
    if not last:
        return
    inv_hi, inv_lo = refs[0], refs[1]

    def finish(k, carry):
        here = lanes_of(k)
        rows = lax.broadcasted_iota(jnp.int32, (BLOCK, LEAD), 0) + k * BLOCK
        lanes = lax.broadcasted_iota(jnp.int32, (BLOCK, LEAD), 1)
        hi, lo = split(jnp.where(rows >= lanes, work[here, :], 0.0))
        inv_hi[here, :] = hi
        inv_lo[here, :] = lo
        return carry

    lax.fori_loop(0, total, finish, 0)


PARTS = 4


def factor_part(part, given, after):
    count = LEAD // BLOCK // PARTS
    whole = pl.BlockSpec(memory_space=pltpu.VMEM)
    last = part == PARTS - 1
    half = jax.ShapeDtypeStruct((LEAD, LEAD), BF16)
    full = jax.ShapeDtypeStruct((LEAD, LEAD), F32)
    return pl.pallas_call(
        functools.partial(factor_kernel, part * count, count, last),
        in_specs=[whole, pl.BlockSpec(memory_space=pl.ANY)],
        out_specs=[whole] * 2 if last else whole,
        out_shape=(half, half) if last else full,
        scratch_shapes=[pltpu.VMEM((LEAD, LEAD), F32)] if last else [],
        compiler_params=params(),
        cost_estimate=cost(25 * 10**9, 8 << 20),
        name="factor_lead",
    )(given, after)


TILE = 512
CHUNK = 1024


def solve_rows(rows, inv_hi, inv_lo):
    hi, lo = split(rows)
    parts = []
    for n in range(LEAD // 256):
        at, upto = pl.ds(n * 256, 256), (n + 1) * 256
        parts.append(
            dot3(hi[:, :upto], lo[:, :upto], inv_hi[at, pl.ds(0, upto)], inv_lo[at, pl.ds(0, upto)])
        )
    return jnp.concatenate(parts, axis=1)


def update_kernel(flags, row_strip, col_strip, inv_hi, inv_lo, parent, out, panel, hi, lo):
    step = pl.program_id(0)

    @pl.when(step == 0)
    def _():
        def chunk(n, carry):
            at = pl.ds(pl.multiple_of(n * CHUNK, CHUNK), CHUNK)
            values = solve_rows(row_strip[at, :], inv_hi, inv_lo)
            panel[at, :] = values
            hi[at, :], lo[at, :] = split(values)
            return carry

        lax.fori_loop(0, LEAD // CHUNK, chunk, 0)

    in_panel = (flags[1] == 0) & (step < LEAD // TILE)
    top = flags[0] == 0

    @pl.when(in_panel)
    def _():
        at = pl.ds(pl.multiple_of(step * TILE, TILE), TILE)
        rows = lax.broadcasted_iota(jnp.int32, (LEAD, TILE), 0)
        lanes = lax.broadcasted_iota(jnp.int32, (LEAD, TILE), 1) + step * TILE
        out[...] = jnp.where((rows >= lanes) | jnp.logical_not(top), panel[:, at], 0.0)

    @pl.when(jnp.logical_not(in_panel) & top)
    def _():
        out[...] = jnp.zeros_like(out)

    @pl.when(jnp.logical_not(in_panel) & jnp.logical_not(top))
    def _():
        right = split(solve_rows(col_strip[...], inv_hi, inv_lo))

        def chunk(n, carry):
            at = pl.ds(pl.multiple_of(n * CHUNK, CHUNK), CHUNK)
            out[at, :] = parent[at, :] - dot3(hi[at, :], lo[at, :], *right)
            return carry

        lax.fori_loop(0, LEAD // CHUNK, chunk, 0)


def update_front(flags, row_strip, col_strip, inv_hi, inv_lo, parent):
    rows, columns = parent.shape
    whole = lambda t, f: (0, 0)
    return pl.pallas_call(
        update_kernel,
        grid_spec=pltpu.PrefetchScalarGridSpec(
            num_scalar_prefetch=1,
            grid=(columns // TILE,),
            in_specs=[
                pl.BlockSpec((LEAD, LEAD), whole),
                pl.BlockSpec((TILE, LEAD), lambda t, f: (t, 0)),
                pl.BlockSpec((LEAD, LEAD), whole),
                pl.BlockSpec((LEAD, LEAD), whole),
                pl.BlockSpec((rows, TILE), lambda t, f: (0, t)),
            ],
            out_specs=pl.BlockSpec((rows, TILE), lambda t, f: (0, t)),
            scratch_shapes=[
                pltpu.VMEM((LEAD, LEAD), F32),
                pltpu.VMEM((LEAD, LEAD), BF16),
                pltpu.VMEM((LEAD, LEAD), BF16),
            ],
        ),
        out_shape=jax.ShapeDtypeStruct((rows, columns), F32),
        compiler_params=params(),
        cost_estimate=cost(40 * 10**9, 32 << 20),
        name="update_front",
    )(flags, row_strip, col_strip, inv_hi, inv_lo, parent)


def place_kernel(source, rank, keep, front, *refs):
    out = refs[-1]
    i = pl.program_id(0)
    for j in range(16):
        at = pl.ds(j * BLOCK, BLOCK)
        value = front[:, at]
        for h in range(2):
            k = rank[h, j]
            near, far = refs[2 * h], refs[2 * h + 1]
            block = jnp.where(
                k < HALF, near[0, jnp.minimum(k, HALF - 1)], far[0, jnp.maximum(k - HALF, 0)]
            )
            value = value + jnp.where(keep[h, i * 16 + j] != 0, block, 0.0)
        out[:, at] = value


def place_children(source, rank, keep, front, near, far):
    rows, columns = front.shape

    def spec(h):
        return pl.BlockSpec((1, HALF, BLOCK, BLOCK), lambda i, s, r, k: (s[h, i], 0, 0, 0))

    return pl.pallas_call(
        place_kernel,
        grid_spec=pltpu.PrefetchScalarGridSpec(
            num_scalar_prefetch=3,
            grid=(rows // BLOCK,),
            in_specs=[pl.BlockSpec((BLOCK, columns), lambda i, s, r, k: (i, 0))]
            + [spec(0), spec(0), spec(1), spec(1)],
            out_specs=pl.BlockSpec((BLOCK, columns), lambda i, s, r, k: (i, 0)),
        ),
        out_shape=jax.ShapeDtypeStruct((rows, columns), F32),
        input_output_aliases={3: 0},
        compiler_params=params(),
        cost_estimate=cost(0, 24 << 20),
        name="place_children",
    )(source, rank, keep, front, near, far, near, far)


def earlier_count(keys):
    places = jnp.arange(keys.shape[-1], dtype=jnp.int32)
    matches = keys[..., :, None] == keys[..., None, :]
    before = places[None, :] < places[:, None]
    return jnp.sum((matches & before).astype(jnp.int32), axis=-1)


def lookup(codes, values, length):
    hits = codes[..., :, None] == jnp.arange(length, dtype=jnp.int32)
    found = jnp.sum(jnp.where(hits, values[..., :, None], 0), axis=-2)
    return found, jnp.any(hits, axis=-2)


def body(parent_front, children, child_map, fill):
    row_index = lax.axis_index("row")
    col_index = lax.axis_index("col")
    child_id = row_index // COLS
    group_row = row_index % COLS
    blocks = child_map.shape[1]
    places = jnp.arange(blocks, dtype=jnp.int32)
    groups = places // GRP
    within = places % GRP
    run16 = child_map // 16
    run8 = child_map // 8
    slot = earlier_count(groups * COLS + run16)
    pick = lambda x: lax.dynamic_index_in_dim(x, child_id, 0, keepdims=False)
    own_map, own_run16, own_run8, own_slot = pick(child_map), pick(run16), pick(run8), pick(slot)

    col_codes = jnp.where(groups == col_index, own_run16 * 2 + own_slot, -1)
    send_cols, _ = lookup(col_codes, within, 2 * COLS)
    row_codes = jnp.where(groups == group_row, own_run8, -1)
    send_rows, sends = lookup(row_codes, within, ROWS)
    ahead = slot[:, None, :] * blocks + places < (slot * blocks + places)[:, :, None]
    rank_all = jnp.sum((ahead & (run16[:, None, :] == run16[:, :, None])).astype(jnp.int32), axis=-1)
    rank_codes = jnp.where(own_run16 == col_index, pick(rank_all), -1)
    origin = jnp.where(own_slot == 0, groups, COLS + (col_index - groups) % COLS)
    pick_cols, _ = lookup(rank_codes, origin, GRP)
    own_codes = jnp.where(own_run16 == col_index, own_map % 16, -1)
    pick_owner, _ = lookup(own_codes, groups * 2 + own_slot, 16)

    tile_rows = jnp.where(run8 == row_index, child_map % 8, -1)
    row_block, row_has = lookup(tile_rows, jnp.broadcast_to(places, (2, blocks)), 8)
    tile_cols = jnp.where(run16 == col_index, child_map % 16, -1)
    col_rank, col_has = lookup(tile_cols, rank_all, 16)
    row_hit = (tile_rows[:, None, :] == jnp.arange(8, dtype=jnp.int32)[None, :, None]).astype(F32)
    col_hit = (tile_cols[:, None, :] == jnp.arange(16, dtype=jnp.int32)[None, :, None]).astype(F32)
    present = fill.astype(F32)
    keep = jnp.einsum("hia,hab->hib", row_hit, present)
    keep = jnp.einsum("hib,hjb->hij", keep, col_hit)
    panel_col = (col_index == 0) & (jnp.arange(16) < NLEAD)
    keep = jnp.where(panel_col | (row_index == 0), 0.0, keep)
    keep = (keep > 0.5).astype(jnp.int32).reshape(2, 8 * 16)
    source = jnp.arange(2, dtype=jnp.int32)[:, None] * COLS + row_block // GRP

    owned = col_index * 16 + row_index
    lead_codes = jnp.where(run8 == 0, groups, -1)
    strip_place, strip_has = lookup(lead_codes, child_map, COLS)
    lead_hit = (lead_codes[:, None, :] == jnp.arange(COLS, dtype=jnp.int32)[None, :, None]).astype(F32)
    owned_hit = (child_map == owned).astype(F32)
    strip_keep = jnp.einsum("hga,hab->hgb", lead_hit, present)
    strip_keep = jnp.sum(strip_keep * owned_hit[:, None, :], axis=-1)
    strip_keep = (strip_keep > 0.5).astype(jnp.int32).reshape(ROWS)
    strip_place = jnp.where(strip_has, strip_place, 0).reshape(ROWS)

    axes = ("row", "col")
    number = lambda r, c: r * COLS + c

    total = lambda values: functools.reduce(lambda x, y: x + y, values)

    total = lambda values: functools.reduce(lambda x, y: x + y, values)

    pieces = cut_strip(parent_front)
    own = total([jnp.where(col_index == 0, pieces[0], 0.0)] + [
        lax.ppermute(pieces[i], axes, [(number(r, 0), number(r, i)) for r in range(ROWS)])
        for i in range(1, NLEAD)
    ])
    pairs = [(number(j % 16, j // 16), number(j // 8, j % 8)) for j in range(128)]
    strip_parent = lax.ppermute(own, axes, [(b, a) for a, b in pairs])

    early = pack_early(jnp.concatenate([send_cols, send_rows[:1]]), children)
    early = lax.all_to_all(early, "col", split_axis=0, concat_axis=0, tiled=True)
    early = pick_early(pick_owner, early, [])
    early = lax.all_to_all(early, "row", split_axis=0, concat_axis=0, tiled=True)
    strip = assemble_strip(strip_place, strip_keep, strip_parent, early, [])

    col_strip = lax.all_gather(strip, "row", axis=0, tiled=True)

    row_raw = lax.ppermute(strip, axes, pairs)

    half = BLOCK // 2
    piece = total([
        lax.ppermute(
            strip[part * half : (part + 1) * half],
            axes,
            [(number(j, 0), number(2 * j + part, 0)) for j in range(NLEAD)],
        )
        for part in range(2)
    ])
    piece = hand_on(piece, [row_raw])
    piece = total([piece] + [
        lax.ppermute(piece, axes, [(number(r, 0), number(r, d)) for r in range(ROWS)])
        for d in range(1, COLS)
    ])
    lead = lax.all_gather(piece, "row", axis=0, tiled=True)

    first = pack_first(send_cols[0::2], children, [piece])
    first = lax.all_to_all(first, "col", split_axis=0, concat_axis=0, tiled=True)


    sends = sends.astype(jnp.int32)
    near_out = pack_rows(send_rows, sends, pick_cols[:HALF], first, [], [col_strip])
    near = lax.all_to_all(near_out, "row", split_axis=0, concat_axis=0, tiled=True)
    shifts = (col_index + jnp.arange(COLS, dtype=jnp.int32)) % COLS
    parts = pack_second(jnp.take(send_cols, shifts * 2 + 1), children, [near_out])
    second = [parts[0]] + [
        lax.ppermute(parts[d], "col", [(c, (c + d) % COLS) for c in range(COLS)])
        for d in range(1, COLS)
    ]
    work = factor_part(0, lead, second[1])
    work = factor_part(1, work, near_out)
    far_out = pack_rows(send_rows, sends, pick_cols[HALF:], first, second, [near, work])
    far = lax.all_to_all(far_out, "row", split_axis=0, concat_axis=0, tiled=True)
    work = factor_part(2, work, far_out)
    inv_hi, inv_lo = factor_part(3, work, far_out)
    row_piece = hand_on(row_raw, [near_out])
    row_strip = lax.all_gather(row_piece, "col", axis=0, tiled=True)
    flags = jnp.stack([row_index, col_index]).astype(jnp.int32)
    front = update_front(flags, row_strip, col_strip, inv_hi, inv_lo, parent_front)
    return place_children(source, col_rank, keep, front, near, far)


def solution(mesh):
    in_specs = (P("row", "col"), P("row", "col"), P(), P())
    out_specs = P("row", "col")
    return jax.shard_map(body, mesh=mesh, in_specs=in_specs, out_specs=out_specs, check_vma=False)
```

```python
import functools

import jax
import jax.numpy as jnp
from jax import lax
from jax.experimental import pallas as pl
from jax.experimental.pallas import tpu as pltpu
from jax.sharding import PartitionSpec as P

BLOCK = 128
LEAD = 1024
NLEAD = LEAD // BLOCK
GRP = 10
ROWS = 16
COLS = 8
VMEM = 56 * 1024 * 1024
F32 = jnp.float32
BF16 = jnp.bfloat16


def params(**kw):
    return pltpu.CompilerParams(vmem_limit_bytes=VMEM, **kw)


def cost(flops, bytes_accessed):
    return pl.CostEstimate(flops=flops, bytes_accessed=bytes_accessed, transcendentals=0)


def gather_call(kernel, tables, arrays, shapes, scratch, sems, name, after=()):
    moved = sum(4 * functools.reduce(lambda x, y: x * y, shape) for shape in shapes)
    count = len(tables) + len(arrays)

    def run(*refs):
        kernel(*refs[:count], *refs[count + len(after) :])

    return pl.pallas_call(
        run,
        in_specs=[pl.BlockSpec(memory_space=pltpu.SMEM)] * len(tables)
        + [pl.BlockSpec(memory_space=pl.ANY)] * (len(arrays) + len(after)),
        out_specs=[pl.BlockSpec(memory_space=pl.ANY)] * len(shapes),
        out_shape=[jax.ShapeDtypeStruct(shape, F32) for shape in shapes],
        scratch_shapes=[pltpu.VMEM(shape, F32) for shape in scratch]
        + [pltpu.SemaphoreType.DMA(sems), pltpu.SemaphoreType.DMA(sems)],
        compiler_params=params(),
        cost_estimate=cost(0, 2 * moved),
        name=name,
    )(*tables, *arrays, *after)


def lanes_of(block):
    return pl.ds(pl.multiple_of(block * BLOCK, BLOCK), BLOCK)


def relay(moves, sem_in, sem_out):
    first = [pltpu.make_async_copy(s, v, sem_in.at[n]) for n, (s, v, t) in enumerate(moves)]
    second = [pltpu.make_async_copy(v, t, sem_out.at[n]) for n, (s, v, t) in enumerate(moves)]
    for copy in first:
        copy.start()
    for one, other in zip(first, second):
        one.wait()
        other.start()
    for copy in second:
        copy.wait()


def pack_early_kernel(table, children, out, held, sem_in, sem_out):
    moves = []
    for s in range(2 * COLS):
        source = children.at[lanes_of(table[2 * COLS]), lanes_of(table[s])]
        moves.append((source, held.at[s], out.at[s]))
    relay(moves, sem_in, sem_out)


def pack_early(table, children):
    shape = (2 * COLS, BLOCK, BLOCK)
    return gather_call(
        pack_early_kernel, [table], [children], [shape], [shape], (2 * COLS,), "pack_early"
    )[0]


def pack_first_kernel(table, children, out, held, sem_in, sem_out):
    moves = [
        (children.at[:, lanes_of(table[s])], held.at[s], out.at[s]) for s in range(COLS)
    ]
    relay(moves, sem_in, sem_out)


def pack_first(table, children, after):
    shape = (COLS, children.shape[0], BLOCK)
    return gather_call(
        pack_first_kernel, [table], [children], [shape], [shape], (COLS,), "pack_first", after
    )[0]


def pack_second_kernel(table, children, *refs):
    wide, sem_in, sem_out = refs[COLS:]
    moves = [
        (children.at[:, lanes_of(table[s])], wide.at[s], refs[s]) for s in range(COLS)
    ]
    relay(moves, sem_in, sem_out)


def pack_second(table, children, after):
    wide = (children.shape[0], BLOCK)
    return gather_call(
        pack_second_kernel,
        [table],
        [children],
        [wide] * COLS,
        [(COLS,) + wide],
        (COLS,),
        "pack_second",
        after,
    )


def cut_kernel(parent, *refs):
    held, sem_in, sem_out = refs[NLEAD:]
    moves = []
    for i in range(NLEAD):
        source = parent.at[pl.ds(i * BLOCK, BLOCK), pl.ds(0, LEAD)]
        moves.append((source, held.at[i], refs[i]))
    relay(moves, sem_in, sem_out)


def cut_strip(parent):
    shape = (BLOCK, LEAD)
    return gather_call(
        cut_kernel, [], [parent], [shape] * NLEAD, [(NLEAD,) + shape], (NLEAD,), "cut_strip"
    )


def pick_early_kernel(table, blocks, out, held, sem_in, sem_out):
    relay([(blocks.at[table[s]], held.at[s], out.at[s]) for s in range(ROWS)], sem_in, sem_out)


def pick_early(table, blocks, after):
    shape = (ROWS, BLOCK, BLOCK)
    return gather_call(
        pick_early_kernel, [table], [blocks], [shape], [shape], (ROWS,), "pick_early", after
    )[0]


HALF = GRP // 2


def pack_rows_kernel(row_table, row_has, origin, first, *refs):
    second, (out, held, sem_in, sem_out) = refs[:-4], refs[-4:]

    def each(act):
        def one(r, carry):
            @pl.when(row_has[r] != 0)
            def _():
                act(r)

            return carry

        lax.fori_loop(0, ROWS, one, 0)

    def start(r):
        for k in range(HALF):
            target = (held.at[r, k], sem_in.at[r, k])

            @pl.when(origin[k] < COLS)
            def _():
                pltpu.make_async_copy(first.at[origin[k], row_table[r]], *target).start()

            for n, source in enumerate(second):

                @pl.when(origin[k] == COLS + n)
                def _():
                    pltpu.make_async_copy(source.at[row_table[r]], *target).start()

    def leave(r):
        return pltpu.make_async_copy(held.at[r], out.at[r], sem_out.at[r, 0])

    def send(r):
        for k in range(HALF):
            pltpu.make_async_copy(first.at[0, 0], held.at[r, k], sem_in.at[r, k]).wait()
        leave(r).start()

    each(start)
    each(send)
    each(lambda r: leave(r).wait())


def pack_rows(row_table, row_has, origin, first, second, after):
    first = first.reshape(COLS, GRP, BLOCK, BLOCK)
    second = [x.reshape(GRP, BLOCK, BLOCK) for x in second]
    shape = (ROWS, HALF, BLOCK, BLOCK)
    return gather_call(
        pack_rows_kernel,
        [row_table, row_has, origin],
        [first] + second,
        [shape],
        [shape],
        (ROWS, HALF),
        "pack_rows",
        after,
    )[0]


def strip_kernel(place, keep, parent, blocks, *refs):
    out = refs[-1]
    out[...] = parent[...]
    for s in range(ROWS):

        @pl.when(keep[s] != 0)
        def _():
            at = lanes_of(place[s])
            out[:, at] = out[:, at] + blocks[s].T


def assemble_strip(place, keep, parent, blocks, after):
    vmem = pl.BlockSpec(memory_space=pltpu.VMEM)
    smem = pl.BlockSpec(memory_space=pltpu.SMEM)
    return pl.pallas_call(
        strip_kernel,
        in_specs=[smem, smem, vmem, vmem] + [pl.BlockSpec(memory_space=pl.ANY)] * len(after),
        out_specs=vmem,
        out_shape=jax.ShapeDtypeStruct((BLOCK, LEAD), F32),
        compiler_params=params(),
        cost_estimate=cost(0, 2 << 20),
        name="assemble_strip",
    )(place, keep, parent, blocks, *after)


def hand_on_kernel(given, *refs):
    refs[-1][...] = given[...]


def hand_on(given, after):
    vmem = pl.BlockSpec(memory_space=pltpu.VMEM)
    return pl.pallas_call(
        hand_on_kernel,
        in_specs=[vmem] + [pl.BlockSpec(memory_space=pl.ANY)] * len(after),
        out_specs=vmem,
        out_shape=jax.ShapeDtypeStruct(given.shape, F32),
        compiler_params=params(),
        cost_estimate=cost(0, 1 << 20),
        name="hand_on",
    )(given, *after)


def pass_on(given, after):
    place = pl.BlockSpec(memory_space=pl.ANY)
    return pl.pallas_call(
        lambda *refs: None,
        in_specs=[place] * (1 + len(after)),
        out_specs=place,
        out_shape=jax.ShapeDtypeStruct(given.shape, F32),
        input_output_aliases={0: 0},
        compiler_params=params(),
        name="pass_on",
    )(given, *after)


def split(x):
    hi = x.astype(BF16)
    return hi, (x - hi.astype(F32)).astype(BF16)


def dot3(a_hi, a_lo, b_hi, b_lo):
    dims = (((1,), (1,)), ((), ()))
    total = lax.dot_general(a_hi, b_lo, dims, preferred_element_type=F32)
    total += lax.dot_general(a_lo, b_hi, dims, preferred_element_type=F32)
    return total + lax.dot_general(a_hi, b_hi, dims, preferred_element_type=F32)


def dot_full(a, b, dims):
    return lax.dot_general(
        a, b, (dims, ((), ())), precision=lax.Precision.HIGHEST, preferred_element_type=F32
    )


def invert_diagonal(work):
    lanes = lax.broadcasted_iota(jnp.int32, (BLOCK, BLOCK), 1)
    rows = lax.broadcasted_iota(jnp.int32, (BLOCK, BLOCK), 0)
    here, below, rest = work[0:8], work[8:16], work[16:]
    done = []
    for t in range(BLOCK // 8):
        base = 8 * t
        last = t == BLOCK // 8 - 1
        part = here if last else jnp.concatenate([here, below], axis=0)
        shape = part.shape
        lane = lanes[: shape[0]]
        row_id = rows[: shape[0]]
        cols = [jnp.broadcast_to(part[:, base + i : base + i + 1], shape) for i in range(8)]
        scale = jnp.zeros((8, BLOCK), F32)
        for i in range(8):
            root = lax.rsqrt(cols[i][i : i + 1])
            scale = jnp.where(row_id[:8] == i, root, scale)
            factor = jnp.where(row_id > i, cols[i] * (root * root), 0.0)
            for other in range(i + 1, 8):
                cols[other] = cols[other] - factor * cols[other][i : i + 1]
            row = jnp.where(lane[:1] == base + i, 1.0, part[i : i + 1])
            part = jnp.where(lane == base + i, jnp.where(row_id == i, 1.0, jnp.where(row_id > i, 0.0, part)), part)
            part = part - factor * row
        here = part[:8] * scale
        done.append(here)
        if t < BLOCK // 8 - 2:
            above = (lane[:8] > base + row_id[:8]) & (lane[:8] < base + 8)
            update = dot_full(here[:, base + 16 :], jnp.where(above, 0.0, here), ((0,), (0,)))
            inside = (lanes[: rest.shape[0]] >= base) & (lanes[: rest.shape[0]] < base + 8)
            rest = jnp.where(inside, 0.0, rest) - update
        if not last:
            here = part[8:]
            below, rest = rest[:8], rest[8:]
    whole = jnp.concatenate(done, axis=0)
    return jnp.where(rows >= lanes, whole, 0.0)


def factor_kernel(first, count, last, *refs):
    given, _, *refs = refs
    work = refs[-1] if last else refs[0]
    work[...] = given[...]
    total = LEAD // BLOCK

    def step(k, carry):
        here = lanes_of(k)
        inverse = invert_diagonal(work[here, here])
        work[here, :] = dot_full(inverse, work[here, :], ((1,), (0,)))
        work[here, here] = inverse

        def below(i, carry):
            there = lanes_of(i)
            lower = work[here, there]
            work[there, here] = jnp.zeros((BLOCK, BLOCK), F32)
            work[there, :] = work[there, :] - dot_full(lower, work[here, :], ((0,), (0,)))
            return carry

        return lax.fori_loop(k + 1, total, below, carry)

    lax.fori_loop(first, first + count, step, 0)
    if not last:
        return
    inv_hi, inv_lo = refs[0], refs[1]

    def finish(k, carry):
        here = lanes_of(k)
        rows = lax.broadcasted_iota(jnp.int32, (BLOCK, LEAD), 0) + k * BLOCK
        lanes = lax.broadcasted_iota(jnp.int32, (BLOCK, LEAD), 1)
        hi, lo = split(jnp.where(rows >= lanes, work[here, :], 0.0))
        inv_hi[here, :] = hi
        inv_lo[here, :] = lo
        return carry

    lax.fori_loop(0, total, finish, 0)


PARTS = 4


def factor_part(part, given, after):
    count = LEAD // BLOCK // PARTS
    whole = pl.BlockSpec(memory_space=pltpu.VMEM)
    last = part == PARTS - 1
    half = jax.ShapeDtypeStruct((LEAD, LEAD), BF16)
    full = jax.ShapeDtypeStruct((LEAD, LEAD), F32)
    return pl.pallas_call(
        functools.partial(factor_kernel, part * count, count, last),
        in_specs=[whole, pl.BlockSpec(memory_space=pl.ANY)],
        out_specs=[whole] * 2 if last else whole,
        out_shape=(half, half) if last else full,
        scratch_shapes=[pltpu.VMEM((LEAD, LEAD), F32)] if last else [],
        compiler_params=params(),
        cost_estimate=cost(0, 0),
        name="factor_lead",
    )(given, after)


TILE = 512
CHUNK = 1024


def solve_rows(rows, inv_hi, inv_lo):
    hi, lo = split(rows)
    parts = []
    for n in range(LEAD // 256):
        at, upto = pl.ds(n * 256, 256), (n + 1) * 256
        parts.append(
            dot3(hi[:, :upto], lo[:, :upto], inv_hi[at, pl.ds(0, upto)], inv_lo[at, pl.ds(0, upto)])
        )
    return jnp.concatenate(parts, axis=1)


def update_kernel(flags, row_strip, col_strip, inv_hi, inv_lo, parent, out, panel, hi, lo):
    step = pl.program_id(0)

    @pl.when(step == 0)
    def _():
        def chunk(n, carry):
            at = pl.ds(pl.multiple_of(n * CHUNK, CHUNK), CHUNK)
            values = solve_rows(row_strip[at, :], inv_hi, inv_lo)
            panel[at, :] = values
            hi[at, :], lo[at, :] = split(values)
            return carry

        lax.fori_loop(0, LEAD // CHUNK, chunk, 0)

    in_panel = (flags[1] == 0) & (step < LEAD // TILE)
    top = flags[0] == 0

    @pl.when(in_panel)
    def _():
        at = pl.ds(pl.multiple_of(step * TILE, TILE), TILE)
        rows = lax.broadcasted_iota(jnp.int32, (LEAD, TILE), 0)
        lanes = lax.broadcasted_iota(jnp.int32, (LEAD, TILE), 1) + step * TILE
        out[...] = jnp.where((rows >= lanes) | jnp.logical_not(top), panel[:, at], 0.0)

    @pl.when(jnp.logical_not(in_panel) & top)
    def _():
        out[...] = jnp.zeros_like(out)

    @pl.when(jnp.logical_not(in_panel) & jnp.logical_not(top))
    def _():
        right = split(solve_rows(col_strip[...], inv_hi, inv_lo))

        def chunk(n, carry):
            at = pl.ds(pl.multiple_of(n * CHUNK, CHUNK), CHUNK)
            out[at, :] = parent[at, :] - dot3(hi[at, :], lo[at, :], *right)
            return carry

        lax.fori_loop(0, LEAD // CHUNK, chunk, 0)


def update_front(flags, row_strip, col_strip, inv_hi, inv_lo, parent):
    rows, columns = parent.shape
    whole = lambda t, f: (0, 0)
    return pl.pallas_call(
        update_kernel,
        grid_spec=pltpu.PrefetchScalarGridSpec(
            num_scalar_prefetch=1,
            grid=(columns // TILE,),
            in_specs=[
                pl.BlockSpec((LEAD, LEAD), whole),
                pl.BlockSpec((TILE, LEAD), lambda t, f: (t, 0)),
                pl.BlockSpec((LEAD, LEAD), whole),
                pl.BlockSpec((LEAD, LEAD), whole),
                pl.BlockSpec((rows, TILE), lambda t, f: (0, t)),
            ],
            out_specs=pl.BlockSpec((rows, TILE), lambda t, f: (0, t)),
            scratch_shapes=[
                pltpu.VMEM((LEAD, LEAD), F32),
                pltpu.VMEM((LEAD, LEAD), BF16),
                pltpu.VMEM((LEAD, LEAD), BF16),
            ],
        ),
        out_shape=jax.ShapeDtypeStruct((rows, columns), F32),
        compiler_params=params(),
        cost_estimate=cost(40 * 10**9, 32 << 20),
        name="update_front",
    )(flags, row_strip, col_strip, inv_hi, inv_lo, parent)


def place_kernel(source, rank, keep, front, *refs):
    out = refs[-1]
    i = pl.program_id(0)
    for j in range(16):
        at = pl.ds(j * BLOCK, BLOCK)
        value = front[:, at]
        for h in range(2):
            k = rank[h, j]
            near, far = refs[2 * h], refs[2 * h + 1]
            block = jnp.where(
                k < HALF, near[0, jnp.minimum(k, HALF - 1)], far[0, jnp.maximum(k - HALF, 0)]
            )
            value = value + jnp.where(keep[h, i * 16 + j] != 0, block, 0.0)
        out[:, at] = value


def place_children(source, rank, keep, front, near, far):
    rows, columns = front.shape

    def spec(h):
        return pl.BlockSpec((1, HALF, BLOCK, BLOCK), lambda i, s, r, k: (s[h, i], 0, 0, 0))

    return pl.pallas_call(
        place_kernel,
        grid_spec=pltpu.PrefetchScalarGridSpec(
            num_scalar_prefetch=3,
            grid=(rows // BLOCK,),
            in_specs=[pl.BlockSpec((BLOCK, columns), lambda i, s, r, k: (i, 0))]
            + [spec(0), spec(0), spec(1), spec(1)],
            out_specs=pl.BlockSpec((BLOCK, columns), lambda i, s, r, k: (i, 0)),
        ),
        out_shape=jax.ShapeDtypeStruct((rows, columns), F32),
        input_output_aliases={3: 0},
        compiler_params=params(),
        cost_estimate=cost(0, 24 << 20),
        name="place_children",
    )(source, rank, keep, front, near, far, near, far)


def earlier_count(keys):
    places = jnp.arange(keys.shape[-1], dtype=jnp.int32)
    matches = keys[..., :, None] == keys[..., None, :]
    before = places[None, :] < places[:, None]
    return jnp.sum((matches & before).astype(jnp.int32), axis=-1)


def lookup(codes, values, length):
    hits = codes[..., :, None] == jnp.arange(length, dtype=jnp.int32)
    found = jnp.sum(jnp.where(hits, values[..., :, None], 0), axis=-2)
    return found, jnp.any(hits, axis=-2)


def body(parent_front, children, child_map, fill):
    row_index = lax.axis_index("row")
    col_index = lax.axis_index("col")
    child_id = row_index // COLS
    group_row = row_index % COLS
    blocks = child_map.shape[1]
    places = jnp.arange(blocks, dtype=jnp.int32)
    groups = places // GRP
    within = places % GRP
    run16 = child_map // 16
    run8 = child_map // 8
    slot = earlier_count(groups * COLS + run16)
    pick = lambda x: lax.dynamic_index_in_dim(x, child_id, 0, keepdims=False)
    own_map, own_run16, own_run8, own_slot = pick(child_map), pick(run16), pick(run8), pick(slot)

    col_codes = jnp.where(groups == col_index, own_run16 * 2 + own_slot, -1)
    send_cols, _ = lookup(col_codes, within, 2 * COLS)
    row_codes = jnp.where(groups == group_row, own_run8, -1)
    send_rows, sends = lookup(row_codes, within, ROWS)
    ahead = slot[:, None, :] * blocks + places < (slot * blocks + places)[:, :, None]
    rank_all = jnp.sum((ahead & (run16[:, None, :] == run16[:, :, None])).astype(jnp.int32), axis=-1)
    rank_codes = jnp.where(own_run16 == col_index, pick(rank_all), -1)
    origin = jnp.where(own_slot == 0, groups, COLS + (col_index - groups) % COLS)
    pick_cols, _ = lookup(rank_codes, origin, GRP)
    own_codes = jnp.where(own_run16 == col_index, own_map % 16, -1)
    pick_owner, _ = lookup(own_codes, groups * 2 + own_slot, 16)

    tile_rows = jnp.where(run8 == row_index, child_map % 8, -1)
    row_block, row_has = lookup(tile_rows, jnp.broadcast_to(places, (2, blocks)), 8)
    tile_cols = jnp.where(run16 == col_index, child_map % 16, -1)
    col_rank, col_has = lookup(tile_cols, rank_all, 16)
    row_hit = (tile_rows[:, None, :] == jnp.arange(8, dtype=jnp.int32)[None, :, None]).astype(F32)
    col_hit = (tile_cols[:, None, :] == jnp.arange(16, dtype=jnp.int32)[None, :, None]).astype(F32)
    present = fill.astype(F32)
    keep = jnp.einsum("hia,hab->hib", row_hit, present)
    keep = jnp.einsum("hib,hjb->hij", keep, col_hit)
    panel_col = (col_index == 0) & (jnp.arange(16) < NLEAD)
    keep = jnp.where(panel_col | (row_index == 0), 0.0, keep)
    keep = (keep > 0.5).astype(jnp.int32).reshape(2, 8 * 16)
    source = jnp.arange(2, dtype=jnp.int32)[:, None] * COLS + row_block // GRP

    owned = col_index * 16 + row_index
    lead_codes = jnp.where(run8 == 0, groups, -1)
    strip_place, strip_has = lookup(lead_codes, child_map, COLS)
    lead_hit = (lead_codes[:, None, :] == jnp.arange(COLS, dtype=jnp.int32)[None, :, None]).astype(F32)
    owned_hit = (child_map == owned).astype(F32)
    strip_keep = jnp.einsum("hga,hab->hgb", lead_hit, present)
    strip_keep = jnp.sum(strip_keep * owned_hit[:, None, :], axis=-1)
    strip_keep = (strip_keep > 0.5).astype(jnp.int32).reshape(ROWS)
    strip_place = jnp.where(strip_has, strip_place, 0).reshape(ROWS)

    axes = ("row", "col")
    number = lambda r, c: r * COLS + c

    total = lambda values: functools.reduce(lambda x, y: x + y, values)

    total = lambda values: functools.reduce(lambda x, y: x + y, values)

    pieces = cut_strip(parent_front)
    own = total([jnp.where(col_index == 0, pieces[0], 0.0)] + [
        lax.ppermute(pieces[i], axes, [(number(r, 0), number(r, i)) for r in range(ROWS)])
        for i in range(1, NLEAD)
    ])
    pairs = [(number(j % 16, j // 16), number(j // 8, j % 8)) for j in range(128)]
    strip_parent = lax.ppermute(own, axes, [(b, a) for a, b in pairs])

    early = pack_early(jnp.concatenate([send_cols, send_rows[:1]]), children)
    early = lax.all_to_all(early, "col", split_axis=0, concat_axis=0, tiled=True)
    early = pick_early(pick_owner, early, [])
    early = lax.all_to_all(early, "row", split_axis=0, concat_axis=0, tiled=True)
    strip = assemble_strip(strip_place, strip_keep, strip_parent, early, [])

    first = pack_first(send_cols[0::2], children, [])
    first = lax.all_to_all(first, "col", split_axis=0, concat_axis=0, tiled=True)

    row_raw = lax.ppermute(strip, axes, pairs)

    half = BLOCK // 2
    piece = total([
        lax.ppermute(
            strip[part * half : (part + 1) * half],
            axes,
            [(number(j, 0), number(2 * j + part, 0)) for j in range(NLEAD)],
        )
        for part in range(2)
    ])
    piece = hand_on(piece, [row_raw])
    piece = total([piece] + [
        lax.ppermute(piece, axes, [(number(r, 0), number(r, d)) for r in range(ROWS)])
        for d in range(1, COLS)
    ])
    lead = lax.all_gather(piece, "row", axis=0, tiled=True)

    col_strip = lax.all_gather(strip, "row", axis=0, tiled=True)

    sends = sends.astype(jnp.int32)
    work = factor_part(0, lead, strip)
    near_out = pack_rows(send_rows, sends, pick_cols[:HALF], first, [], [])
    near = lax.all_to_all(near_out, "row", split_axis=0, concat_axis=0, tiled=True)
    shifts = (col_index + jnp.arange(COLS, dtype=jnp.int32)) % COLS
    parts = pack_second(jnp.take(send_cols, shifts * 2 + 1), children, [near_out])
    second = [parts[0]] + [
        lax.ppermute(parts[d], "col", [(c, (c + d) % COLS) for c in range(COLS)])
        for d in range(1, COLS)
    ]
    work = factor_part(1, work, near_out)
    far_out = pack_rows(send_rows, sends, pick_cols[HALF:], first, second, [work])
    far_out = pass_on(far_out, [near])
    work = factor_part(2, work, far_out)
    far = lax.all_to_all(far_out, "row", split_axis=0, concat_axis=0, tiled=True)
    inv_hi, inv_lo = factor_part(3, work, col_strip)
    row_piece = hand_on(row_raw, [near_out])
    row_strip = lax.all_gather(row_piece, "col", axis=0, tiled=True)
    flags = jnp.stack([row_index, col_index]).astype(jnp.int32)
    front = update_front(flags, row_strip, col_strip, inv_hi, inv_lo, parent_front)
    return place_children(source, col_rank, keep, front, near, far)


def solution(mesh):
    in_specs = (P("row", "col"), P("row", "col"), P(), P())
    out_specs = P("row", "col")
    return jax.shard_map(body, mesh=mesh, in_specs=in_specs, out_specs=out_specs, check_vma=False)
```
